32 devices in a mesh: dp: 8 (over z, x), seq: 4 (over y, core).
Axes of the slice: x: 2, y: 2, z: 4, core: 2. Of those that a mesh axis runs over, the one named last changes fastest.
Arguments:
- grad_out: bfloat16 [8, 1024, 4096], P('dp', 'seq'), may hold values from -6 to 6
- queries: bfloat16 [8, 1024, 4096], P('dp', 'seq'), may hold values from -45 to 45
- keys: bfloat16 [8, 1024, 1024], P('dp', 'seq'), may hold values from -4 to 4
- values: bfloat16 [8, 1024, 1024], P('dp', 'seq'), may hold values from -6 to 6
- out_weight: bfloat16 [4096, 4096], P('seq'), may hold values from -0.09375 to 0.09375
- doc_starts: int32 [8, 8], P('dp'), may hold values from 0 to 1020, as said below
Outputs:
- grad_queries: bfloat16 [8, 1024, 4096], P('dp', 'seq')
- grad_keys: bfloat16 [8, 1024, 1024], P('dp', 'seq')
- grad_values: bfloat16 [8, 1024, 1024], P('dp', 'seq')
- grad_weight: float32 [4096, 4096], P('seq', 'dp')
The draws below stay inside these ranges and needn't reach their ends.
Inputs may be any that keep to these rules, and one draw needn't show every extreme that they name: `doc_starts`: each row strictly increases, holds multiples of 4, begins with 0 and ends with 1020.
All inputs are finite; a program needn't handle non-finite values.
Results may differ from the reference program's by a relative error of at most 0.015.
Values may be sent and summed in bfloat16 or wider, within the bound.
No kernel may reach another device: no remote copies, remote signals or barrier semaphores. Data moves between devices by JAX's collectives and lax.ppermute only.
A program may use at most 128 MiB of HBM per device.

```python
import math
import jax
import jax.numpy as jnp
from jax import lax

HEADS = 32
KV_HEADS = 8
HEAD_DIM = 128
D = 4096
SEQ_LEN = 1024
NDOC = 8
SEQS = 8


def pair_draw(key):
    base = jax.random.fold_in(key, 7)
    key_first, key_second = jax.random.split(base, 2)
    keys_out = jax.random.truncated_normal(key_first, -4.0, 4.0, (SEQS, SEQ_LEN, KV_HEADS * HEAD_DIM), jnp.float32)
    query_out = jax.random.truncated_normal(key_second, -4.0, 4.0, (SEQS, SEQ_LEN, HEADS * HEAD_DIM), jnp.float32)
    return (query_out, keys_out)


def draw_queries(key, part):
    return pair_draw(key)[0].astype(jnp.bfloat16)


def draw_keys(key, part):
    return pair_draw(key)[1].astype(jnp.bfloat16)


def draw_doc_starts(key, part):

    def one_row(index):
        chosen = jax.random.permutation(jax.random.fold_in(key, index), SEQ_LEN // 4 - 2)[:NDOC - 2] + 1
        middle = (jnp.sort(chosen) * 4).astype(jnp.int32)
        return jnp.concatenate([jnp.zeros((1,), jnp.int32), middle, jnp.full((1,), SEQ_LEN - 4, jnp.int32)])
    return jax.vmap(one_row)(jnp.arange(SEQS))


def spiked(result, own_key, source, target, blocks, factor):
    owner, partner = [(jnp.arange(result.shape[dim]) // (result.shape[dim] // blocks)).reshape([-1 if axis == dim else 1 for axis in range(result.ndim)]) for dim in (source, target)]
    chosen = jax.random.permutation(own_key, blocks)[partner]
    strong = (owner == chosen) | (owner == (partner + blocks // 2) % blocks)
    return jnp.where(strong, factor * result, result)


def steps_of(stream_key, dims, shards, least, high):
    def one(dim, blocks):
        steps = jax.random.uniform(jax.random.fold_in(jax.random.fold_in(stream_key, 6), dim), (blocks,), jnp.float32, least / len(shards), high / len(shards))
        return jnp.repeat(jnp.exp(steps), dims[dim] // blocks).reshape((-1,) + (1,) * (len(dims) - dim - 1))

    gain = one(*shards[0])
    for cut in shards[1:]:
        gain = gain * one(*cut)
    return gain


def bell_draw(stream_key, dims, scale, bound, cuts=(), held_as=jnp.bfloat16):
    level = steps_of(stream_key, dims, cuts, -0.22, 0.18) if cuts else 1.0
    entries = jax.random.normal(stream_key, dims, jnp.float32) * scale * level
    return jnp.minimum(jnp.maximum(entries, -bound), bound).astype(held_as)


def heavy_noise(stream_key, dims, width, reach, pieces, heavy, kind=jnp.bfloat16):
    drawn = width * jax.random.normal(stream_key, dims, jnp.float32)
    if pieces:
        drawn = drawn * steps_of(stream_key, dims, pieces, -0.22, 0.18)
    return jnp.clip(spiked(drawn, jax.random.fold_in(stream_key, 3), *heavy), -reach, reach).astype(kind)


def setup_inputs(seed: int = 0) -> dict:
    seeds = jax.random.split(jax.random.key(seed), 7)
    return {
        "grad_out": heavy_noise(seeds[0], (SEQS, SEQ_LEN, D), 1.0, 6.0, ((0, 8), (1, 4)), (0, 2, 8, 2.0)),
        "queries": draw_queries(jax.random.fold_in(seeds[6], 71), 0),
        "keys": draw_keys(jax.random.fold_in(seeds[6], 71), 0),
        "values": bell_draw(seeds[3], (SEQS, SEQ_LEN, KV_HEADS * HEAD_DIM), 1.0, 6.0, ((0, 8), (1, 4))),
        "out_weight": bell_draw(seeds[4], (D, D), D ** -0.5, 0.09375, ((0, 4),)),
        "doc_starts": draw_doc_starts(jax.random.fold_in(seeds[6], 71), 0),
    }


def visible(starts, first_row, row_count, key_count):
    rows_pos = first_row + jnp.arange(row_count, dtype=jnp.int32)
    keys_pos = jnp.arange(key_count, dtype=jnp.int32)
    opening = lax.optimization_barrier(jnp.max(jnp.where(starts[None, :] <= rows_pos[:, None], starts[None, :], 0), axis=1))
    return (keys_pos[None, :] >= opening[:, None]) & (keys_pos[None, :] <= rows_pos[:, None])

def weights_of(query_rows, key_rows, allowed, scale):
    scores = lax.dot_general(query_rows, key_rows, (((1,), (1,)), ((), ())), preferred_element_type=jnp.float32) * scale
    scores = jnp.where(allowed, scores, -1e+30)
    highest = lax.optimization_barrier(jnp.max(scores, axis=1, keepdims=True))
    raised = jnp.exp(scores - highest)
    return raised / lax.optimization_barrier(jnp.sum(raised, axis=1, keepdims=True))

def attend(query_all, key_all, value_all, starts, group, head_dim, block, trimmed):
    length = query_all.shape[0]
    scale = 1.0 / math.sqrt(head_dim)
    columns = []
    for member in range(query_all.shape[1] // head_dim):
        shared = member // group
        query_head = query_all[:, member * head_dim:(member + 1) * head_dim]
        key_head = key_all[:, shared * head_dim:(shared + 1) * head_dim]
        value_head = value_all[:, shared * head_dim:(shared + 1) * head_dim]
        blocks = []
        for section in range(length // block):
            first = section * block
            ending = first + block if trimmed else length
            allowed = visible(starts, first, block, ending)
            probs = weights_of(query_head[first:first + block], key_head[:ending], allowed, scale)
            blocks.append(jnp.dot(probs.astype(jnp.bfloat16), value_head[:ending], preferred_element_type=jnp.float32).astype(jnp.bfloat16))
        columns.append(jnp.concatenate(blocks, axis=0))
    return jnp.concatenate(columns, axis=1)

def attend_back(query_all, key_all, value_all, out_all, grad_all, starts, group, head_dim, block, trimmed):
    length = query_all.shape[0]
    scale = 1.0 / math.sqrt(head_dim)
    shared_count = key_all.shape[1] // head_dim
    key_grads = [jnp.zeros((length, head_dim), jnp.float32) for shared in range(shared_count)]
    value_grads = [jnp.zeros((length, head_dim), jnp.float32) for shared in range(shared_count)]
    query_grads = []
    for member in range(query_all.shape[1] // head_dim):
        shared = member // group
        lo_col = member * head_dim
        query_head = query_all[:, lo_col:lo_col + head_dim]
        key_head = key_all[:, shared * head_dim:(shared + 1) * head_dim]
        value_head = value_all[:, shared * head_dim:(shared + 1) * head_dim]
        blocks = []
        for section in range(length // block):
            first = section * block
            ending = first + block if trimmed else length
            allowed = visible(starts, first, block, ending)
            query_rows = query_head[first:first + block]
            probs = weights_of(query_rows, key_head[:ending], allowed, scale)
            probs_low = probs.astype(jnp.bfloat16)
            grad_rows = grad_all[first:first + block, lo_col:lo_col + head_dim]
            out_rows = out_all[first:first + block, lo_col:lo_col + head_dim]
            value_grads[shared] = value_grads[shared].at[:ending].add(lax.dot_general(probs_low, grad_rows, (((0,), (0,)), ((), ())), preferred_element_type=jnp.float32))
            grad_probs = lax.dot_general(grad_rows, value_head[:ending], (((1,), (1,)), ((), ())), preferred_element_type=jnp.float32)
            delta = lax.optimization_barrier(jnp.sum(grad_rows.astype(jnp.float32) * out_rows.astype(jnp.float32), axis=1, keepdims=True))
            grad_scores = (probs * (grad_probs - delta)).astype(jnp.bfloat16)
            blocks.append((jnp.dot(grad_scores, key_head[:ending], preferred_element_type=jnp.float32) * scale).astype(jnp.bfloat16))
            key_grads[shared] = key_grads[shared].at[:ending].add(lax.dot_general(grad_scores, query_rows, (((0,), (0,)), ((), ())), preferred_element_type=jnp.float32) * scale)
        query_grads.append(jnp.concatenate(blocks, axis=0))
    grad_q = jnp.concatenate(query_grads, axis=1)
    grad_k = jnp.concatenate(key_grads, axis=1).astype(jnp.bfloat16)
    grad_v = jnp.concatenate(value_grads, axis=1).astype(jnp.bfloat16)
    return (grad_q, grad_k, grad_v)

def reference(grad_out, queries, keys, values, out_weight, doc_starts):
    group = HEADS // KV_HEADS
    block = min(512, SEQ_LEN)

    def one_sequence(weight_sum, inputs):
        grad_rows, query_all, key_all, value_all, starts = inputs
        out_all = attend(query_all, key_all, value_all, starts, group, HEAD_DIM, block, False)
        grad_attn = lax.dot_general(grad_rows, out_weight, (((1,), (1,)), ((), ())), preferred_element_type=jnp.float32).astype(jnp.bfloat16)
        weight_sum = weight_sum + lax.dot_general(out_all, grad_rows, (((0,), (0,)), ((), ())), preferred_element_type=jnp.float32)
        grads = attend_back(query_all, key_all, value_all, out_all, grad_attn, starts, group, HEAD_DIM, block, False)
        return (weight_sum, grads)
    weight_sum, grads = lax.scan(one_sequence, jnp.zeros((D, D), jnp.float32), (grad_out, queries, keys, values, doc_starts))
    scaled = weight_sum * (1.0 / math.sqrt(SEQS * SEQ_LEN))
    return (grads[0], grads[1], grads[2], scaled)
```

```python
import functools
import math

import jax
import jax.numpy as jnp
from jax import lax
from jax.experimental import pallas as pl
from jax.experimental.pallas import tpu as pltpu
from jax.sharding import PartitionSpec as P

HEADS = 32
KV_HEADS = 8
HEAD_DIM = 128
GROUP = HEADS // KV_HEADS
MASKED = -1e30
NT = (((1,), (1,)), ((), ()))
NN = (((1,), (0,)), ((), ()))


def mm(a, b, dims=NN):
    return lax.dot_general(a, b, dims, preferred_element_type=jnp.float32)


def params(mib):
    return pltpu.CompilerParams(vmem_limit_bytes=mib * 2**20)


def cost(flops, nbytes):
    return pl.CostEstimate(flops=int(flops), bytes_accessed=int(nbytes), transcendentals=0)


def pack_kernel(parts, info_ref, *refs):
    q_refs, k_refs, v_refs, out_refs = (refs[i * parts : (i + 1) * parts] for i in range(4))
    wide = GROUP * HEAD_DIM
    for d in range(parts):
        out_refs[d][:, :wide] = q_refs[d][...]
        out_refs[d][:, wide : wide + HEAD_DIM] = k_refs[d][...]
        out_refs[d][:, wide + HEAD_DIM :] = v_refs[d][...]


def pack(info, queries, keys, values, parts, groups, gp):
    rows = queries.shape[0]
    wide = GROUP * HEAD_DIM
    step = min(128, rows)

    def pick(d):
        return lambda i, info: (i, (info[0] ^ d) * groups + gp)

    return pl.pallas_call(
        functools.partial(pack_kernel, parts),
        grid_spec=pltpu.PrefetchScalarGridSpec(
            num_scalar_prefetch=1,
            grid=(rows // step,),
            in_specs=[pl.BlockSpec((step, wide), pick(d)) for d in range(parts)]
            + [pl.BlockSpec((step, HEAD_DIM), pick(d)) for d in range(parts)] * 2,
            out_specs=[
                pl.BlockSpec((step, wide + 2 * HEAD_DIM), lambda i, info: (i, 0))
                for d in range(parts)
            ],
        ),
        out_shape=[
            jax.ShapeDtypeStruct((rows, wide + 2 * HEAD_DIM), jnp.bfloat16) for d in range(parts)
        ],
        compiler_params=params(32),
        cost_estimate=cost(0, 4 * parts * rows * (wide + 2 * HEAD_DIM)),
        name="pack",
    )(info, *[queries] * parts, *[keys] * parts, *[values] * parts)


def unpack_kernel(parts, groups, info_ref, *refs):
    count = parts * groups
    q_ref, k_ref, v_ref = refs[count:]
    wide = GROUP * HEAD_DIM
    for gp in range(groups):
        for d in range(parts):
            piece = refs[gp * parts + d]
            place = (info_ref[0] ^ d) * groups + gp
            q_ref[:, pl.ds(pl.multiple_of(place * wide, wide), wide)] = piece[:, :wide]
            narrow = pl.ds(pl.multiple_of(place * HEAD_DIM, HEAD_DIM), HEAD_DIM)
            k_ref[:, narrow] = piece[:, wide : wide + HEAD_DIM]
            v_ref[:, narrow] = piece[:, wide + HEAD_DIM :]


def unpack(info, pieces, parts, groups):
    rows, cols = pieces[0].shape
    wide = GROUP * HEAD_DIM
    step = min(64, rows)
    total = parts * groups
    widths = (total * wide, total * HEAD_DIM, total * HEAD_DIM)
    return pl.pallas_call(
        functools.partial(unpack_kernel, parts, groups),
        grid_spec=pltpu.PrefetchScalarGridSpec(
            num_scalar_prefetch=1,
            grid=(rows // step,),
            in_specs=[pl.BlockSpec((step, cols), lambda i, info: (i, 0))] * total,
            out_specs=[pl.BlockSpec((step, w), lambda i, info: (i, 0)) for w in widths],
        ),
        out_shape=[jax.ShapeDtypeStruct((rows, w), jnp.bfloat16) for w in widths],
        compiler_params=params(32),
        cost_estimate=cost(0, 4 * total * rows * cols),
        name="unpack",
    )(info, *pieces)


def pair_index(qb, kb):
    return qb * (qb + 1) // 2 + kb


def prepare(parts, block, docs, info_ref, bias_ref, open_ref):
    for qb in range(parts):
        lanes = qb * block + lax.broadcasted_iota(jnp.int32, (1, block), 1)
        opening = jnp.zeros((1, block), jnp.int32)
        first = jnp.int32(0)
        for n in range(docs):
            start = info_ref[2 + n]
            opening = jnp.where(start <= lanes, jnp.maximum(opening, start), opening)
            first = jnp.where(start <= qb * block, jnp.maximum(first, start), first)
        open_ref[qb] = first
        for kb in range(qb + 1):
            down = kb * block + lax.broadcasted_iota(jnp.int32, (block, block), 0)
            seen = (down >= opening) & (down <= lanes)
            bias_ref[pair_index(qb, kb)] = jnp.where(seen, 0.0, MASKED).astype(jnp.float32)


def flip(x):
    return jnp.transpose(x.astype(jnp.float32))


def forward_kernel(parts, block, docs, info_ref, *refs):
    pieces = refs[:parts]
    out_ref, lse_ref = refs[parts : parts + 2]
    bias_ref, open_ref, q_s, k_s, vt_s, top_s, sum_s, acc_s = refs[parts + 2 :]
    head = pl.program_id(0)
    me = info_ref[0]
    wide = GROUP * HEAD_DIM
    factor = math.log2(math.e) / math.sqrt(HEAD_DIM)

    @pl.when(head == 0)
    def _():
        prepare(parts, block, docs, info_ref, bias_ref, open_ref)
        for d in range(parts):
            k_s[me ^ d] = pieces[d][:, wide : wide + HEAD_DIM]
            vt_s[me ^ d] = flip(pieces[d][:, wide + HEAD_DIM :]).astype(jnp.bfloat16)

    own = pl.ds(pl.multiple_of(head * HEAD_DIM, HEAD_DIM), HEAD_DIM)
    for d in range(parts):
        q_s[me ^ d] = pieces[d][:, own]

    def scores(qb, kb):
        return mm(k_s[kb], q_s[qb], NT) * factor + bias_ref[pair_index(qb, kb)]

    for qb in range(parts):
        raw = scores(qb, qb)
        top = jnp.max(raw, axis=0, keepdims=True)
        raised = jnp.exp2(raw - top)
        top_s[...] = top
        sum_s[...] = jnp.sum(raised, axis=0, keepdims=True)
        acc_s[...] = mm(vt_s[qb], raised.astype(jnp.bfloat16))
        for kb in range(qb - 1, -1, -1):

            @pl.when(open_ref[qb] < (kb + 1) * block)
            def _():
                raw = scores(qb, kb)
                old = top_s[...]
                top = jnp.maximum(old, jnp.max(raw, axis=0, keepdims=True))
                shrink = jnp.exp2(old - top)
                raised = jnp.exp2(raw - top)
                top_s[...] = top
                sum_s[...] = sum_s[...] * shrink + jnp.sum(raised, axis=0, keepdims=True)
                acc_s[...] = acc_s[...] * shrink + mm(vt_s[kb], raised.astype(jnp.bfloat16))

        out_ref[me ^ qb] = (acc_s[...] / sum_s[...]).astype(jnp.bfloat16)
        lse_ref[0, me ^ qb] = jnp.broadcast_to(top_s[...] + jnp.log2(sum_s[...]), (8, block))


def attention(info, pieces, parts, docs):
    block, cols = pieces[0].shape
    pairs = parts * (parts + 1) // 2
    vm = pltpu.VMEM
    return pl.pallas_call(
        functools.partial(forward_kernel, parts, block, docs),
        grid_spec=pltpu.PrefetchScalarGridSpec(
            num_scalar_prefetch=1,
            grid=(GROUP,),
            in_specs=[pl.BlockSpec((block, cols), lambda h, info: (0, 0))] * parts,
            out_specs=[
                pl.BlockSpec((parts, HEAD_DIM, block), lambda h, info: (0, h, 0)),
                pl.BlockSpec((1, parts, 8, block), lambda h, info: (h, 0, 0, 0)),
            ],
            scratch_shapes=[
                vm((pairs, block, block), jnp.float32),
                pltpu.SMEM((parts,), jnp.int32),
                vm((parts, block, HEAD_DIM), jnp.bfloat16),
                vm((parts, block, HEAD_DIM), jnp.bfloat16),
                vm((parts, HEAD_DIM, block), jnp.bfloat16),
                vm((1, block), jnp.float32),
                vm((1, block), jnp.float32),
                vm((HEAD_DIM, block), jnp.float32),
            ],
        ),
        out_shape=[
            jax.ShapeDtypeStruct((parts, GROUP * HEAD_DIM, block), jnp.bfloat16),
            jax.ShapeDtypeStruct((GROUP, parts, 8, block), jnp.float32),
        ],
        compiler_params=params(32),
        cost_estimate=cost(6e9, 4 * parts * block * cols),
        name="attention",
    )(info, *pieces)


def backward_kernel(parts, block, docs, info_ref, *refs):
    pieces = refs[:parts]
    grads = refs[parts : 2 * parts]
    out_ref, lse_ref, res_ref = refs[2 * parts : 2 * parts + 3]
    bias_ref, open_ref, q_s, k_s, kt_s, v_s, do_s, dk_s, dv_s, dq_s = refs[2 * parts + 3 :]
    head = pl.program_id(0)
    me = info_ref[0]
    wide = GROUP * HEAD_DIM
    scale = 1.0 / math.sqrt(HEAD_DIM)
    factor = math.log2(math.e) * scale

    @pl.when(head == 0)
    def _():
        prepare(parts, block, docs, info_ref, bias_ref, open_ref)
        for d in range(parts):
            k_s[me ^ d] = pieces[d][:, wide : wide + HEAD_DIM]
            kt_s[me ^ d] = flip(pieces[d][:, wide : wide + HEAD_DIM]).astype(jnp.bfloat16)
            v_s[me ^ d] = pieces[d][:, wide + HEAD_DIM :]
        dk_s[...] = jnp.zeros_like(dk_s)
        dv_s[...] = jnp.zeros_like(dv_s)

    own = pl.ds(pl.multiple_of(head * HEAD_DIM, HEAD_DIM), HEAD_DIM)
    for d in range(parts):
        q_s[me ^ d] = pieces[d][:, own]
        do_s[me ^ d] = grads[d][...]

    for qb in range(parts):
        delta = jnp.sum(flip(do_s[qb]) * out_ref[me ^ qb].astype(jnp.float32), axis=0, keepdims=True)
        lse = lse_ref[0, me ^ qb][:1]

        def pair(kb):
            query, grad = q_s[qb], do_s[qb]
            raw = mm(k_s[kb], query, NT) * factor + bias_ref[pair_index(qb, kb)]
            probs = jnp.exp2(raw - lse)
            dv_s[kb] += mm(probs.astype(jnp.bfloat16), grad)
            slope = (probs * (mm(v_s[kb], grad, NT) - delta)).astype(jnp.bfloat16)
            dk_s[kb] += mm(slope, query)
            return mm(kt_s[kb], slope)

        dq_s[...] = pair(qb)
        for kb in range(qb - 1, -1, -1):

            @pl.when(open_ref[qb] < (kb + 1) * block)
            def _():
                dq_s[...] += pair(kb)

        res_ref[me ^ qb, :, own] = (jnp.transpose(dq_s[...]) * scale).astype(jnp.bfloat16)

    @pl.when(head == GROUP - 1)
    def _():
        for kb in range(parts):
            res_ref[me ^ kb, :, wide : wide + HEAD_DIM] = (dk_s[kb] * scale).astype(jnp.bfloat16)
            res_ref[me ^ kb, :, wide + HEAD_DIM :] = dv_s[kb].astype(jnp.bfloat16)


def attention_back(info, pieces, grads, out, lse, parts, docs, gp):
    block, cols = pieces[0].shape
    pairs = parts * (parts + 1) // 2
    vm = pltpu.VMEM
    return pl.pallas_call(
        functools.partial(backward_kernel, parts, block, docs),
        grid_spec=pltpu.PrefetchScalarGridSpec(
            num_scalar_prefetch=1,
            grid=(GROUP,),
            in_specs=[pl.BlockSpec((block, cols), lambda h, info: (0, 0))] * parts
            + [pl.BlockSpec((block, HEAD_DIM), lambda h, info: (0, gp * GROUP + h))] * parts
            + [
                pl.BlockSpec((parts, HEAD_DIM, block), lambda h, info: (0, h, 0)),
                pl.BlockSpec((1, parts, 8, block), lambda h, info: (h, 0, 0, 0)),
            ],
            out_specs=pl.BlockSpec((parts, block, cols), lambda h, info: (0, 0, 0)),
            scratch_shapes=[
                vm((pairs, block, block), jnp.float32),
                pltpu.SMEM((parts,), jnp.int32),
                vm((parts, block, HEAD_DIM), jnp.bfloat16),
                vm((parts, block, HEAD_DIM), jnp.bfloat16),
                vm((parts, HEAD_DIM, block), jnp.bfloat16),
                vm((parts, block, HEAD_DIM), jnp.bfloat16),
                vm((parts, block, HEAD_DIM), jnp.bfloat16),
                vm((parts, block, HEAD_DIM), jnp.float32),
                vm((parts, block, HEAD_DIM), jnp.float32),
                vm((HEAD_DIM, block), jnp.float32),
            ],
        ),
        out_shape=jax.ShapeDtypeStruct((parts, block, cols), jnp.bfloat16),
        compiler_params=params(32),
        cost_estimate=cost(12e9, 8 * parts * block * cols),
        name="attention_back",
    )(info, *pieces, *grads, out, lse)


def reverse_bits(x, bits):
    out = 0 * x
    for b in range(bits):
        out = out + ((x >> b) & 1) * (1 << (bits - 1 - b))
    return out


def weight_kernel(parts, groups, width, info_ref, *refs):
    outs, grads = refs[:groups], refs[groups : groups + parts]
    keep_ref, send_ref = refs[groups + parts :]
    odd = (info_ref[1] & 1) == 1
    rows = GROUP * HEAD_DIM
    for gp in range(groups):
        total = mm(outs[gp][0], grads[0][...])
        for d in range(1, parts):
            total += mm(outs[gp][d], grads[d][...])
        low, high = total[:, :width], total[:, width:]
        place = slice(gp * rows, (gp + 1) * rows)
        keep_ref[0, place] = jnp.where(odd, high, low)
        send_ref[0, place] = jnp.where(odd, low, high).astype(jnp.bfloat16)


def weight_terms(info, outs, grads, shares, width):
    groups, parts = len(outs), len(grads)
    _, rows, block = outs[0].shape
    half = shares // 2
    bits = half.bit_length() - 1
    spot = pl.BlockSpec((1, groups * rows, width), lambda t, info: (reverse_bits(t, bits), 0, 0))
    return pl.pallas_call(
        functools.partial(weight_kernel, parts, groups, width),
        grid_spec=pltpu.PrefetchScalarGridSpec(
            num_scalar_prefetch=1,
            grid=(half,),
            in_specs=[pl.BlockSpec((parts, rows, block), lambda t, info: (0, 0, 0))] * groups
            + [pl.BlockSpec((block, 2 * width), lambda t, info: (0, t ^ (info[1] >> 1)))] * parts,
            out_specs=[spot, spot],
        ),
        out_shape=[
            jax.ShapeDtypeStruct((half, groups * rows, width), jnp.float32),
            jax.ShapeDtypeStruct((half, groups * rows, width), jnp.bfloat16),
        ],
        compiler_params=params(32),
        cost_estimate=cost(
            2 * groups * rows * block * parts * shares * width, 8 * groups * rows * shares * width
        ),
        name="weight_terms",
    )(info, *outs, *grads)


def body(grad_out, queries, keys, values, out_weight, doc_starts):
    parts, shares = lax.axis_size("seq"), lax.axis_size("dp")
    groups = KV_HEADS // parts
    docs = doc_starts.shape[-1]
    cotangent = grad_out[0]
    rows, model = cotangent.shape
    feats = out_weight.shape[0]
    chunks = max(1, min(4, model // shares // 128))
    width = model // shares // chunks
    info = jnp.concatenate(
        [
            jnp.stack([lax.axis_index("seq"), lax.axis_index("dp")]).astype(jnp.int32),
            doc_starts[0],
        ]
    )

    def over_seq(x, d):
        return lax.ppermute(x, "seq", [(i, i ^ d) for i in range(parts)])

    def over_dp(x, d):
        return lax.ppermute(x, "dp", [(i, i ^ d) for i in range(shares)])

    def after(x, *others):
        return lax.optimization_barrier((x, *others))[0]

    pieces = []
    for gp in range(groups):
        sent = pack(info, queries[0], keys[0], values[0], parts, groups, gp)
        pieces.append([sent[0]] + [over_seq(sent[d], d) for d in range(1, parts)])

    split_g = cotangent.reshape(rows, shares, chunks, width).transpose(2, 0, 1, 3)
    split_w = out_weight.reshape(feats, shares, chunks, width).transpose(2, 0, 1, 3)
    phases = [group[-1] for group in pieces]
    gathered = []
    for c in range(chunks):
        mine = after(split_g[c].reshape(rows, shares * width), phases[max(0, len(phases) - 2)])
        got = {0: mine}
        for d in range(2, parts, 2):
            got[d] = over_seq(mine, d)
        for d in range(0, parts, 2):
            got[d + 1] = over_seq(got[d], 1)
        gathered.append([got[d] for d in range(parts)])
        phases.append(got[parts - 2])

    fwd = [attention(info, pieces[gp], parts, docs) for gp in range(groups)]
    outs = [pair[0] for pair in fwd]

    grads = [0.0] * parts
    finished = []
    for c in range(chunks):
        part_w = split_w[c].reshape(feats, shares * width)
        grads = [grads[d] + mm(gathered[c][d], part_w, NT) for d in range(parts)]
        keep, send = weight_terms(info, outs, gathered[c], shares, width)
        hop = 1
        while hop < shares:
            total = keep + over_dp(send, hop).astype(jnp.float32)
            half = total.shape[0] // 2
            keep, send = total[:half], total[half:].astype(jnp.bfloat16)
            hop *= 2
        finished.append(total[0])
    grads = [grad.astype(jnp.bfloat16) for grad in grads]
    weight_grad = jnp.concatenate(finished, axis=1) * (1.0 / math.sqrt(rows * parts * shares))

    back = []
    for gp in range(groups):
        res = attention_back(info, pieces[gp], grads, outs[gp], fwd[gp][1], parts, docs, gp)
        back += [res[0]] + [over_seq(res[d], d) for d in range(1, parts)]
    grad_q, grad_k, grad_v = unpack(info, back, parts, groups)
    return (grad_q[None], grad_k[None], grad_v[None], weight_grad)


def solution(mesh):
    return jax.shard_map(
        body,
        mesh=mesh,
        in_specs=(
            P("dp", "seq", None),
            P("dp", "seq", None),
            P("dp", "seq", None),
            P("dp", "seq", None),
            P("seq", None),
            P("dp", None),
        ),
        out_specs=(
            P("dp", "seq", None),
            P("dp", "seq", None),
            P("dp", "seq", None),
            P("seq", "dp"),
        ),
        check_vma=False,
    )
```

```python
import functools
import math

import jax
import jax.numpy as jnp
from jax import lax
from jax.experimental import pallas as pl
from jax.experimental.pallas import tpu as pltpu
from jax.sharding import PartitionSpec as P

HEADS = 32
KV_HEADS = 8
HEAD_DIM = 128
GROUP = HEADS // KV_HEADS
MASKED = -1e30
NT = (((1,), (1,)), ((), ()))
NN = (((1,), (0,)), ((), ()))


def mm(a, b, dims=NN):
    return lax.dot_general(a, b, dims, preferred_element_type=jnp.float32)


def params(mib):
    return pltpu.CompilerParams(vmem_limit_bytes=mib * 2**20)


def cost(flops, nbytes):
    return pl.CostEstimate(flops=int(flops) // 1000, bytes_accessed=int(nbytes) // 1000, transcendentals=0)


ANY = pl.BlockSpec(memory_space=pl.ANY)


def shape(dims, dtype=jnp.bfloat16):
    return jax.ShapeDtypeStruct(dims, dtype)


def gate(arrays, *tokens):
    return list(lax.optimization_barrier((*arrays, *tokens)))[: len(arrays)]


def pack_kernel(parts, info_ref, *refs):
    q_refs, k_refs, v_refs, out_refs = (refs[i * parts : (i + 1) * parts] for i in range(4))
    wide = GROUP * HEAD_DIM
    for d in range(parts):
        out_refs[d][:, :wide] = q_refs[d][...]
        out_refs[d][:, wide : wide + HEAD_DIM] = k_refs[d][...]
        out_refs[d][:, wide + HEAD_DIM :] = v_refs[d][...]


def pack(info, queries, keys, values, parts, groups, gp):
    rows = queries.shape[0]
    wide = GROUP * HEAD_DIM
    step = min(128, rows)

    def pick(d):
        return lambda i, info: (i, (info[0] ^ d) * groups + gp)

    return pl.pallas_call(
        functools.partial(pack_kernel, parts),
        grid_spec=pltpu.PrefetchScalarGridSpec(
            num_scalar_prefetch=1,
            grid=(rows // step,),
            in_specs=[pl.BlockSpec((step, wide), pick(d)) for d in range(parts)]
            + [pl.BlockSpec((step, HEAD_DIM), pick(d)) for d in range(parts)] * 2,
            out_specs=[
                pl.BlockSpec((step, wide + 2 * HEAD_DIM), lambda i, info: (i, 0))
                for d in range(parts)
            ],
        ),
        out_shape=[shape((rows, wide + 2 * HEAD_DIM)) for d in range(parts)],
        compiler_params=params(56),
        cost_estimate=cost(0, 4 * parts * rows * (wide + 2 * HEAD_DIM)),
        name="pack",
    )(info, *[queries] * parts, *[keys] * parts, *[values] * parts)


def column(share, c, chunks, width):
    return slice((share * chunks + c) * width, (share * chunks + c + 1) * width)


def pack_chunks_kernel(orders, shares, width, g_ref, *out_refs):
    for c, order in enumerate(orders):
        for place in range(shares):
            share = unplace(place, order)
            out_refs[c][:, place * width : (place + 1) * width] = g_ref[
                :, column(share, c, len(orders), width)
            ]


def pack_chunks(cotangent, orders, shares, width):
    rows, model = cotangent.shape
    step = min(64, rows)
    return pl.pallas_call(
        functools.partial(pack_chunks_kernel, orders, shares, width),
        grid=(rows // step,),
        in_specs=[pl.BlockSpec((step, model), lambda i: (i, 0))],
        out_specs=[pl.BlockSpec((step, shares * width), lambda i: (i, 0))] * len(orders),
        out_shape=[shape((rows, shares * width)) for order in orders],
        compiler_params=params(56),
        cost_estimate=cost(0, 4 * rows * model),
        name="pack_chunks",
    )(cotangent)


def unpack_kernel(parts, groups, info_ref, *refs):
    count = parts * groups
    q_ref, k_ref, v_ref = refs[count:]
    wide = GROUP * HEAD_DIM
    for gp in range(groups):
        for d in range(parts):
            piece = refs[gp * parts + d]
            place = (info_ref[0] ^ d) * groups + gp
            q_ref[:, pl.ds(pl.multiple_of(place * wide, wide), wide)] = piece[:, :wide]
            narrow = pl.ds(pl.multiple_of(place * HEAD_DIM, HEAD_DIM), HEAD_DIM)
            k_ref[:, narrow] = piece[:, wide : wide + HEAD_DIM]
            v_ref[:, narrow] = piece[:, wide + HEAD_DIM :]


def unpack(info, pieces, parts, groups):
    rows, cols = pieces[0].shape
    wide = GROUP * HEAD_DIM
    step = min(64, rows)
    total = parts * groups
    widths = (total * wide, total * HEAD_DIM, total * HEAD_DIM)
    return pl.pallas_call(
        functools.partial(unpack_kernel, parts, groups),
        grid_spec=pltpu.PrefetchScalarGridSpec(
            num_scalar_prefetch=1,
            grid=(rows // step,),
            in_specs=[pl.BlockSpec((step, cols), lambda i, info: (i, 0))] * total,
            out_specs=[pl.BlockSpec((step, w), lambda i, info: (i, 0)) for w in widths],
        ),
        out_shape=[shape((rows, w)) for w in widths],
        compiler_params=params(16),
        cost_estimate=cost(0, 4 * total * rows * cols),
        name="unpack",
    )(info, *pieces)


def pair_index(qb, kb):
    return qb * (qb + 1) // 2 + kb


def prepare(parts, block, docs, info_ref, bias_ref, open_ref):
    down = lax.broadcasted_iota(jnp.int32, (block, block), 0)
    across = lax.broadcasted_iota(jnp.int32, (1, block), 1)
    for qb in range(parts):
        lanes = qb * block + across
        opening = jnp.zeros((1, block), jnp.int32)
        first = jnp.int32(0)
        for n in range(docs):
            start = info_ref[2 + n]
            opening = jnp.where(start <= lanes, jnp.maximum(opening, start), opening)
            first = jnp.where(start <= qb * block, jnp.maximum(first, start), first)
        open_ref[qb] = first // block
        for kb in range(qb + 1):
            seen = down >= opening - kb * block
            if kb == qb:
                seen = seen & (down <= across)
            bias_ref[pair_index(qb, kb)] = jnp.where(seen, 0.0, MASKED).astype(jnp.float32)


def flip(x):
    return jnp.transpose(x.astype(jnp.float32))


def head_cols(h):
    return slice(h * HEAD_DIM, (h + 1) * HEAD_DIM)


def forward_kernel(parts, block, docs, info_ref, *refs):
    pieces = refs[:parts]
    out_ref, lse_ref = refs[parts : parts + 2]
    bias_ref, open_ref, q_s, k_s, vt_s, top_s, sum_s, acc_s = refs[parts + 2 :]
    me = info_ref[0]
    wide = GROUP * HEAD_DIM
    factor = math.log2(math.e) / math.sqrt(HEAD_DIM)
    prepare(parts, block, docs, info_ref, bias_ref, open_ref)
    for d in range(parts):
        q_s[me ^ d] = pieces[d][:, :wide]
        k_s[me ^ d] = pieces[d][:, wide : wide + HEAD_DIM]
        vt_s[me ^ d] = flip(pieces[d][:, wide + HEAD_DIM :]).astype(jnp.bfloat16)

    def rows_of(qb, carry):
        top_s[...] = jnp.full_like(top_s, 2.0 * MASKED)
        sum_s[...] = jnp.zeros_like(sum_s)
        acc_s[...] = jnp.zeros_like(acc_s)

        def pair(back, carry):
            kb = qb - back
            bias = bias_ref.at[pair_index(qb, kb)]
            for h in range(GROUP):
                raw = mm(k_s[kb], q_s[qb, :, head_cols(h)], NT) * factor + bias[...]
                old = top_s[h]
                top = jnp.maximum(old, jnp.max(raw, axis=0, keepdims=True))
                shrink = jnp.exp2(old - top)
                raised = jnp.exp2(raw - top)
                top_s[h] = top
                sum_s[h] = sum_s[h] * shrink + jnp.sum(raised, axis=0, keepdims=True)
                acc_s[h] = acc_s[h] * shrink + mm(vt_s[kb], raised.astype(jnp.bfloat16))
            return carry

        lax.fori_loop(0, qb - open_ref[qb] + 1, pair, 0)
        for h in range(GROUP):
            out_ref[me ^ qb, head_cols(h)] = (acc_s[h] / sum_s[h]).astype(jnp.bfloat16)
            lse_ref[h, me ^ qb] = jnp.broadcast_to(top_s[h] + jnp.log2(sum_s[h]), (8, block))
        return carry

    lax.fori_loop(0, parts, rows_of, 0)


def whole_block(dims):
    return pl.BlockSpec(dims, lambda i, info: (0,) * len(dims))


def attention(info, pieces, token, parts, docs):
    block, cols = pieces[0].shape
    pairs = parts * (parts + 1) // 2
    wide = GROUP * HEAD_DIM
    vm = pltpu.VMEM
    return pl.pallas_call(
        functools.partial(forward_kernel, parts, block, docs),
        grid_spec=pltpu.PrefetchScalarGridSpec(
            num_scalar_prefetch=1,
            grid=(1,),
            in_specs=[whole_block((block, cols))] * parts,
            out_specs=[
                whole_block((parts, wide, block)),
                whole_block((GROUP, parts, 8, block)),
            ],
            scratch_shapes=[
                vm((pairs, block, block), jnp.float32),
                pltpu.SMEM((parts,), jnp.int32),
                vm((parts, block, wide), jnp.bfloat16),
                vm((parts, block, HEAD_DIM), jnp.bfloat16),
                vm((parts, HEAD_DIM, block), jnp.bfloat16),
                vm((GROUP, 1, block), jnp.float32),
                vm((GROUP, 1, block), jnp.float32),
                vm((GROUP, HEAD_DIM, block), jnp.float32),
            ],
        ),
        out_shape=[
            shape((parts, wide, block)),
            shape((GROUP, parts, 8, block), jnp.float32),
        ],
        compiler_params=params(16),
        cost_estimate=cost(8e9, 4 * parts * block * cols),
        name="attention",
    )(gate([info], token)[0], *pieces)


def backward_kernel(parts, block, docs, info_ref, *refs):
    pieces = refs[:parts]
    grad_ref, out_ref, lse_ref = refs[parts : parts + 3]
    res_ref = refs[parts + 3]
    bias_ref, open_ref, q_s, k_s, kt_s, v_s, dk_s, dv_s, dq_s, delta_s = refs[parts + 4 :]
    me = info_ref[0]
    wide = GROUP * HEAD_DIM
    scale = 1.0 / math.sqrt(HEAD_DIM)
    factor = math.log2(math.e) * scale
    prepare(parts, block, docs, info_ref, bias_ref, open_ref)
    for d in range(parts):
        q_s[me ^ d] = pieces[d][:, :wide]
        k_s[me ^ d] = pieces[d][:, wide : wide + HEAD_DIM]
        kt_s[me ^ d] = flip(pieces[d][:, wide : wide + HEAD_DIM]).astype(jnp.bfloat16)
        v_s[me ^ d] = pieces[d][:, wide + HEAD_DIM :]
    dk_s[...] = jnp.zeros_like(dk_s)
    dv_s[...] = jnp.zeros_like(dv_s)

    def rows_of(qb, carry):
        spot = me ^ qb
        dq_s[...] = jnp.zeros_like(dq_s)
        for h in range(GROUP):
            product = flip(grad_ref[spot, :, head_cols(h)]) * out_ref[spot, head_cols(h)].astype(
                jnp.float32
            )
            delta_s[h] = jnp.sum(product, axis=0, keepdims=True)

        def pair(back, carry):
            kb = qb - back
            bias = bias_ref.at[pair_index(qb, kb)]
            key, value = k_s[kb], v_s[kb]
            dk = dk_s[kb]
            dv = dv_s[kb]
            for h in range(GROUP):
                query, grad = q_s[qb, :, head_cols(h)], grad_ref[spot, :, head_cols(h)]
                raw = mm(key, query, NT) * factor + bias[...]
                probs = jnp.exp2(raw - lse_ref[h, spot, :1])
                dv += mm(probs.astype(jnp.bfloat16), grad)
                slope = (probs * (mm(value, grad, NT) - delta_s[h])).astype(jnp.bfloat16)
                dk += mm(slope, query)
                dq_s[h] += mm(kt_s[kb], slope)
            dk_s[kb] = dk
            dv_s[kb] = dv
            return carry

        lax.fori_loop(0, qb - open_ref[qb] + 1, pair, 0)
        for h in range(GROUP):
            res_ref[spot, :, head_cols(h)] = (jnp.transpose(dq_s[h]) * scale).astype(jnp.bfloat16)
        return carry

    lax.fori_loop(0, parts, rows_of, 0)
    for kb in range(parts):
        res_ref[me ^ kb, :, wide : wide + HEAD_DIM] = (dk_s[kb] * scale).astype(jnp.bfloat16)
        res_ref[me ^ kb, :, wide + HEAD_DIM :] = dv_s[kb].astype(jnp.bfloat16)


def attention_back(info, pieces, grads, out, lse, token, parts, docs, gp):
    block, cols = pieces[0].shape
    pairs = parts * (parts + 1) // 2
    wide = GROUP * HEAD_DIM
    vm = pltpu.VMEM
    return pl.pallas_call(
        functools.partial(backward_kernel, parts, block, docs),
        grid_spec=pltpu.PrefetchScalarGridSpec(
            num_scalar_prefetch=1,
            grid=(1,),
            in_specs=[whole_block((block, cols))] * parts
            + [
                pl.BlockSpec((parts, block, wide), lambda i, info: (0, 0, gp)),
                whole_block((parts, wide, block)),
                whole_block((GROUP, parts, 8, block)),
            ],
            out_specs=whole_block((parts, block, cols)),
            scratch_shapes=[
                vm((pairs, block, block), jnp.float32),
                pltpu.SMEM((parts,), jnp.int32),
                vm((parts, block, wide), jnp.bfloat16),
                vm((parts, block, HEAD_DIM), jnp.bfloat16),
                vm((parts, HEAD_DIM, block), jnp.bfloat16),
                vm((parts, block, HEAD_DIM), jnp.bfloat16),
                vm((parts, block, HEAD_DIM), jnp.float32),
                vm((parts, block, HEAD_DIM), jnp.float32),
                vm((GROUP, HEAD_DIM, block), jnp.float32),
                vm((GROUP, 1, block), jnp.float32),
            ],
        ),
        out_shape=shape((parts, block, cols)),
        compiler_params=params(20),
        cost_estimate=cost(14e9, 8 * parts * block * cols),
        name="attention_back",
    )(gate([info], token)[0], *pieces, grads, out, lse)


def place_of(share, order):
    out = 0 * share
    for k, bit in enumerate(order):
        out = out + ((share >> bit) & 1) * (1 << k)
    return out


def unplace(place, order):
    out = 0 * place
    for k, bit in enumerate(order):
        out = out + ((place >> k) & 1) * (1 << bit)
    return out


def reverse_bits(x, bits):
    out = 0 * x
    for b in range(bits):
        out = out + ((x >> b) & 1) * (1 << (bits - 1 - b))
    return out


def weight_kernel(parts, groups, width, order, info_ref, *refs):
    outs, lows, highs = refs[:groups], refs[groups : groups + 2], refs[groups + 2 : groups + 4]
    chunk = refs[groups + 4 : groups + 2 + parts]
    keep_ref, send_ref = refs[groups + 2 + parts :]
    odd = ((info_ref[1] >> order[0]) & 1) == 1
    rows = GROUP * HEAD_DIM
    grads = [jnp.concatenate([lows[d][...], highs[d][...]], axis=1) for d in range(2)]
    for gp in range(groups):
        total = mm(outs[gp][0], grads[0]) + mm(outs[gp][1], grads[1])
        for d in range(2, parts):
            total += mm(outs[gp][d], chunk[d - 2][...])
        low, high = total[:, :width], total[:, width:]
        spot = slice(gp * rows, (gp + 1) * rows)
        keep_ref[0, spot] = jnp.where(odd, high, low)
        send_ref[0, spot] = jnp.where(odd, low, high).astype(jnp.bfloat16)


def weight_terms(info, outs, near, chunk, token, shares, c, chunks, width, order):
    groups, parts = len(outs), 2 + len(chunk)
    _, rows, block = outs[0].shape
    half = shares // 2
    bits = half.bit_length() - 1
    spot = pl.BlockSpec((1, groups * rows, width), lambda t, info: (reverse_bits(t, bits), 0, 0))

    def mate(t, info):
        return t ^ (place_of(info[1], order) >> 1)

    def original(side):
        return pl.BlockSpec(
            (block, width),
            lambda t, info: (0, unplace(2 * mate(t, info) + side, order) * chunks + c),
        )

    return pl.pallas_call(
        functools.partial(weight_kernel, parts, groups, width, order),
        grid_spec=pltpu.PrefetchScalarGridSpec(
            num_scalar_prefetch=1,
            grid=(half,),
            in_specs=[pl.BlockSpec((parts, rows, block), lambda t, info: (0, 0, 0))] * groups
            + [original(0)] * 2
            + [original(1)] * 2
            + [pl.BlockSpec((block, 2 * width), lambda t, info: (0, mate(t, info)))] * len(chunk),
            out_specs=[spot, spot],
        ),
        out_shape=[
            shape((half, groups * rows, width), jnp.float32),
            shape((half, groups * rows, width)),
        ],
        compiler_params=params(16),
        cost_estimate=cost(
            2 * groups * rows * block * parts * shares * width, 8 * groups * rows * shares * width
        ),
        name="weight_terms",
    )(gate([info], token)[0], *outs, *near, *near, *chunk)


def merge_kernel(keep_low, keep_high, got_low, got_high, keep_ref, send_ref):
    keep_ref[...] = keep_low[...] + got_low[...].astype(jnp.float32)
    send_ref[...] = (keep_high[...] + got_high[...].astype(jnp.float32)).astype(jnp.bfloat16)


def merge(keep, got, token):
    count, rows, width = keep.shape
    half = count // 2
    keep = gate([keep], token)[0]
    low = pl.BlockSpec((1, rows, width), lambda t: (t, 0, 0))
    high = pl.BlockSpec((1, rows, width), lambda t: (t + half, 0, 0))
    return pl.pallas_call(
        merge_kernel,
        grid=(half,),
        in_specs=[low, high, low, high],
        out_specs=[low, low],
        out_shape=[
            shape((half, rows, width), jnp.float32),
            shape((half, rows, width)),
        ],
        compiler_params=params(12),
        cost_estimate=cost(0, 8 * count * rows * width),
        name="merge",
    )(keep, keep, got, got)


def finish_kernel(scale, keep_ref, got_ref, *refs):
    refs[-1][...] = (keep_ref[0] + got_ref[0].astype(jnp.float32)) * scale


def finish(keep, got, so_far, token, c, chunks, scale):
    _, rows, width = keep.shape
    more = [] if so_far is None else [so_far]
    step = rows // 2
    spec = pl.BlockSpec((1, step, width), lambda i: (0, i, 0))
    return pl.pallas_call(
        functools.partial(finish_kernel, scale),
        grid=(rows // step,),
        in_specs=[spec, spec] + [ANY] * len(more),
        out_specs=pl.BlockSpec((step, width), lambda i: (i, c)),
        out_shape=shape((rows, width * chunks), jnp.float32),
        input_output_aliases={2: 0} if more else {},
        compiler_params=params(8),
        cost_estimate=cost(0, 10 * rows * width),
        name="finish",
    )(gate([keep], token)[0], got, *more)


def project_kernel(parts, shares, width, chunks, orders, picked, first, last, *refs):
    w_ref, near = refs[0], refs[1:3]
    far = refs[3 : 3 + len(picked) * (parts - 2)]
    acc_ref, out_ref = refs[-2] if not first else None, refs[-1]
    columns = [(c, unplace(p, orders[c])) for c in picked for p in range(shares)]
    weights = jnp.concatenate([w_ref[:, column(j, c, chunks, width)] for c, j in columns], axis=1)
    for d in range(parts):
        if d < 2:
            rows = jnp.concatenate([near[d][:, column(j, c, chunks, width)] for c, j in columns], axis=1)
        else:
            mine = [far[i * (parts - 2) + d - 2][...] for i in range(len(picked))]
            rows = mine[0] if len(mine) == 1 else jnp.concatenate(mine, axis=1)
        total = mm(rows, weights, NT)
        if not first:
            total += acc_ref[d]
        out_ref[d] = total.astype(out_ref.dtype)


def project(out_weight, near, far, acc, token, orders, picked, shares, width, last):
    feats, model = out_weight.shape
    rows = near[0].shape[0]
    parts = 2 + len(far[0])
    step = min(256, feats)
    flat = [x for group in far for x in group]
    first = acc is None
    block = pl.BlockSpec((parts, rows, step), lambda i: (0, 0, i))
    return pl.pallas_call(
        functools.partial(
            project_kernel, parts, shares, width, len(orders), orders, picked, first, last
        ),
        grid=(feats // step,),
        in_specs=[pl.BlockSpec((step, model), lambda i: (i, 0))]
        + [pl.BlockSpec((rows, model), lambda i: (0, 0))] * 2
        + [pl.BlockSpec((rows, shares * width), lambda i: (0, 0))] * len(flat)
        + ([] if first else [block]),
        out_specs=block,
        out_shape=shape((parts, rows, feats), jnp.bfloat16 if last else jnp.float32),
        compiler_params=params(24),
        cost_estimate=cost(
            2 * feats * rows * parts * shares * width * len(picked), 4 * feats * rows * parts
        ),
        name="project",
    )(gate([out_weight], token)[0], *near, *flat, *([] if first else [acc]))


def body(grad_out, queries, keys, values, out_weight, doc_starts):
    parts, shares = lax.axis_size("seq"), lax.axis_size("dp")
    groups = KV_HEADS // parts
    docs = doc_starts.shape[-1]
    cotangent = grad_out[0]
    rows, model = cotangent.shape
    chunks = max(1, min(4, model // shares // 128))
    width = model // shares // chunks
    bits = tuple(range(shares.bit_length() - 1))
    turned = bits[1:] + bits[:1]
    orders = [turned if c == 1 else bits for c in range(chunks)]
    scale = 1.0 / math.sqrt(rows * parts * shares)
    info = jnp.concatenate(
        [
            jnp.stack([lax.axis_index("seq"), lax.axis_index("dp")]).astype(jnp.int32),
            doc_starts[0],
        ]
    )

    def over_seq(x, d):
        return lax.ppermute(x, "seq", [(i, i ^ d) for i in range(parts)])

    def over_dp(x, d):
        return lax.ppermute(x, "dp", [(i, i ^ d) for i in range(shares)])

    near = [cotangent, over_seq(cotangent, 1)]
    packed = [pack(info, queries[0], keys[0], values[0], parts, groups, gp) for gp in range(groups)]
    sends = pack_chunks(cotangent, orders, shares, width)

    pieces, fwd = [], []
    token = near[1]
    for gp in range(groups):
        sent = packed[gp]
        if gp:
            sent = [sent[0]] + gate(sent[1:], *pieces[-1][1:])
        pieces.append([sent[0]] + [over_seq(sent[d], d) for d in range(1, parts)])
    far_half = {}

    def send_chunk(c, *tokens):
        mine = gate([sends[c]], *tokens)[0]
        far_half[c] = [over_seq(mine, d) for d in range(2, parts, 2)]

    def chunk_pieces(c):
        out = []
        for x in far_half[c]:
            out += [x, over_seq(x, 1)]
        return out

    for gp in range(groups):
        fwd.append(attention(info, pieces[gp], token, parts, docs))
        token = fwd[-1][0]
        if gp == 0:
            send_chunk(0, token)
    outs = [pair[0] for pair in fwd]

    state = {}
    result = None

    def run_merge(c):
        nonlocal token, result
        keep, send, hop = state[c]
        got = over_dp(send, 1 << orders[c][hop])
        if hop == len(bits) - 1:
            result = finish(keep, got, result, token, c, chunks, scale)
            token = result
            state[c] = (None, None, None)
        else:
            keep, send = merge(keep, got, token)
            state[c] = (keep, send, hop + 1)
            token = send

    fars = {}
    back, results = {}, {}
    acc = None

    def weigh(c):
        nonlocal token
        fars[c] = chunk_pieces(c)
        keep, send = weight_terms(
            info, outs, near, fars[c], token, shares, c, chunks, width, orders[c]
        )
        state[c] = (keep, send, 0)
        token = send

    def project_step(picked, last):
        nonlocal token, acc
        acc = project(
            out_weight, near, [fars[c] for c in picked], acc, token, orders, picked, shares, width, last
        )
        token = acc

    def send_back(gp):
        nonlocal token
        res = attention_back(info, pieces[gp], acc, outs[gp], fwd[gp][1], token, parts, docs, gp)
        token = results[gp] = res
        back[gp] = [res[0], None] + [over_seq(res[d], d) for d in range(2, parts)]

    for c in range(1, chunks):
        if c == 1:
            send_chunk(1, *pieces[-1][1:])
        else:
            send_chunk(c, *far_half[c - 2])
    last = chunks - 1
    done = set()

    def step_merge(c):
        if c in state and c not in done:
            run_merge(c)
            if state[c][2] is None:
                done.add(c)

    weigh(0)
    if chunks > 1:
        weigh(1)
    step_merge(0)
    if chunks > 2:
        weigh(2)
    if last:
        project_step(list(range(last)), False)
    step_merge(1)
    if chunks > 3:
        weigh(3)
    project_step([last], True)
    step_merge(0)
    send_back(0)
    step_merge(2)
    step_merge(0)
    step_merge(1)
    for gp in range(1, groups):
        send_back(gp)
    step_merge(2)
    if groups > 1:
        token = gate([token], *back[0][2:])[0]
    step_merge(3)
    step_merge(1)
    step_merge(2)
    for gp in range(groups):
        mine = gate([results[gp][1]], *back[0][2:])[0]
        back[gp][1] = over_seq(mine, 1)
    step_merge(3)
    if groups > 1:
        token = gate([token], *back[groups - 1][2:])[0]
    for _ in bits:
        for c in range(chunks):
            step_merge(c)
    back = [x for gp in range(groups) for x in back[gp]]
    grad_q, grad_k, grad_v = unpack(info, back, parts, groups)
    return (grad_q[None], grad_k[None], grad_v[None], result)


def solution(mesh):
    return jax.shard_map(
        body,
        mesh=mesh,
        in_specs=(
            P("dp", "seq", None),
            P("dp", "seq", None),
            P("dp", "seq", None),
            P("dp", "seq", None),
            P("seq", None),
            P("dp", None),
        ),
        out_specs=(
            P("dp", "seq", None),
            P("dp", "seq", None),
            P("dp", "seq", None),
            P("seq", "dp"),
        ),
        check_vma=False,
    )
```

```python
import functools
import math

import jax
import jax.numpy as jnp
from jax import lax
from jax.experimental import pallas as pl
from jax.experimental.pallas import tpu as pltpu
from jax.sharding import PartitionSpec as P

HEADS = 32
KV_HEADS = 8
HEAD_DIM = 128
GROUP = HEADS // KV_HEADS
MASKED = -1e30
NT = (((1,), (1,)), ((), ()))
NN = (((1,), (0,)), ((), ()))


def mm(a, b, dims=NN):
    return lax.dot_general(a, b, dims, preferred_element_type=jnp.float32)


def params(mib):
    return pltpu.CompilerParams(vmem_limit_bytes=mib * 2**20)


def cost(us):
    return pl.CostEstimate(flops=int(us * 1.15e9), bytes_accessed=1024, transcendentals=0)


ANY = pl.BlockSpec(memory_space=pl.ANY)


def shape(dims, dtype=jnp.bfloat16):
    return jax.ShapeDtypeStruct(dims, dtype)


def gate(arrays, *tokens):
    flat = [x for token in tokens for x in (token if isinstance(token, tuple) else (token,))]
    return list(lax.optimization_barrier((*arrays, *flat)))[: len(arrays)]


def pack_kernel(parts, jobs, *refs):
    sources, outs, sem = refs[:3], refs[4:-1], refs[-1]
    me = lax.axis_index("seq")
    wide = GROUP * HEAD_DIM
    groups = KV_HEADS // parts
    copies = []
    for out, (d, members) in zip(outs, jobs):
        for slot, gp in enumerate(members):
            place = (me ^ d) * groups + gp
            start = slot * (wide + 2 * HEAD_DIM)
            for source, width in zip(sources, (wide, HEAD_DIM, HEAD_DIM)):
                copies.append(
                    pltpu.make_async_copy(
                        source.at[:, pl.ds(pl.multiple_of(place * width, width), width)],
                        out.at[:, pl.ds(start, width)],
                        sem.at[len(copies)],
                    )
                )
                start += width
    for copy in copies:
        copy.start()
    for copy in copies:
        copy.wait()


def pack(queries, keys, values, token, parts, jobs):
    rows = queries.shape[0]
    size = (GROUP + 2) * HEAD_DIM
    count = 3 * sum(len(members) for d, members in jobs)
    return pl.pallas_call(
        functools.partial(pack_kernel, parts, jobs),
        in_specs=[ANY] * 4,
        out_specs=[ANY] * len(jobs),
        out_shape=[shape((rows, size * len(members))) for d, members in jobs],
        scratch_shapes=[pltpu.SemaphoreType.DMA((count,))],
        compiler_params=params(60),
        cost_estimate=cost(2.0),
        name="pack",
    )(queries, keys, values, token)


def column(share, c, chunks, width):
    return slice((share * chunks + c) * width, (share * chunks + c + 1) * width)


def pack_chunks_kernel(chunks, shares, width, g_ref, *out_refs):
    for c in range(chunks):
        for share in range(shares):
            out_refs[c][:, share * width : (share + 1) * width] = g_ref[
                :, column(share, c, chunks, width)
            ]


def pack_chunks(cotangent, chunks, shares, width):
    rows, model = cotangent.shape
    step = min(64, rows)
    return pl.pallas_call(
        functools.partial(pack_chunks_kernel, chunks, shares, width),
        grid=(rows // step,),
        in_specs=[pl.BlockSpec((step, model), lambda i: (i, 0))],
        out_specs=[pl.BlockSpec((step, shares * width), lambda i: (i, 0))] * chunks,
        out_shape=[shape((rows, shares * width)) for c in range(chunks)],
        compiler_params=params(56),
        cost_estimate=cost(3.8),
        name="pack_chunks",
    )(cotangent)


def unpack_kernel(parts, groups, info_ref, *refs):
    count = parts * groups
    q_ref, k_ref, v_ref = refs[count:]
    wide = GROUP * HEAD_DIM
    for gp in range(groups):
        for d in range(parts):
            piece = refs[gp * parts + d]
            place = (info_ref[0] ^ d) * groups + gp
            q_ref[:, pl.ds(pl.multiple_of(place * wide, wide), wide)] = piece[:, :wide]
            narrow = pl.ds(pl.multiple_of(place * HEAD_DIM, HEAD_DIM), HEAD_DIM)
            k_ref[:, narrow] = piece[:, wide : wide + HEAD_DIM]
            v_ref[:, narrow] = piece[:, wide + HEAD_DIM :]


def unpack(info, pieces, parts, groups):
    rows, cols = pieces[0].shape
    wide = GROUP * HEAD_DIM
    step = min(64, rows)
    total = parts * groups
    widths = (total * wide, total * HEAD_DIM, total * HEAD_DIM)
    return pl.pallas_call(
        functools.partial(unpack_kernel, parts, groups),
        grid_spec=pltpu.PrefetchScalarGridSpec(
            num_scalar_prefetch=1,
            grid=(rows // step,),
            in_specs=[pl.BlockSpec((step, cols), lambda i, info: (i, 0))] * total,
            out_specs=[pl.BlockSpec((step, w), lambda i, info: (i, 0)) for w in widths],
        ),
        out_shape=[shape((rows, w)) for w in widths],
        compiler_params=params(16),
        cost_estimate=cost(2.8),
        name="unpack",
    )(info, *pieces)


def pair_index(qb, kb):
    return qb * (qb + 1) // 2 + kb


def prepare(parts, block, docs, info_ref, bias_ref, open_ref):
    down = lax.broadcasted_iota(jnp.int32, (block, block), 0)
    across = lax.broadcasted_iota(jnp.int32, (1, block), 1)
    for qb in range(parts):
        lanes = qb * block + across
        opening = jnp.zeros((1, block), jnp.int32)
        first = jnp.int32(0)
        for n in range(docs):
            start = info_ref[2 + n]
            opening = jnp.where(start <= lanes, jnp.maximum(opening, start), opening)
            first = jnp.where(start <= qb * block, jnp.maximum(first, start), first)
        open_ref[qb] = first // block
        for kb in range(qb + 1):
            seen = down >= opening - kb * block
            if kb == qb:
                seen = seen & (down <= across)
            bias_ref[pair_index(qb, kb)] = jnp.where(seen, 0.0, MASKED).astype(jnp.float32)


def flip(x):
    return jnp.transpose(x.astype(jnp.float32))


def head_cols(h):
    return slice(h * HEAD_DIM, (h + 1) * HEAD_DIM)


def forward_kernel(parts, block, docs, info_ref, *refs):
    pieces = refs[:parts]
    out_ref, lse_ref = refs[parts : parts + 2]
    bias_ref, open_ref, q_s, k_s, vt_s, top_s, sum_s, acc_s = refs[parts + 2 :]
    me = info_ref[0]
    wide = GROUP * HEAD_DIM
    factor = math.log2(math.e) / math.sqrt(HEAD_DIM)
    prepare(parts, block, docs, info_ref, bias_ref, open_ref)
    for d in range(parts):
        q_s[me ^ d] = pieces[d][:, :wide]
        k_s[me ^ d] = pieces[d][:, wide : wide + HEAD_DIM]
        vt_s[me ^ d] = flip(pieces[d][:, wide + HEAD_DIM :]).astype(jnp.bfloat16)

    def rows_of(qb, carry):
        top_s[...] = jnp.full_like(top_s, 2.0 * MASKED)
        sum_s[...] = jnp.zeros_like(sum_s)
        acc_s[...] = jnp.zeros_like(acc_s)

        def pair(back, carry):
            kb = qb - back
            bias = bias_ref.at[pair_index(qb, kb)]
            for h in range(GROUP):
                raw = mm(k_s[kb], q_s[qb, :, head_cols(h)], NT) * factor + bias[...]
                old = top_s[h]
                top = jnp.maximum(old, jnp.max(raw, axis=0, keepdims=True))
                shrink = jnp.exp2(old - top)
                raised = jnp.exp2(raw - top)
                top_s[h] = top
                sum_s[h] = sum_s[h] * shrink + jnp.sum(raised, axis=0, keepdims=True)
                acc_s[h] = acc_s[h] * shrink + mm(vt_s[kb], raised.astype(jnp.bfloat16))
            return carry

        lax.fori_loop(0, qb - open_ref[qb] + 1, pair, 0)
        for h in range(GROUP):
            out_ref[me ^ qb, head_cols(h)] = (acc_s[h] / sum_s[h]).astype(jnp.bfloat16)
            lse_ref[h, me ^ qb] = jnp.broadcast_to(top_s[h] + jnp.log2(sum_s[h]), (8, block))
        return carry

    lax.fori_loop(0, parts, rows_of, 0)


def whole_block(dims):
    return pl.BlockSpec(dims, lambda i, info: (0,) * len(dims))


def piece_block(rows, cols, at):
    return pl.BlockSpec((rows, cols), lambda i, info: (0, at))


def attention(info, pieces, token, parts, docs):
    block, cols = pieces[-1][0].shape
    pairs = parts * (parts + 1) // 2
    wide = GROUP * HEAD_DIM
    vm = pltpu.VMEM
    return pl.pallas_call(
        functools.partial(forward_kernel, parts, block, docs),
        grid_spec=pltpu.PrefetchScalarGridSpec(
            num_scalar_prefetch=1,
            grid=(1,),
            in_specs=[piece_block(block, cols, at) for x, at in pieces],
            out_specs=[
                whole_block((parts, wide, block)),
                whole_block((GROUP, parts, 8, block)),
            ],
            scratch_shapes=[
                vm((pairs, block, block), jnp.float32),
                pltpu.SMEM((parts,), jnp.int32),
                vm((parts, block, wide), jnp.bfloat16),
                vm((parts, block, HEAD_DIM), jnp.bfloat16),
                vm((parts, HEAD_DIM, block), jnp.bfloat16),
                vm((GROUP, 1, block), jnp.float32),
                vm((GROUP, 1, block), jnp.float32),
                vm((GROUP, HEAD_DIM, block), jnp.float32),
            ],
        ),
        out_shape=[
            shape((parts, wide, block)),
            shape((GROUP, parts, 8, block), jnp.float32),
        ],
        compiler_params=params(16),
        cost_estimate=cost(10.0),
        name="attention",
    )(gate([info], token)[0], *[x for x, at in pieces])


def backward_kernel(parts, block, docs, info_ref, *refs):
    pieces = refs[:parts]
    grad_ref, out_ref, lse_ref = refs[parts : parts + 3]
    res_ref = refs[parts + 3]
    bias_ref, open_ref, q_s, k_s, kt_s, v_s, dk_s, dv_s, dq_s, delta_s = refs[parts + 4 :]
    me = info_ref[0]
    wide = GROUP * HEAD_DIM
    scale = 1.0 / math.sqrt(HEAD_DIM)
    factor = math.log2(math.e) * scale
    prepare(parts, block, docs, info_ref, bias_ref, open_ref)
    for d in range(parts):
        q_s[me ^ d] = pieces[d][:, :wide]
        k_s[me ^ d] = pieces[d][:, wide : wide + HEAD_DIM]
        kt_s[me ^ d] = flip(pieces[d][:, wide : wide + HEAD_DIM]).astype(jnp.bfloat16)
        v_s[me ^ d] = pieces[d][:, wide + HEAD_DIM :]
    dk_s[...] = jnp.zeros_like(dk_s)
    dv_s[...] = jnp.zeros_like(dv_s)

    def rows_of(qb, carry):
        spot = me ^ qb
        dq_s[...] = jnp.zeros_like(dq_s)
        for h in range(GROUP):
            product = flip(grad_ref[spot, :, head_cols(h)]) * out_ref[spot, head_cols(h)].astype(
                jnp.float32
            )
            delta_s[h] = jnp.sum(product, axis=0, keepdims=True)

        def pair(back, carry):
            kb = qb - back
            bias = bias_ref.at[pair_index(qb, kb)]
            key, value = k_s[kb], v_s[kb]
            dk = dk_s[kb]
            dv = dv_s[kb]
            for h in range(GROUP):
                query, grad = q_s[qb, :, head_cols(h)], grad_ref[spot, :, head_cols(h)]
                raw = mm(key, query, NT) * factor + bias[...]
                probs = jnp.exp2(raw - lse_ref[h, spot, :1])
                dv += mm(probs.astype(jnp.bfloat16), grad)
                slope = (probs * (mm(value, grad, NT) - delta_s[h])).astype(jnp.bfloat16)
                dk += mm(slope, query)
                dq_s[h] += mm(kt_s[kb], slope)
            dk_s[kb] = dk
            dv_s[kb] = dv
            return carry

        lax.fori_loop(0, qb - open_ref[qb] + 1, pair, 0)
        for h in range(GROUP):
            res_ref[spot, :, head_cols(h)] = (jnp.transpose(dq_s[h]) * scale).astype(jnp.bfloat16)
        return carry

    lax.fori_loop(0, parts, rows_of, 0)
    for kb in range(parts):
        res_ref[me ^ kb, :, wide : wide + HEAD_DIM] = (dk_s[kb] * scale).astype(jnp.bfloat16)
        res_ref[me ^ kb, :, wide + HEAD_DIM :] = dv_s[kb].astype(jnp.bfloat16)


def attention_back(info, pieces, grads, out, lse, token, parts, docs, gp):
    block, cols = pieces[-1][0].shape
    pairs = parts * (parts + 1) // 2
    wide = GROUP * HEAD_DIM
    vm = pltpu.VMEM
    return pl.pallas_call(
        functools.partial(backward_kernel, parts, block, docs),
        grid_spec=pltpu.PrefetchScalarGridSpec(
            num_scalar_prefetch=1,
            grid=(1,),
            in_specs=[piece_block(block, cols, at) for x, at in pieces]
            + [
                pl.BlockSpec((parts, block, wide), lambda i, info: (0, 0, gp)),
                whole_block((parts, wide, block)),
                whole_block((GROUP, parts, 8, block)),
            ],
            out_specs=whole_block((parts, block, cols)),
            scratch_shapes=[
                vm((pairs, block, block), jnp.float32),
                pltpu.SMEM((parts,), jnp.int32),
                vm((parts, block, wide), jnp.bfloat16),
                vm((parts, block, HEAD_DIM), jnp.bfloat16),
                vm((parts, HEAD_DIM, block), jnp.bfloat16),
                vm((parts, block, HEAD_DIM), jnp.bfloat16),
                vm((parts, block, HEAD_DIM), jnp.float32),
                vm((parts, block, HEAD_DIM), jnp.float32),
                vm((GROUP, HEAD_DIM, block), jnp.float32),
                vm((GROUP, 1, block), jnp.float32),
            ],
        ),
        out_shape=shape((parts, block, cols)),
        compiler_params=params(20),
        cost_estimate=cost(3.0),
        name="attention_back",
    )(gate([info], token)[0], *[x for x, at in pieces], grads, out, lse)


def weight_kernel(parts, groups, width, across, info_ref, *refs):
    outs, lows, highs = refs[:groups], refs[groups : groups + 2], refs[groups + 2 : groups + 4]
    chunk = refs[groups + 4 : groups + 2 + parts]
    results = refs[groups + 2 + parts :]
    odd = (info_ref[1] & 1) == 1
    rows = GROUP * HEAD_DIM
    grads = [jnp.concatenate([lows[d][...], highs[d][...]], axis=1) for d in range(2)]
    for gp in range(groups):
        total = mm(outs[gp][0], grads[0]) + mm(outs[gp][1], grads[1])
        for d in range(2, parts):
            total += mm(outs[gp][d], chunk[d - 2][...])
        low, high = total[:, :width], total[:, width:]
        spot = slice(gp * rows, (gp + 1) * rows)
        keep = jnp.where(odd, high, low)
        send = jnp.where(odd, low, high).astype(jnp.bfloat16)
        if across:
            results[0][0, spot] = keep
            results[1][0, spot] = send
        else:
            results[0][0, 0, spot] = keep.astype(jnp.bfloat16)
            results[0][0, 1, spot] = send


def weight_terms(info, outs, near, chunk, token, shares, c, chunks, width, across):
    groups, parts = len(outs), 2 + len(chunk)
    _, rows, block = outs[0].shape
    half = shares // 2
    feats = groups * rows

    def original(side):
        return pl.BlockSpec((block, width), lambda t, info: (0, (2 * t + side) * chunks + c))

    if across:
        out_specs = [pl.BlockSpec((1, feats, width), lambda t, info: (t, 0, 0))] * 2
        out_shape = [shape((half, feats, width), jnp.float32), shape((half, feats, width))]
    else:
        out_specs = [pl.BlockSpec((1, 2, feats, width), lambda t, info: (t, 0, 0, 0))]
        out_shape = [shape((half, 2, feats, width))]
    return pl.pallas_call(
        functools.partial(weight_kernel, parts, groups, width, across),
        grid_spec=pltpu.PrefetchScalarGridSpec(
            num_scalar_prefetch=1,
            grid=(half,),
            in_specs=[pl.BlockSpec((parts, rows, block), lambda t, info: (0, 0, 0))] * groups
            + [original(0)] * 2
            + [original(1)] * 2
            + [pl.BlockSpec((block, 2 * width), lambda t, info: (0, t))] * len(chunk),
            out_specs=out_specs,
        ),
        out_shape=out_shape,
        compiler_params=params(16),
        cost_estimate=cost(1.0),
        name="weight_terms",
    )(gate([info], token)[0], *outs, *near, *near, *chunk)


def merge_kernel(keep_ref, got_ref, sum_ref):
    sum_ref[...] = (keep_ref[...] + got_ref[...].astype(jnp.float32)).astype(jnp.bfloat16)


def merge(keep, got, token):
    count, rows, width = keep.shape
    spec = pl.BlockSpec((1, rows, width), lambda t: (t, 0, 0))
    return pl.pallas_call(
        merge_kernel,
        grid=(count,),
        in_specs=[spec, spec],
        out_specs=spec,
        out_shape=shape((count, rows, width)),
        compiler_params=params(12),
        cost_estimate=cost(0.5),
        name="merge",
    )(gate([keep], token)[0], got)


def finish_kernel(scale, count, *refs):
    total = refs[0][...].astype(jnp.float32)
    for ref in refs[1:count]:
        total += ref[...].astype(jnp.float32)
    refs[-1][...] = total * scale


def finish(terms, so_far, token, c, chunks, scale):
    rows, width = terms[0].shape
    more = [] if so_far is None else [so_far]
    step = rows // 2
    spec = pl.BlockSpec((step, width), lambda i: (i, 0))
    return pl.pallas_call(
        functools.partial(finish_kernel, scale, len(terms)),
        grid=(rows // step,),
        in_specs=[spec] * len(terms) + [ANY] * len(more),
        out_specs=pl.BlockSpec((step, width), lambda i: (i, c)),
        out_shape=shape((rows, width * chunks), jnp.float32),
        input_output_aliases={len(terms): 0} if more else {},
        compiler_params=params(8),
        cost_estimate=cost(0.8),
        name="finish",
    )(*gate(terms, token), *more)


def project_kernel(parts, shares, width, chunks, picked, first, *refs):
    w_ref, near = refs[0], refs[1:3]
    far = refs[3 : 3 + len(picked) * (parts - 2)]
    acc_ref, out_ref = refs[-2] if not first else None, refs[-1]
    columns = [(c, share) for c in picked for share in range(shares)]
    weights = jnp.concatenate([w_ref[:, column(j, c, chunks, width)] for c, j in columns], axis=1)
    for d in range(parts):
        if d < 2:
            rows = jnp.concatenate([near[d][:, column(j, c, chunks, width)] for c, j in columns], axis=1)
        else:
            mine = [far[i * (parts - 2) + d - 2][...] for i in range(len(picked))]
            rows = mine[0] if len(mine) == 1 else jnp.concatenate(mine, axis=1)
        total = mm(rows, weights, NT)
        if not first:
            total += acc_ref[d]
        out_ref[d] = total.astype(out_ref.dtype)


def project(out_weight, near, far, acc, token, chunks, picked, shares, width, last):
    feats, model = out_weight.shape
    rows = near[0].shape[0]
    parts = 2 + len(far[0])
    step = min(256, feats)
    flat = [x for group in far for x in group]
    first = acc is None
    block = pl.BlockSpec((parts, rows, step), lambda i: (0, 0, i))
    return pl.pallas_call(
        functools.partial(
            project_kernel, parts, shares, width, chunks, picked, first
        ),
        grid=(feats // step,),
        in_specs=[pl.BlockSpec((step, model), lambda i: (i, 0))]
        + [pl.BlockSpec((rows, model), lambda i: (0, 0))] * 2
        + [pl.BlockSpec((rows, shares * width), lambda i: (0, 0))] * len(flat)
        + ([] if first else [block]),
        out_specs=block,
        out_shape=shape((parts, rows, feats), jnp.bfloat16 if last else jnp.float32),
        compiler_params=params(24),
        cost_estimate=cost(0.7 * len(picked)),
        name="project",
    )(gate([out_weight], token)[0], *near, *flat, *([] if first else [acc]))


def body(grad_out, queries, keys, values, out_weight, doc_starts):
    parts, shares = lax.axis_size("seq"), lax.axis_size("dp")
    groups = KV_HEADS // parts
    docs = doc_starts.shape[-1]
    cotangent = grad_out[0]
    rows, model = cotangent.shape
    chunks = max(1, min(4, model // shares // 128))
    width = model // shares // chunks
    scale = 1.0 / math.sqrt(rows * parts * shares)
    columns = [list(range(side, shares, 2)) for side in range(2)]
    info = jnp.concatenate(
        [
            jnp.stack([lax.axis_index("seq"), lax.axis_index("dp")]).astype(jnp.int32),
            doc_starts[0],
        ]
    )

    def over_seq(x, d):
        return lax.ppermute(x, "seq", [(i, i ^ d) for i in range(parts)])

    def across(x):
        return lax.ppermute(x, "dp", [(i, i ^ 1) for i in range(shares)])

    def along(x):
        return lax.psum_scatter(
            x, "dp", scatter_dimension=0, axis_index_groups=columns, tiled=True
        )[0]

    far = range(2, parts)
    all_groups = tuple(range(groups))
    sources = (queries[0], keys[0], values[0])
    packed = [pack(*sources, doc_starts, parts, tuple((d, (0,)) for d in far))]
    rest = [(d, (gp,)) for gp in range(1, groups) for d in far]
    rest = pack(*sources, packed[0][0], parts, tuple([(0, all_groups), (1, all_groups)] + rest))
    for gp in range(1, groups):
        packed.append(rest[2 + (gp - 1) * len(far) : 2 + gp * len(far)])
    sent_far = [[over_seq(x, d) for x, d in zip(group, far)] for group in packed]
    core = over_seq(rest[1], 1)
    pieces = [[(rest[0], gp), (core, gp)] + [(x, 0) for x in sent_far[gp]] for gp in range(groups)]
    sends = pack_chunks(gate([cotangent], rest[0])[0], chunks, shares, width)
    near = [cotangent, over_seq(gate([cotangent], *sent_far[0], sends[-1])[0], 1)]

    far_half = {}

    def send_chunk(c, *tokens):
        mine = gate([sends[c]], *tokens)[0]
        far_half[c] = [over_seq(mine, d) for d in range(2, parts, 2)]

    fwd = []
    token = sends[-1]
    for gp in range(groups):
        fwd.append(attention(info, pieces[gp], token, parts, docs))
        token = fwd[-1][0]
        if gp == 0:
            send_chunk(0, *sent_far[0])
            token = (token, near[1])
    for c in range(1, chunks):
        if c < groups:
            send_chunk(c, *sent_far[c])
        else:
            send_chunk(c, *far_half[max(0, c - groups)])
    outs = [pair[0] for pair in fwd]

    fars, waiting, back, results = {}, {}, {}, {}
    acc = weight_grad = None

    def weigh(c):
        nonlocal token
        fars[c] = []
        for x in gate(far_half[c], token):
            fars[c] += [x, over_seq(x, 1)]
        first_across = c != 0
        terms = weight_terms(
            info, outs, near, fars[c], token, shares, c, chunks, width, first_across
        )
        token = terms[-1]
        if first_across:
            waiting[c] = (terms[0], across(terms[1]))
        else:
            waiting[c] = along(terms[0])

    def combine(c):
        nonlocal token
        if c != 0:
            token = merge(*waiting[c], token)
            waiting[c] = (along(token),)
        else:
            keep, send = gate([waiting[c]], token)[0]
            waiting[c] = (keep, across(send))

    def settle(c):
        nonlocal token, weight_grad
        token = weight_grad = finish(waiting[c], weight_grad, token, c, chunks, scale)

    def project_step(picked, last):
        nonlocal token, acc
        token = acc = project(
            out_weight, near, [fars[c] for c in picked], acc, token, chunks, picked, shares, width, last
        )

    def send_back(gp):
        nonlocal token
        res = attention_back(info, pieces[gp], acc, outs[gp], fwd[gp][1], token, parts, docs, gp)
        token = results[gp] = res
        back[gp] = [res[0], None] + [over_seq(res[d], d) for d in far]

    last = chunks - 1
    for c in range(last):
        weigh(c)
    if last:
        project_step(list(range(last)), False)
        combine(0)
    weigh(last)
    project_step([last], True)
    if last > 1:
        combine(1)
    send_back(0)
    for c in range(2, last):
        combine(c)
    if last:
        settle(0)
    for gp in range(1, groups):
        send_back(gp)
    if groups > 1:
        token = (token, *back[0][2:])
    if last:
        combine(last)
    else:
        combine(0)
    token = (token, *back[groups - 1][2:])
    for c in range(1, last):
        settle(c)
    core = over_seq(jnp.concatenate([results[gp][1] for gp in range(groups)], axis=0), 1)
    for gp in range(groups):
        back[gp][1] = core[gp * rows : (gp + 1) * rows]
    back = [x for gp in range(groups) for x in back[gp]]
    grad_q, grad_k, grad_v = unpack(gate([info], token)[0], back, parts, groups)
    token = grad_q
    settle(last)
    return (grad_q[None], grad_k[None], grad_v[None], weight_grad)


def solution(mesh):
    return jax.shard_map(
        body,
        mesh=mesh,
        in_specs=(
            P("dp", "seq", None),
            P("dp", "seq", None),
            P("dp", "seq", None),
            P("dp", "seq", None),
            P("seq", None),
            P("dp", None),
        ),
        out_specs=(
            P("dp", "seq", None),
            P("dp", "seq", None),
            P("dp", "seq", None),
            P("seq", "dp"),
        ),
        check_vma=False,
    )
```

```python
import functools
import math

import jax
import jax.numpy as jnp
from jax import lax
from jax.experimental import pallas as pl
from jax.experimental.pallas import tpu as pltpu
from jax.sharding import PartitionSpec as P

HEADS = 32
KV_HEADS = 8
HEAD_DIM = 128
GROUP = HEADS // KV_HEADS
MASKED = -1e30
NT = (((1,), (1,)), ((), ()))
NN = (((1,), (0,)), ((), ()))


def mm(a, b, dims=NN):
    return lax.dot_general(a, b, dims, preferred_element_type=jnp.float32)


def params(mib):
    return pltpu.CompilerParams(vmem_limit_bytes=mib * 2**20)


def cost(us):
    return pl.CostEstimate(flops=int(us * 0.25 * 1.15e9), bytes_accessed=1024, transcendentals=0)


ANY = pl.BlockSpec(memory_space=pl.ANY)


def shape(dims, dtype=jnp.bfloat16):
    return jax.ShapeDtypeStruct(dims, dtype)


def gate(arrays, *tokens):
    flat = [x for token in tokens for x in (token if isinstance(token, tuple) else (token,))]
    return list(lax.optimization_barrier((*arrays, *flat)))[: len(arrays)]


def pack_kernel(jobs, me_ref, *refs):
    wide = GROUP * HEAD_DIM
    size = wide + 2 * HEAD_DIM
    sources, outs = iter(refs[: len(refs) - len(jobs)]), refs[len(refs) - len(jobs) :]
    for out, (d, members) in zip(outs, jobs):
        for slot in range(len(members)):
            start = slot * size
            for width in (wide, HEAD_DIM, HEAD_DIM):
                out[:, start : start + width] = next(sources)[...]
                start += width


def pack(me, sources, parts, jobs):
    rows = sources[0].shape[0]
    groups = KV_HEADS // parts
    wide = GROUP * HEAD_DIM
    size = wide + 2 * HEAD_DIM
    step = min(128, rows)

    def pick(width, d, gp):
        return pl.BlockSpec((step, width), lambda i, me: (i, (me[0] ^ d) * groups + gp))

    specs = [
        pick(width, d, gp)
        for d, members in jobs
        for gp in members
        for width in (wide, HEAD_DIM, HEAD_DIM)
    ]
    return pl.pallas_call(
        functools.partial(pack_kernel, jobs),
        grid_spec=pltpu.PrefetchScalarGridSpec(
            num_scalar_prefetch=1,
            grid=(rows // step,),
            in_specs=specs,
            out_specs=[
                pl.BlockSpec((step, size * len(members)), lambda i, me: (i, 0))
                for d, members in jobs
            ],
        ),
        out_shape=[shape((rows, size * len(members))) for d, members in jobs],
        compiler_params=params(60),
        cost_estimate=cost(2.0),
        name="pack",
    )(me, *sources * (len(specs) // 3))


def column(share, c, chunks, width):
    return slice((share * chunks + c) * width, (share * chunks + c + 1) * width)


def pack_chunks_kernel(orders, shares, width, g_ref, *out_refs):
    for c, order in enumerate(orders):
        for place in range(shares):
            share = unplace(place, order)
            out_refs[c][:, place * width : (place + 1) * width] = g_ref[
                :, column(share, c, len(orders), width)
            ]


def pack_chunks(cotangent, orders, shares, width):
    rows, model = cotangent.shape
    step = min(64, rows)
    return pl.pallas_call(
        functools.partial(pack_chunks_kernel, orders, shares, width),
        grid=(rows // step,),
        in_specs=[pl.BlockSpec((step, model), lambda i: (i, 0))],
        out_specs=[pl.BlockSpec((step, shares * width), lambda i: (i, 0))] * len(orders),
        out_shape=[shape((rows, shares * width)) for order in orders],
        compiler_params=params(40),
        cost_estimate=cost(3.8),
        name="pack_chunks",
    )(cotangent)


def unpack_kernel(parts, groups, info_ref, *refs):
    count = parts * groups
    q_ref, k_ref, v_ref = refs[count:]
    wide = GROUP * HEAD_DIM
    for gp in range(groups):
        for d in range(parts):
            piece = refs[gp * parts + d]
            place = (info_ref[0] ^ d) * groups + gp
            q_ref[:, pl.ds(pl.multiple_of(place * wide, wide), wide)] = piece[:, :wide]
            narrow = pl.ds(pl.multiple_of(place * HEAD_DIM, HEAD_DIM), HEAD_DIM)
            k_ref[:, narrow] = piece[:, wide : wide + HEAD_DIM]
            v_ref[:, narrow] = piece[:, wide + HEAD_DIM :]


def unpack(info, pieces, parts, groups):
    rows, cols = pieces[0].shape
    wide = GROUP * HEAD_DIM
    step = min(64, rows)
    total = parts * groups
    widths = (total * wide, total * HEAD_DIM, total * HEAD_DIM)
    return pl.pallas_call(
        functools.partial(unpack_kernel, parts, groups),
        grid_spec=pltpu.PrefetchScalarGridSpec(
            num_scalar_prefetch=1,
            grid=(rows // step,),
            in_specs=[pl.BlockSpec((step, cols), lambda i, info: (i, 0))] * total,
            out_specs=[pl.BlockSpec((step, w), lambda i, info: (i, 0)) for w in widths],
        ),
        out_shape=[shape((rows, w)) for w in widths],
        compiler_params=params(40),
        cost_estimate=cost(2.8),
        name="unpack",
    )(info, *pieces)


def pair_index(qb, kb):
    return qb * (qb + 1) // 2 + kb


def prepare(parts, block, docs, info_ref, bias_ref, open_ref):
    down = lax.broadcasted_iota(jnp.int32, (block, block), 0)
    across = lax.broadcasted_iota(jnp.int32, (1, block), 1)
    for qb in range(parts):
        lanes = qb * block + across
        opening = jnp.zeros((1, block), jnp.int32)
        first = jnp.int32(0)
        for n in range(docs):
            start = info_ref[2 + n]
            opening = jnp.where(start <= lanes, jnp.maximum(opening, start), opening)
            first = jnp.where(start <= qb * block, jnp.maximum(first, start), first)
        open_ref[qb] = first // block
        for kb in range(qb + 1):
            seen = down >= opening - kb * block
            if kb == qb:
                seen = seen & (down <= across)
            bias_ref[pair_index(qb, kb)] = jnp.where(seen, 0.0, MASKED).astype(jnp.float32)


def flip(x):
    return jnp.transpose(x.astype(jnp.float32))


def head_cols(h):
    return slice(h * HEAD_DIM, (h + 1) * HEAD_DIM)


def forward_kernel(parts, block, docs, info_ref, *refs):
    pieces = refs[:parts]
    out_ref, lse_ref = refs[parts : parts + 2]
    bias_ref, open_ref, q_s, k_s, vt_s, top_s, sum_s, acc_s = refs[parts + 2 :]
    me = info_ref[0]
    wide = GROUP * HEAD_DIM
    factor = math.log2(math.e) / math.sqrt(HEAD_DIM)
    prepare(parts, block, docs, info_ref, bias_ref, open_ref)
    for d in range(parts):
        q_s[me ^ d] = pieces[d][:, :wide]
        k_s[me ^ d] = pieces[d][:, wide : wide + HEAD_DIM]
        vt_s[me ^ d] = flip(pieces[d][:, wide + HEAD_DIM :]).astype(jnp.bfloat16)

    def rows_of(qb, carry):
        top_s[...] = jnp.full_like(top_s, 2.0 * MASKED)
        sum_s[...] = jnp.zeros_like(sum_s)
        acc_s[...] = jnp.zeros_like(acc_s)

        def pair(back, carry):
            kb = qb - back
            bias = bias_ref.at[pair_index(qb, kb)]
            for h in range(GROUP):
                raw = mm(k_s[kb], q_s[qb, :, head_cols(h)], NT) * factor + bias[...]
                old = top_s[h]
                top = jnp.maximum(old, jnp.max(raw, axis=0, keepdims=True))
                shrink = jnp.exp2(old - top)
                raised = jnp.exp2(raw - top)
                top_s[h] = top
                sum_s[h] = sum_s[h] * shrink + jnp.sum(raised, axis=0, keepdims=True)
                acc_s[h] = acc_s[h] * shrink + mm(vt_s[kb], raised.astype(jnp.bfloat16))
            return carry

        lax.fori_loop(0, qb - open_ref[qb] + 1, pair, 0)
        for h in range(GROUP):
            out_ref[me ^ qb, head_cols(h)] = (acc_s[h] / sum_s[h]).astype(jnp.bfloat16)
            lse_ref[h, me ^ qb] = jnp.broadcast_to(top_s[h] + jnp.log2(sum_s[h]), (8, block))
        return carry

    lax.fori_loop(0, parts, rows_of, 0)


def whole_block(dims):
    return pl.BlockSpec(dims, lambda i, info: (0,) * len(dims))


def piece_block(rows, cols, at):
    return pl.BlockSpec((rows, cols), lambda i, info: (0, at))


def attention(info, pieces, token, parts, docs):
    block, cols = pieces[-1][0].shape
    pairs = parts * (parts + 1) // 2
    wide = GROUP * HEAD_DIM
    vm = pltpu.VMEM
    return pl.pallas_call(
        functools.partial(forward_kernel, parts, block, docs),
        grid_spec=pltpu.PrefetchScalarGridSpec(
            num_scalar_prefetch=1,
            grid=(1,),
            in_specs=[piece_block(block, cols, at) for x, at in pieces],
            out_specs=[
                whole_block((parts, wide, block)),
                whole_block((GROUP, parts, 8, block)),
            ],
            scratch_shapes=[
                vm((pairs, block, block), jnp.float32),
                pltpu.SMEM((parts,), jnp.int32),
                vm((parts, block, wide), jnp.bfloat16),
                vm((parts, block, HEAD_DIM), jnp.bfloat16),
                vm((parts, HEAD_DIM, block), jnp.bfloat16),
                vm((GROUP, 1, block), jnp.float32),
                vm((GROUP, 1, block), jnp.float32),
                vm((GROUP, HEAD_DIM, block), jnp.float32),
            ],
        ),
        out_shape=[
            shape((parts, wide, block)),
            shape((GROUP, parts, 8, block), jnp.float32),
        ],
        compiler_params=params(40),
        cost_estimate=cost(10.0),
        name="attention",
    )(gate([info], token)[0], *[x for x, at in pieces])


def backward_kernel(parts, block, docs, info_ref, *refs):
    pieces = refs[:parts]
    grad_ref, out_ref, lse_ref = refs[parts : parts + 3]
    res_ref = refs[parts + 3]
    bias_ref, open_ref, q_s, k_s, kt_s, v_s, dk_s, dv_s, dq_s, delta_s = refs[parts + 4 :]
    me = info_ref[0]
    wide = GROUP * HEAD_DIM
    scale = 1.0 / math.sqrt(HEAD_DIM)
    factor = math.log2(math.e) * scale
    prepare(parts, block, docs, info_ref, bias_ref, open_ref)
    for d in range(parts):
        q_s[me ^ d] = pieces[d][:, :wide]
        k_s[me ^ d] = pieces[d][:, wide : wide + HEAD_DIM]
        kt_s[me ^ d] = flip(pieces[d][:, wide : wide + HEAD_DIM]).astype(jnp.bfloat16)
        v_s[me ^ d] = pieces[d][:, wide + HEAD_DIM :]
    dk_s[...] = jnp.zeros_like(dk_s)
    dv_s[...] = jnp.zeros_like(dv_s)

    def rows_of(qb, carry):
        spot = me ^ qb
        dq_s[...] = jnp.zeros_like(dq_s)
        for h in range(GROUP):
            product = flip(grad_ref[spot, :, head_cols(h)]) * out_ref[spot, head_cols(h)].astype(
                jnp.float32
            )
            delta_s[h] = jnp.sum(product, axis=0, keepdims=True)

        def pair(back, carry):
            kb = qb - back
            bias = bias_ref.at[pair_index(qb, kb)]
            key, value = k_s[kb], v_s[kb]
            dk = dk_s[kb]
            dv = dv_s[kb]
            for h in range(GROUP):
                query, grad = q_s[qb, :, head_cols(h)], grad_ref[spot, :, head_cols(h)]
                raw = mm(key, query, NT) * factor + bias[...]
                probs = jnp.exp2(raw - lse_ref[h, spot, :1])
                dv += mm(probs.astype(jnp.bfloat16), grad)
                slope = (probs * (mm(value, grad, NT) - delta_s[h])).astype(jnp.bfloat16)
                dk += mm(slope, query)
                dq_s[h] += mm(kt_s[kb], slope)
            dk_s[kb] = dk
            dv_s[kb] = dv
            return carry

        lax.fori_loop(0, qb - open_ref[qb] + 1, pair, 0)
        for h in range(GROUP):
            res_ref[spot, :, head_cols(h)] = (jnp.transpose(dq_s[h]) * scale).astype(jnp.bfloat16)
        return carry

    lax.fori_loop(0, parts, rows_of, 0)
    for kb in range(parts):
        res_ref[me ^ kb, :, wide : wide + HEAD_DIM] = (dk_s[kb] * scale).astype(jnp.bfloat16)
        res_ref[me ^ kb, :, wide + HEAD_DIM :] = dv_s[kb].astype(jnp.bfloat16)


def attention_back(info, pieces, grads, out, lse, token, parts, docs, gp):
    block, cols = pieces[-1][0].shape
    pairs = parts * (parts + 1) // 2
    wide = GROUP * HEAD_DIM
    vm = pltpu.VMEM
    return pl.pallas_call(
        functools.partial(backward_kernel, parts, block, docs),
        grid_spec=pltpu.PrefetchScalarGridSpec(
            num_scalar_prefetch=1,
            grid=(1,),
            in_specs=[piece_block(block, cols, at) for x, at in pieces]
            + [
                pl.BlockSpec((parts, block, wide), lambda i, info: (0, 0, gp)),
                whole_block((parts, wide, block)),
                whole_block((GROUP, parts, 8, block)),
            ],
            out_specs=whole_block((parts, block, cols)),
            scratch_shapes=[
                vm((pairs, block, block), jnp.float32),
                pltpu.SMEM((parts,), jnp.int32),
                vm((parts, block, wide), jnp.bfloat16),
                vm((parts, block, HEAD_DIM), jnp.bfloat16),
                vm((parts, HEAD_DIM, block), jnp.bfloat16),
                vm((parts, block, HEAD_DIM), jnp.bfloat16),
                vm((parts, block, HEAD_DIM), jnp.float32),
                vm((parts, block, HEAD_DIM), jnp.float32),
                vm((GROUP, HEAD_DIM, block), jnp.float32),
                vm((GROUP, 1, block), jnp.float32),
            ],
        ),
        out_shape=shape((parts, block, cols)),
        compiler_params=params(40),
        cost_estimate=cost(12.5),
        name="attention_back",
    )(gate([info], token)[0], *[x for x, at in pieces], grads, out, lse)


def place_of(share, order):
    out = 0 * share
    for k, bit in enumerate(order):
        out = out + ((share >> bit) & 1) * (1 << k)
    return out


def unplace(place, order):
    out = 0 * place
    for k, bit in enumerate(order):
        out = out + ((place >> k) & 1) * (1 << bit)
    return out


def reverse_bits(x, bits):
    out = 0 * x
    for b in range(bits):
        out = out + ((x >> b) & 1) * (1 << (bits - 1 - b))
    return out


def weight_kernel(parts, groups, width, order, info_ref, *refs):
    outs, lows, highs = refs[:groups], refs[groups : groups + 2], refs[groups + 2 : groups + 4]
    chunk = refs[groups + 4 : groups + 2 + parts]
    keep_ref, send_ref = refs[groups + 2 + parts :]
    odd = ((info_ref[1] >> order[0]) & 1) == 1
    rows = GROUP * HEAD_DIM
    grads = [jnp.concatenate([lows[d][...], highs[d][...]], axis=1) for d in range(2)]
    for gp in range(groups):
        total = mm(outs[gp][0], grads[0]) + mm(outs[gp][1], grads[1])
        for d in range(2, parts):
            total += mm(outs[gp][d], chunk[d - 2][...])
        low, high = total[:, :width], total[:, width:]
        spot = slice(gp * rows, (gp + 1) * rows)
        keep_ref[0, spot] = jnp.where(odd, high, low)
        send_ref[0, spot] = jnp.where(odd, low, high).astype(jnp.bfloat16)


def weight_terms(info, outs, near, chunk, token, shares, c, chunks, width, order):
    groups, parts = len(outs), 2 + len(chunk)
    _, rows, block = outs[0].shape
    half = shares // 2
    bits = half.bit_length() - 1
    spot = pl.BlockSpec((1, groups * rows, width), lambda t, info: (reverse_bits(t, bits), 0, 0))

    def mate(t, info):
        return t ^ (place_of(info[1], order) >> 1)

    def original(side):
        return pl.BlockSpec(
            (block, width),
            lambda t, info: (0, unplace(2 * mate(t, info) + side, order) * chunks + c),
        )

    return pl.pallas_call(
        functools.partial(weight_kernel, parts, groups, width, order),
        grid_spec=pltpu.PrefetchScalarGridSpec(
            num_scalar_prefetch=1,
            grid=(half,),
            in_specs=[pl.BlockSpec((parts, rows, block), lambda t, info: (0, 0, 0))] * groups
            + [original(0)] * 2
            + [original(1)] * 2
            + [pl.BlockSpec((block, 2 * width), lambda t, info: (0, mate(t, info)))] * len(chunk),
            out_specs=[spot, spot],
        ),
        out_shape=[
            shape((half, groups * rows, width), jnp.float32),
            shape((half, groups * rows, width)),
        ],
        compiler_params=params(40),
        cost_estimate=cost(4.3),
        name="weight_terms",
    )(gate([info], token)[0], *outs, *near, *near, *chunk)


def merge_kernel(keep_low, keep_high, got_low, got_high, keep_ref, send_ref):
    keep_ref[...] = keep_low[...] + got_low[...].astype(jnp.float32)
    send_ref[...] = (keep_high[...] + got_high[...].astype(jnp.float32)).astype(jnp.bfloat16)


def merge(keep, got, token):
    count, rows, width = keep.shape
    half = count // 2
    keep = gate([keep], token)[0]
    low = pl.BlockSpec((1, rows, width), lambda t: (t, 0, 0))
    high = pl.BlockSpec((1, rows, width), lambda t: (t + half, 0, 0))
    return pl.pallas_call(
        merge_kernel,
        grid=(half,),
        in_specs=[low, high, low, high],
        out_specs=[low, low],
        out_shape=[
            shape((half, rows, width), jnp.float32),
            shape((half, rows, width)),
        ],
        compiler_params=params(40),
        cost_estimate=cost(0.5),
        name="merge",
    )(keep, keep, got, got)


def finish_kernel(scale, keep_ref, got_ref, *refs):
    refs[-1][...] = (keep_ref[0] + got_ref[0].astype(jnp.float32)) * scale


def finish(keep, got, so_far, token, c, chunks, scale):
    _, rows, width = keep.shape
    more = [] if so_far is None else [so_far]
    step = rows // 2
    spec = pl.BlockSpec((1, step, width), lambda i: (0, i, 0))
    return pl.pallas_call(
        functools.partial(finish_kernel, scale),
        grid=(rows // step,),
        in_specs=[spec, spec] + [ANY] * len(more),
        out_specs=pl.BlockSpec((step, width), lambda i: (i, c)),
        out_shape=shape((rows, width * chunks), jnp.float32),
        input_output_aliases={2: 0} if more else {},
        compiler_params=params(40),
        cost_estimate=cost(0.8),
        name="finish",
    )(gate([keep], token)[0], got, *more)


def project_kernel(parts, shares, width, chunks, orders, picked, first, last, *refs):
    w_ref, near = refs[0], refs[1:3]
    far = refs[3 : 3 + len(picked) * (parts - 2)]
    acc_ref, out_ref = refs[-2] if not first else None, refs[-1]
    columns = [(c, unplace(p, orders[c])) for c in picked for p in range(shares)]
    weights = jnp.concatenate([w_ref[:, column(j, c, chunks, width)] for c, j in columns], axis=1)
    for d in range(parts):
        if d < 2:
            rows = jnp.concatenate([near[d][:, column(j, c, chunks, width)] for c, j in columns], axis=1)
        else:
            mine = [far[i * (parts - 2) + d - 2][...] for i in range(len(picked))]
            rows = mine[0] if len(mine) == 1 else jnp.concatenate(mine, axis=1)
        total = mm(rows, weights, NT)
        if not first:
            total += acc_ref[d]
        out_ref[d] = total.astype(out_ref.dtype)


def project(out_weight, near, far, acc, token, orders, picked, shares, width, last):
    feats, model = out_weight.shape
    rows = near[0].shape[0]
    parts = 2 + len(far[0])
    step = min(256, feats)
    flat = [x for group in far for x in group]
    first = acc is None
    block = pl.BlockSpec((parts, rows, step), lambda i: (0, 0, i))
    return pl.pallas_call(
        functools.partial(
            project_kernel, parts, shares, width, len(orders), orders, picked, first, last
        ),
        grid=(feats // step,),
        in_specs=[pl.BlockSpec((step, model), lambda i: (i, 0))]
        + [pl.BlockSpec((rows, model), lambda i: (0, 0))] * 2
        + [pl.BlockSpec((rows, shares * width), lambda i: (0, 0))] * len(flat)
        + ([] if first else [block]),
        out_specs=block,
        out_shape=shape((parts, rows, feats), jnp.bfloat16 if last else jnp.float32),
        compiler_params=params(40),
        cost_estimate=cost(2.5 * len(picked)),
        name="project",
    )(gate([out_weight], token)[0], *near, *flat, *([] if first else [acc]))


def body(grad_out, queries, keys, values, out_weight, doc_starts):
    parts, shares = lax.axis_size("seq"), lax.axis_size("dp")
    groups = KV_HEADS // parts
    docs = doc_starts.shape[-1]
    cotangent = grad_out[0]
    rows, model = cotangent.shape
    chunks = max(1, min(4, model // shares // 128))
    width = model // shares // chunks
    bits = tuple(range(shares.bit_length() - 1))
    turned = bits[1:] + bits[:1]
    orders = [turned if c == 0 else bits for c in range(chunks)]
    scale = 1.0 / math.sqrt(rows * parts * shares)
    info = jnp.concatenate(
        [
            jnp.stack([lax.axis_index("seq"), lax.axis_index("dp")]).astype(jnp.int32),
            doc_starts[0],
        ]
    )

    def over_seq(x, d):
        return lax.ppermute(x, "seq", [(i, i ^ d) for i in range(parts)])

    def over_dp(x, d):
        return lax.ppermute(x, "dp", [(i, i ^ d) for i in range(shares)])

    far = range(2, parts)
    all_groups = tuple(range(groups))
    me = lax.axis_index("seq").astype(jnp.int32).reshape(1)
    sources = (queries[0], keys[0], values[0])
    packed = [pack(me, sources, parts, tuple((d, (0,)) for d in far))]
    rest = [(d, (gp,)) for gp in range(1, groups) for d in far]
    rest = pack(
        gate([me], packed[0][0])[0],
        sources,
        parts,
        tuple([(0, all_groups), (1, all_groups)] + rest),
    )
    for gp in range(1, groups):
        packed.append(rest[2 + (gp - 1) * len(far) : 2 + gp * len(far)])
    sent_far = [[over_seq(x, d) for x, d in zip(group, far)] for group in packed]
    core = over_seq(rest[1], 1)
    pieces = [[(rest[0], gp), (core, gp)] + [(x, 0) for x in sent_far[gp]] for gp in range(groups)]
    sends = pack_chunks(gate([cotangent], rest[0])[0], orders, shares, width)
    near = [cotangent, over_seq(gate([cotangent], *sent_far[0])[0], 1)]

    far_half = {}

    def send_chunk(c, *tokens):
        mine = gate([sends[c]], *tokens)[0]
        far_half[c] = [over_seq(mine, d) for d in range(2, parts, 2)]

    for c in range(chunks):
        if c < groups:
            send_chunk(c, *sent_far[c])
        else:
            send_chunk(c, *far_half[max(0, c - groups)])

    fwd = []
    token = sends[-1]
    for gp in range(groups):
        fwd.append(attention(info, pieces[gp], token, parts, docs))
        token = fwd[-1][0]
        if gp == 0:
            token = (token, near[1])
    outs = [pair[0] for pair in fwd]

    fars, state, back, results = {}, {}, {}, {}
    acc = weight_grad = None

    def hop(c, send, stage):
        return over_dp(send, 1 << orders[c][stage])

    def weigh(c):
        nonlocal token
        fars[c] = []
        for x in gate(far_half[c], token):
            fars[c] += [x, over_seq(x, 1)]
        keep, send = weight_terms(
            info, outs, near, fars[c], token, shares, c, chunks, width, orders[c]
        )
        token = send
        state[c] = (keep, hop(c, send, 0), 1)

    def advance(c):
        nonlocal token, weight_grad
        if c not in state or state[c] is None:
            return
        keep, got, stage = state[c]
        if stage == len(bits):
            token = weight_grad = finish(keep, got, weight_grad, token, c, chunks, scale)
            state[c] = None
        else:
            keep, send = merge(keep, got, token)
            token = send
            state[c] = (keep, hop(c, send, stage), stage + 1)

    def project_step(picked, last):
        nonlocal token, acc
        token = acc = project(
            out_weight, near, [fars[c] for c in picked], acc, token, orders, picked, shares, width, last
        )

    def send_back(gp):
        nonlocal token
        res = attention_back(info, pieces[gp], acc, outs[gp], fwd[gp][1], token, parts, docs, gp)
        token = results[gp] = res
        back[gp] = [res[0], None] + [over_seq(res[d], d) for d in far]

    last = chunks - 1
    for c in range(last):
        weigh(c)
    if last:
        project_step(list(range(last)), False)
    advance(0)
    weigh(last)
    project_step([last], True)
    advance(1)
    send_back(0)
    for c in (0, 1, 2):
        advance(c)
    for gp in range(1, groups):
        send_back(gp)
    advance(0)
    token = (token, *back[0][2:])
    advance(2)
    both = over_seq(jnp.concatenate([results[gp][1] for gp in range(groups)], axis=0), 1)
    token = (token, back[groups - 1][-1])
    advance(3)
    advance(1)
    token = (token, *back[groups - 1][2:])
    advance(3)
    for gp in range(groups):
        back[gp][1] = both[gp * rows : (gp + 1) * rows]
    for _ in bits:
        for c in range(last):
            advance(c)
    back = [x for gp in range(groups) for x in back[gp]]
    grad_q, grad_k, grad_v = unpack(gate([info], token)[0], back, parts, groups)
    token = grad_q
    for _ in bits:
        advance(last)
    return (grad_q[None], grad_k[None], grad_v[None], weight_grad)


def solution(mesh):
    return jax.shard_map(
        body,
        mesh=mesh,
        in_specs=(
            P("dp", "seq", None),
            P("dp", "seq", None),
            P("dp", "seq", None),
            P("dp", "seq", None),
            P("seq", None),
            P("dp", None),
        ),
        out_specs=(
            P("dp", "seq", None),
            P("dp", "seq", None),
            P("dp", "seq", None),
            P("seq", "dp"),
        ),
        check_vma=False,
    )
```

```python
import functools
import math

import jax
import jax.numpy as jnp
from jax import lax
from jax.experimental import pallas as pl
from jax.experimental.pallas import tpu as pltpu
from jax.sharding import PartitionSpec as P

HEADS = 32
KV_HEADS = 8
HEAD_DIM = 128
GROUP = HEADS // KV_HEADS
MASKED = -1e30
NT = (((1,), (1,)), ((), ()))
NN = (((1,), (0,)), ((), ()))


def mm(a, b, dims=NN):
    return lax.dot_general(a, b, dims, preferred_element_type=jnp.float32)


def params(mib):
    return pltpu.CompilerParams(vmem_limit_bytes=mib * 2**20)


def cost(weight):
    return pl.CostEstimate(flops=int(weight * 1e9), bytes_accessed=1024, transcendentals=0)


ANY = pl.BlockSpec(memory_space=pl.ANY)


def shape(dims, dtype=jnp.bfloat16):
    return jax.ShapeDtypeStruct(dims, dtype)


def gate(arrays, *tokens):
    flat = [x for token in tokens for x in (token if isinstance(token, tuple) else (token,))]
    return list(lax.optimization_barrier((*arrays, *flat)))[: len(arrays)]


def pack_kernel(jobs, joined, me_ref, *refs):
    wide = GROUP * HEAD_DIM
    size = wide + 2 * HEAD_DIM
    sources, outs = iter(refs[: len(refs) - len(jobs)]), refs[len(refs) - len(jobs) :]
    if joined:
        outs[1][:, size * len(jobs[1][1]) :] = refs[0][...]
        next(sources)
    for out, (d, members) in zip(outs, jobs):
        for slot in range(len(members)):
            start = slot * size
            for width in (wide, HEAD_DIM, HEAD_DIM):
                out[:, start : start + width] = next(sources)[...]
                start += width


def pack(me, sources, parts, jobs, joined=None):
    rows = sources[0].shape[0]
    groups = KV_HEADS // parts
    wide = GROUP * HEAD_DIM
    size = wide + 2 * HEAD_DIM
    step = min(128, rows)

    def pick(width, d, gp):
        return pl.BlockSpec((step, width), lambda i, me: (i, (me[0] ^ d) * groups + gp))

    specs = [
        pick(width, d, gp)
        for d, members in jobs
        for gp in members
        for width in (wide, HEAD_DIM, HEAD_DIM)
    ]
    more = [] if joined is None else [joined]
    widths = [size * len(members) for d, members in jobs]
    if more:
        widths[1] += joined.shape[1]
    return pl.pallas_call(
        functools.partial(pack_kernel, jobs, bool(more)),
        grid_spec=pltpu.PrefetchScalarGridSpec(
            num_scalar_prefetch=1,
            grid=(rows // step,),
            in_specs=[pl.BlockSpec((step, x.shape[1]), lambda i, me: (i, 0)) for x in more] + specs,
            out_specs=[pl.BlockSpec((step, width), lambda i, me: (i, 0)) for width in widths],
        ),
        out_shape=[shape((rows, width)) for width in widths],
        compiler_params=params(60),
        cost_estimate=cost(0.2),
        name="pack",
    )(me, *more, *sources * (len(specs) // 3))


def column(share, c, chunks, width):
    return slice((share * chunks + c) * width, (share * chunks + c + 1) * width)


def pack_chunks_kernel(orders, shares, width, g_ref, *out_refs):
    for c, order in enumerate(orders):
        for place in range(shares):
            share = unplace(place, order)
            out_refs[c][:, place * width : (place + 1) * width] = g_ref[
                :, column(share, c, len(orders), width)
            ]


def pack_chunks(cotangent, orders, shares, width):
    rows, model = cotangent.shape
    step = min(64, rows)
    return pl.pallas_call(
        functools.partial(pack_chunks_kernel, orders, shares, width),
        grid=(rows // step,),
        in_specs=[pl.BlockSpec((step, model), lambda i: (i, 0))],
        out_specs=[pl.BlockSpec((step, shares * width), lambda i: (i, 0))] * len(orders),
        out_shape=[shape((rows, shares * width)) for order in orders],
        compiler_params=params(60),
        cost_estimate=cost(0.2),
        name="pack_chunks",
    )(cotangent)


def unpack_kernel(parts, groups, info_ref, *refs):
    count = parts * groups
    q_ref, k_ref, v_ref = refs[count:]
    wide = GROUP * HEAD_DIM
    for gp in range(groups):
        for d in range(parts):
            piece = refs[gp * parts + d]
            place = (info_ref[0] ^ d) * groups + gp
            q_ref[:, pl.ds(pl.multiple_of(place * wide, wide), wide)] = piece[:, :wide]
            narrow = pl.ds(pl.multiple_of(place * HEAD_DIM, HEAD_DIM), HEAD_DIM)
            k_ref[:, narrow] = piece[:, wide : wide + HEAD_DIM]
            v_ref[:, narrow] = piece[:, wide + HEAD_DIM :]


def unpack(info, pieces, parts, groups):
    rows, cols = pieces[0].shape
    wide = GROUP * HEAD_DIM
    step = min(64, rows)
    total = parts * groups
    widths = (total * wide, total * HEAD_DIM, total * HEAD_DIM)
    return pl.pallas_call(
        functools.partial(unpack_kernel, parts, groups),
        grid_spec=pltpu.PrefetchScalarGridSpec(
            num_scalar_prefetch=1,
            grid=(rows // step,),
            in_specs=[pl.BlockSpec((step, cols), lambda i, info: (i, 0))] * total,
            out_specs=[pl.BlockSpec((step, w), lambda i, info: (i, 0)) for w in widths],
        ),
        out_shape=[shape((rows, w)) for w in widths],
        compiler_params=params(16),
        cost_estimate=cost(0.2),
        name="unpack",
    )(info, *pieces)


def pair_index(qb, kb):
    return qb * (qb + 1) // 2 + kb


def prepare(parts, block, docs, info_ref, bias_ref, open_ref):
    down = lax.broadcasted_iota(jnp.int32, (block, block), 0)
    across = lax.broadcasted_iota(jnp.int32, (1, block), 1)
    for qb in range(parts):
        lanes = qb * block + across
        opening = jnp.zeros((1, block), jnp.int32)
        first = jnp.int32(0)
        for n in range(docs):
            start = info_ref[2 + n]
            opening = jnp.where(start <= lanes, jnp.maximum(opening, start), opening)
            first = jnp.where(start <= qb * block, jnp.maximum(first, start), first)
        open_ref[qb] = first // block
        for kb in range(qb + 1):
            seen = down >= opening - kb * block
            if kb == qb:
                seen = seen & (down <= across)
            bias_ref[pair_index(qb, kb)] = jnp.where(seen, 0.0, MASKED).astype(jnp.float32)


def flip(x):
    return jnp.transpose(x.astype(jnp.float32))


def head_cols(h):
    return slice(h * HEAD_DIM, (h + 1) * HEAD_DIM)


def forward_kernel(parts, block, docs, info_ref, *refs):
    pieces = refs[:parts]
    out_ref, lse_ref = refs[parts : parts + 2]
    bias_ref, open_ref, q_s, k_s, vt_s, top_s, sum_s, acc_s = refs[parts + 2 :]
    me = info_ref[0]
    wide = GROUP * HEAD_DIM
    factor = math.log2(math.e) / math.sqrt(HEAD_DIM)
    prepare(parts, block, docs, info_ref, bias_ref, open_ref)
    for d in range(parts):
        q_s[me ^ d] = pieces[d][:, :wide]
        k_s[me ^ d] = pieces[d][:, wide : wide + HEAD_DIM]
        vt_s[me ^ d] = flip(pieces[d][:, wide + HEAD_DIM :]).astype(jnp.bfloat16)

    def rows_of(qb, carry):
        top_s[...] = jnp.full_like(top_s, 2.0 * MASKED)
        sum_s[...] = jnp.zeros_like(sum_s)
        acc_s[...] = jnp.zeros_like(acc_s)

        def pair(back, carry):
            kb = qb - back
            bias = bias_ref.at[pair_index(qb, kb)]
            for h in range(GROUP):
                raw = mm(k_s[kb], q_s[qb, :, head_cols(h)], NT) * factor + bias[...]
                old = top_s[h]
                top = jnp.maximum(old, jnp.max(raw, axis=0, keepdims=True))
                shrink = jnp.exp2(old - top)
                raised = jnp.exp2(raw - top)
                top_s[h] = top
                sum_s[h] = sum_s[h] * shrink + jnp.sum(raised, axis=0, keepdims=True)
                acc_s[h] = acc_s[h] * shrink + mm(vt_s[kb], raised.astype(jnp.bfloat16))
            return carry

        lax.fori_loop(0, qb - open_ref[qb] + 1, pair, 0)
        for h in range(GROUP):
            out_ref[me ^ qb, head_cols(h)] = (acc_s[h] / sum_s[h]).astype(jnp.bfloat16)
            lse_ref[h, me ^ qb] = jnp.broadcast_to(top_s[h] + jnp.log2(sum_s[h]), (8, block))
        return carry

    lax.fori_loop(0, parts, rows_of, 0)


def whole_block(dims):
    return pl.BlockSpec(dims, lambda i, info: (0,) * len(dims))


def piece_block(rows, cols, at):
    return pl.BlockSpec((rows, cols), lambda i, info: (0, at))


def attention(info, pieces, token, parts, docs):
    block, cols = pieces[-1][0].shape
    pairs = parts * (parts + 1) // 2
    wide = GROUP * HEAD_DIM
    vm = pltpu.VMEM
    return pl.pallas_call(
        functools.partial(forward_kernel, parts, block, docs),
        grid_spec=pltpu.PrefetchScalarGridSpec(
            num_scalar_prefetch=1,
            grid=(1,),
            in_specs=[piece_block(block, cols, at) for x, at in pieces],
            out_specs=[
                whole_block((parts, wide, block)),
                whole_block((GROUP, parts, 8, block)),
            ],
            scratch_shapes=[
                vm((pairs, block, block), jnp.float32),
                pltpu.SMEM((parts,), jnp.int32),
                vm((parts, block, wide), jnp.bfloat16),
                vm((parts, block, HEAD_DIM), jnp.bfloat16),
                vm((parts, HEAD_DIM, block), jnp.bfloat16),
                vm((GROUP, 1, block), jnp.float32),
                vm((GROUP, 1, block), jnp.float32),
                vm((GROUP, HEAD_DIM, block), jnp.float32),
            ],
        ),
        out_shape=[
            shape((parts, wide, block)),
            shape((GROUP, parts, 8, block), jnp.float32),
        ],
        compiler_params=params(16),
        cost_estimate=cost(1.0),
        name="attention",
    )(gate([info], token)[0], *[x for x, at in pieces])


def backward_kernel(parts, block, docs, info_ref, *refs):
    pieces = refs[:parts]
    grad_ref, out_ref, lse_ref = refs[parts : parts + 3]
    res_ref = refs[parts + 3]
    bias_ref, open_ref, q_s, k_s, kt_s, v_s, dk_s, dv_s, dq_s, delta_s = refs[parts + 4 :]
    me = info_ref[0]
    wide = GROUP * HEAD_DIM
    scale = 1.0 / math.sqrt(HEAD_DIM)
    factor = math.log2(math.e) * scale
    prepare(parts, block, docs, info_ref, bias_ref, open_ref)
    for d in range(parts):
        q_s[me ^ d] = pieces[d][:, :wide]
        k_s[me ^ d] = pieces[d][:, wide : wide + HEAD_DIM]
        kt_s[me ^ d] = flip(pieces[d][:, wide : wide + HEAD_DIM]).astype(jnp.bfloat16)
        v_s[me ^ d] = pieces[d][:, wide + HEAD_DIM :]
    dk_s[...] = jnp.zeros_like(dk_s)
    dv_s[...] = jnp.zeros_like(dv_s)

    def rows_of(qb, carry):
        spot = me ^ qb
        dq_s[...] = jnp.zeros_like(dq_s)
        for h in range(GROUP):
            product = flip(grad_ref[spot, :, head_cols(h)]) * out_ref[spot, head_cols(h)].astype(
                jnp.float32
            )
            delta_s[h] = jnp.sum(product, axis=0, keepdims=True)

        def pair(back, carry):
            kb = qb - back
            bias = bias_ref.at[pair_index(qb, kb)]
            key, value = k_s[kb], v_s[kb]
            dk = dk_s[kb]
            dv = dv_s[kb]
            for h in range(GROUP):
                query, grad = q_s[qb, :, head_cols(h)], grad_ref[spot, :, head_cols(h)]
                raw = mm(key, query, NT) * factor + bias[...]
                probs = jnp.exp2(raw - lse_ref[h, spot, :1])
                dv += mm(probs.astype(jnp.bfloat16), grad)
                slope = (probs * (mm(value, grad, NT) - delta_s[h])).astype(jnp.bfloat16)
                dk += mm(slope, query)
                dq_s[h] += mm(kt_s[kb], slope)
            dk_s[kb] = dk
            dv_s[kb] = dv
            return carry

        lax.fori_loop(0, qb - open_ref[qb] + 1, pair, 0)
        for h in range(GROUP):
            res_ref[spot, :, head_cols(h)] = (jnp.transpose(dq_s[h]) * scale).astype(jnp.bfloat16)
        return carry

    lax.fori_loop(0, parts, rows_of, 0)
    for kb in range(parts):
        res_ref[me ^ kb, :, wide : wide + HEAD_DIM] = (dk_s[kb] * scale).astype(jnp.bfloat16)
        res_ref[me ^ kb, :, wide + HEAD_DIM :] = dv_s[kb].astype(jnp.bfloat16)


def attention_back(info, pieces, grads, out, lse, token, parts, docs, gp):
    block, cols = pieces[-1][0].shape
    pairs = parts * (parts + 1) // 2
    wide = GROUP * HEAD_DIM
    vm = pltpu.VMEM
    return pl.pallas_call(
        functools.partial(backward_kernel, parts, block, docs),
        grid_spec=pltpu.PrefetchScalarGridSpec(
            num_scalar_prefetch=1,
            grid=(1,),
            in_specs=[piece_block(block, cols, at) for x, at in pieces]
            + [
                pl.BlockSpec((parts, block, wide), lambda i, info: (0, 0, gp)),
                whole_block((parts, wide, block)),
                whole_block((GROUP, parts, 8, block)),
            ],
            out_specs=whole_block((parts, block, cols)),
            scratch_shapes=[
                vm((pairs, block, block), jnp.float32),
                pltpu.SMEM((parts,), jnp.int32),
                vm((parts, block, wide), jnp.bfloat16),
                vm((parts, block, HEAD_DIM), jnp.bfloat16),
                vm((parts, HEAD_DIM, block), jnp.bfloat16),
                vm((parts, block, HEAD_DIM), jnp.bfloat16),
                vm((parts, block, HEAD_DIM), jnp.float32),
                vm((parts, block, HEAD_DIM), jnp.float32),
                vm((GROUP, HEAD_DIM, block), jnp.float32),
                vm((GROUP, 1, block), jnp.float32),
            ],
        ),
        out_shape=shape((parts, block, cols)),
        compiler_params=params(20),
        cost_estimate=cost(1.5),
        name="attention_back",
    )(gate([info], token)[0], *[x for x, at in pieces], grads, out, lse)


def place_of(share, order):
    out = 0 * share
    for k, bit in enumerate(order):
        out = out + ((share >> bit) & 1) * (1 << k)
    return out


def unplace(place, order):
    out = 0 * place
    for k, bit in enumerate(order):
        out = out + ((place >> k) & 1) * (1 << bit)
    return out


def reverse_bits(x, bits):
    out = 0 * x
    for b in range(bits):
        out = out + ((x >> b) & 1) * (1 << (bits - 1 - b))
    return out


def weight_kernel(parts, groups, width, order, info_ref, *refs):
    outs, lows, highs = refs[:groups], refs[groups : groups + 2], refs[groups + 2 : groups + 4]
    chunk = refs[groups + 4 : groups + 2 + parts]
    keep_ref, send_ref = refs[groups + 2 + parts :]
    odd = ((info_ref[1] >> order[0]) & 1) == 1
    rows = GROUP * HEAD_DIM
    grads = [jnp.concatenate([lows[d][...], highs[d][...]], axis=1) for d in range(2)]
    for gp in range(groups):
        total = mm(outs[gp][0], grads[0]) + mm(outs[gp][1], grads[1])
        for d in range(2, parts):
            total += mm(outs[gp][d], chunk[d - 2][...])
        low, high = total[:, :width], total[:, width:]
        spot = slice(gp * rows, (gp + 1) * rows)
        keep_ref[0, spot] = jnp.where(odd, high, low)
        send_ref[0, spot] = jnp.where(odd, low, high).astype(jnp.bfloat16)


def weight_terms(info, outs, near, chunk, token, shares, c, chunks, width, order):
    groups, parts = len(outs), 2 + len(chunk)
    _, rows, block = outs[0].shape
    half = shares // 2
    bits = half.bit_length() - 1
    spot = pl.BlockSpec((1, groups * rows, width), lambda t, info: (reverse_bits(t, bits), 0, 0))

    def mate(t, info):
        return t ^ (place_of(info[1], order) >> 1)

    def original(side, x):
        shift = (x.shape[1] - shares * chunks * width) // width
        return pl.BlockSpec(
            (block, width),
            lambda t, info: (0, shift + unplace(2 * mate(t, info) + side, order) * chunks + c),
        )

    return pl.pallas_call(
        functools.partial(weight_kernel, parts, groups, width, order),
        grid_spec=pltpu.PrefetchScalarGridSpec(
            num_scalar_prefetch=1,
            grid=(half,),
            in_specs=[pl.BlockSpec((parts, rows, block), lambda t, info: (0, 0, 0))] * groups
            + [original(side, x) for side in range(2) for x in near]
            + [pl.BlockSpec((block, 2 * width), lambda t, info: (0, mate(t, info)))] * len(chunk),
            out_specs=[spot, spot],
        ),
        out_shape=[
            shape((half, groups * rows, width), jnp.float32),
            shape((half, groups * rows, width)),
        ],
        compiler_params=params(16),
        cost_estimate=cost(0.3),
        name="weight_terms",
    )(gate([info], token)[0], *outs, *near, *near, *chunk)


def merge_kernel(keep_low, keep_high, got_low, got_high, keep_ref, send_ref):
    keep_ref[...] = keep_low[...] + got_low[...].astype(jnp.float32)
    send_ref[...] = (keep_high[...] + got_high[...].astype(jnp.float32)).astype(jnp.bfloat16)


def merge(keep, got, token):
    count, rows, width = keep.shape
    half = count // 2
    keep = gate([keep], token)[0]
    low = pl.BlockSpec((1, rows, width), lambda t: (t, 0, 0))
    high = pl.BlockSpec((1, rows, width), lambda t: (t + half, 0, 0))
    return pl.pallas_call(
        merge_kernel,
        grid=(half,),
        in_specs=[low, high, low, high],
        out_specs=[low, low],
        out_shape=[
            shape((half, rows, width), jnp.float32),
            shape((half, rows, width)),
        ],
        compiler_params=params(12),
        cost_estimate=cost(0.02),
        name="merge",
    )(keep, keep, got, got)


def finish_kernel(scale, keep_ref, got_ref, *refs):
    refs[-1][...] = (keep_ref[0] + got_ref[0].astype(jnp.float32)) * scale


def finish(keep, got, so_far, token, c, chunks, scale):
    _, rows, width = keep.shape
    more = [] if so_far is None else [so_far]
    step = rows // 2
    spec = pl.BlockSpec((1, step, width), lambda i: (0, i, 0))
    return pl.pallas_call(
        functools.partial(finish_kernel, scale),
        grid=(rows // step,),
        in_specs=[spec, spec] + [ANY] * len(more),
        out_specs=pl.BlockSpec((step, width), lambda i: (i, c)),
        out_shape=shape((rows, width * chunks), jnp.float32),
        input_output_aliases={2: 0} if more else {},
        compiler_params=params(8),
        cost_estimate=cost(0.02),
        name="finish",
    )(gate([keep], token)[0], got, *more)


def shifted(ref, like, columns):
    more = ref.shape[1] - like.shape[1]
    return slice(columns.start + more, columns.stop + more)


def project_kernel(parts, shares, width, chunks, orders, picked, first, last, *refs):
    w_ref, near = refs[0], refs[1:3]
    far = refs[3 : 3 + len(picked) * (parts - 2)]
    acc_ref, out_ref = refs[-2] if not first else None, refs[-1]
    columns = [(c, unplace(p, orders[c])) for c in picked for p in range(shares)]
    weights = jnp.concatenate([w_ref[:, column(j, c, chunks, width)] for c, j in columns], axis=1)
    for d in range(parts):
        if d < 2:
            rows = jnp.concatenate([near[d][:, shifted(near[d], w_ref, column(j, c, chunks, width))] for c, j in columns], axis=1)
        else:
            mine = [far[i * (parts - 2) + d - 2][...] for i in range(len(picked))]
            rows = mine[0] if len(mine) == 1 else jnp.concatenate(mine, axis=1)
        total = mm(rows, weights, NT)
        if not first:
            total += acc_ref[d]
        out_ref[d] = total.astype(out_ref.dtype)


def project(out_weight, near, far, acc, token, orders, picked, shares, width, last):
    feats, model = out_weight.shape
    rows = near[0].shape[0]
    parts = 2 + len(far[0])
    step = min(256, feats)
    flat = [x for group in far for x in group]
    first = acc is None
    block = pl.BlockSpec((parts, rows, step), lambda i: (0, 0, i))
    return pl.pallas_call(
        functools.partial(
            project_kernel, parts, shares, width, len(orders), orders, picked, first, last
        ),
        grid=(feats // step,),
        in_specs=[pl.BlockSpec((step, model), lambda i: (i, 0))]
        + [pl.BlockSpec((rows, x.shape[1]), lambda i: (0, 0)) for x in near]
        + [pl.BlockSpec((rows, shares * width), lambda i: (0, 0))] * len(flat)
        + ([] if first else [block]),
        out_specs=block,
        out_shape=shape((parts, rows, feats), jnp.bfloat16 if last else jnp.float32),
        compiler_params=params(24),
        cost_estimate=cost(0.5),
        name="project",
    )(gate([out_weight], token)[0], *near, *flat, *([] if first else [acc]))


def body(grad_out, queries, keys, values, out_weight, doc_starts):
    parts, shares = lax.axis_size("seq"), lax.axis_size("dp")
    groups = KV_HEADS // parts
    docs = doc_starts.shape[-1]
    cotangent = grad_out[0]
    rows, model = cotangent.shape
    chunks = max(1, min(4, model // shares // 128))
    width = model // shares // chunks
    bits = tuple(range(shares.bit_length() - 1))
    turned = bits[1:] + bits[:1]
    orders = [turned if c == 0 else bits for c in range(chunks)]
    scale = 1.0 / math.sqrt(rows * parts * shares)
    info = jnp.concatenate(
        [
            jnp.stack([lax.axis_index("seq"), lax.axis_index("dp")]).astype(jnp.int32),
            doc_starts[0],
        ]
    )

    def over_seq(x, d):
        return lax.ppermute(x, "seq", [(i, i ^ d) for i in range(parts)])

    def over_dp(x, d):
        return lax.ppermute(x, "dp", [(i, i ^ d) for i in range(shares)])

    far = range(2, parts)
    all_groups = tuple(range(groups))
    me = lax.axis_index("seq").astype(jnp.int32).reshape(1)
    sources = (queries[0], keys[0], values[0])
    packed = [pack(me, sources, parts, tuple((d, (0,)) for d in far))]
    rest = [(d, (gp,)) for gp in range(1, groups) for d in far]
    rest = pack(
        gate([me], packed[0][0])[0],
        sources,
        parts,
        tuple([(0, all_groups), (1, all_groups)] + rest),
    )
    for gp in range(1, groups):
        packed.append(rest[2 + (gp - 1) * len(far) : 2 + gp * len(far)])
    sent_far = [[over_seq(x, d) for x, d in zip(group, far)] for group in packed]
    core = over_seq(rest[1], 1)
    pieces = [[(rest[0], gp), (core, gp)] + [(x, 0) for x in sent_far[gp]] for gp in range(groups)]
    sends = pack_chunks(gate([cotangent], rest[0])[0], orders, shares, width)
    near = [cotangent, over_seq(gate([cotangent], *sent_far[0], sends[-1])[0], 1)]

    far_half = {}

    def send_chunk(c, *tokens):
        mine = gate([sends[c]], *tokens)[0]
        far_half[c] = [over_seq(mine, d) for d in range(2, parts, 2)]

    for c in range(chunks):
        if c < groups:
            send_chunk(c, *sent_far[c], sends[-1])
        else:
            send_chunk(c, *far_half[max(0, c - groups)])

    fwd = []
    token = sends[-1]
    for gp in range(groups):
        fwd.append(attention(info, pieces[gp], token, parts, docs))
        token = fwd[-1][0]
        if gp == 0:
            token = (token, near[1])
    outs = [pair[0] for pair in fwd]

    fars, state, back, results = {}, {}, {}, {}
    acc = weight_grad = None

    def hop(c, send, stage):
        return over_dp(send, 1 << orders[c][stage])

    def weigh(c):
        nonlocal token
        fars[c] = []
        for x in gate(far_half[c], token):
            fars[c] += [x, over_seq(x, 1)]
        keep, send = weight_terms(
            info, outs, near, fars[c], token, shares, c, chunks, width, orders[c]
        )
        token = send
        state[c] = (keep, hop(c, send, 0), 1)

    def advance(c):
        nonlocal token, weight_grad
        if c not in state or state[c] is None:
            return
        keep, got, stage = state[c]
        if stage == len(bits):
            token = weight_grad = finish(keep, got, weight_grad, token, c, chunks, scale)
            state[c] = None
        else:
            keep, send = merge(keep, got, token)
            token = send
            state[c] = (keep, hop(c, send, stage), stage + 1)

    def project_step(picked, last):
        nonlocal token, acc
        token = acc = project(
            out_weight, near, [fars[c] for c in picked], acc, token, orders, picked, shares, width, last
        )

    def send_back(gp, *tokens):
        nonlocal token
        res = attention_back(info, pieces[gp], acc, outs[gp], fwd[gp][1], token, parts, docs, gp)
        token = res
        parted = gate([res[d] for d in range(parts)], *tokens)
        results[gp] = parted
        back[gp] = [parted[0], None] + [over_seq(parted[d], d) for d in far]

    last = chunks - 1
    for c in range(last):
        weigh(c)
    advance(0)
    if last:
        project_step(list(range(last)), False)
    weigh(last)
    advance(1)
    project_step([last], True)
    send_back(0)
    for c in (0, 1, 2, 0):
        advance(c)
    for gp in range(1, groups):
        send_back(gp, *back[gp - 1][2:])
    advance(1)
    advance(2)
    token = (token, back[groups - 1][2])
    advance(3)
    both = over_seq(jnp.concatenate([results[gp][1] for gp in range(groups)], axis=0), 1)
    token = (token, *back[groups - 1][2:])
    advance(3)
    for gp in range(groups):
        back[gp][1] = both[gp * rows : (gp + 1) * rows]
    for _ in bits:
        for c in range(last):
            advance(c)
    back = [x for gp in range(groups) for x in back[gp]]
    grad_q, grad_k, grad_v = unpack(gate([info], token)[0], back, parts, groups)
    token = grad_q
    for _ in bits:
        advance(last)
    return (grad_q[None], grad_k[None], grad_v[None], weight_grad)


def solution(mesh):
    return jax.shard_map(
        body,
        mesh=mesh,
        in_specs=(
            P("dp", "seq", None),
            P("dp", "seq", None),
            P("dp", "seq", None),
            P("dp", "seq", None),
            P("seq", None),
            P("dp", None),
        ),
        out_specs=(
            P("dp", "seq", None),
            P("dp", "seq", None),
            P("dp", "seq", None),
            P("seq", "dp"),
        ),
        check_vma=False,
    )
```

```python
import functools
import math

import jax
import jax.numpy as jnp
from jax import lax
from jax.experimental import pallas as pl
from jax.experimental.pallas import tpu as pltpu
from jax.sharding import PartitionSpec as P

HEADS = 32
KV_HEADS = 8
HEAD_DIM = 128
GROUP = HEADS // KV_HEADS
MASKED = -1e30
NT = (((1,), (1,)), ((), ()))
NN = (((1,), (0,)), ((), ()))


def mm(a, b, dims=NN):
    return lax.dot_general(a, b, dims, preferred_element_type=jnp.float32)


def params(mib):
    return pltpu.CompilerParams(vmem_limit_bytes=mib * 2**20)


def cost(weight):
    return pl.CostEstimate(flops=int(weight * 1e9), bytes_accessed=1024, transcendentals=0)


ANY = pl.BlockSpec(memory_space=pl.ANY)


def shape(dims, dtype=jnp.bfloat16):
    return jax.ShapeDtypeStruct(dims, dtype)


def gate(arrays, *tokens):
    flat = [x for token in tokens for x in (token if isinstance(token, tuple) else (token,))]
    return list(lax.optimization_barrier((*arrays, *flat)))[: len(arrays)]


def pack_kernel(jobs, joined, me_ref, *refs):
    wide = GROUP * HEAD_DIM
    size = wide + 2 * HEAD_DIM
    sources, outs = iter(refs[: len(refs) - len(jobs)]), refs[len(refs) - len(jobs) :]
    if joined:
        outs[1][:, size * len(jobs[1][1]) :] = refs[0][...]
        next(sources)
    for out, (d, members) in zip(outs, jobs):
        for slot in range(len(members)):
            start = slot * size
            for width in (wide, HEAD_DIM, HEAD_DIM):
                out[:, start : start + width] = next(sources)[...]
                start += width


def pack(me, sources, parts, jobs, joined=None):
    rows = sources[0].shape[0]
    groups = KV_HEADS // parts
    wide = GROUP * HEAD_DIM
    size = wide + 2 * HEAD_DIM
    step = min(128, rows)

    def pick(width, d, gp):
        return pl.BlockSpec((step, width), lambda i, me: (i, (me[0] ^ d) * groups + gp))

    specs = [
        pick(width, d, gp)
        for d, members in jobs
        for gp in members
        for width in (wide, HEAD_DIM, HEAD_DIM)
    ]
    more = [] if joined is None else [joined]
    widths = [size * len(members) for d, members in jobs]
    if more:
        widths[1] += joined.shape[1]
    return pl.pallas_call(
        functools.partial(pack_kernel, jobs, bool(more)),
        grid_spec=pltpu.PrefetchScalarGridSpec(
            num_scalar_prefetch=1,
            grid=(rows // step,),
            in_specs=[pl.BlockSpec((step, x.shape[1]), lambda i, me: (i, 0)) for x in more] + specs,
            out_specs=[pl.BlockSpec((step, width), lambda i, me: (i, 0)) for width in widths],
        ),
        out_shape=[shape((rows, width)) for width in widths],
        compiler_params=params(60),
        cost_estimate=cost(0.2),
        name="pack",
    )(me, *more, *sources * (len(specs) // 3))


def column(share, c, chunks, width):
    return slice((share * chunks + c) * width, (share * chunks + c + 1) * width)


def pack_chunks_kernel(orders, shares, width, g_ref, *out_refs):
    for c, order in enumerate(orders):
        for place in range(shares):
            share = unplace(place, order)
            out_refs[c][:, place * width : (place + 1) * width] = g_ref[
                :, column(share, c, len(orders), width)
            ]


def pack_chunks(cotangent, orders, shares, width):
    rows, model = cotangent.shape
    step = min(64, rows)
    return pl.pallas_call(
        functools.partial(pack_chunks_kernel, orders, shares, width),
        grid=(rows // step,),
        in_specs=[pl.BlockSpec((step, model), lambda i: (i, 0))],
        out_specs=[pl.BlockSpec((step, shares * width), lambda i: (i, 0))] * len(orders),
        out_shape=[shape((rows, shares * width)) for order in orders],
        compiler_params=params(60),
        cost_estimate=cost(0.2),
        name="pack_chunks",
    )(cotangent)


def unpack_kernel(parts, groups, info_ref, *refs):
    count = parts * groups
    q_ref, k_ref, v_ref = refs[count:]
    wide = GROUP * HEAD_DIM
    for gp in range(groups):
        for d in range(parts):
            piece = refs[gp * parts + d]
            place = (info_ref[0] ^ d) * groups + gp
            q_ref[:, pl.ds(pl.multiple_of(place * wide, wide), wide)] = piece[:, :wide]
            narrow = pl.ds(pl.multiple_of(place * HEAD_DIM, HEAD_DIM), HEAD_DIM)
            k_ref[:, narrow] = piece[:, wide : wide + HEAD_DIM]
            v_ref[:, narrow] = piece[:, wide + HEAD_DIM :]


def unpack(info, pieces, parts, groups):
    rows, cols = pieces[0].shape
    wide = GROUP * HEAD_DIM
    step = min(64, rows)
    total = parts * groups
    widths = (total * wide, total * HEAD_DIM, total * HEAD_DIM)
    return pl.pallas_call(
        functools.partial(unpack_kernel, parts, groups),
        grid_spec=pltpu.PrefetchScalarGridSpec(
            num_scalar_prefetch=1,
            grid=(rows // step,),
            in_specs=[pl.BlockSpec((step, cols), lambda i, info: (i, 0))] * total,
            out_specs=[pl.BlockSpec((step, w), lambda i, info: (i, 0)) for w in widths],
        ),
        out_shape=[shape((rows, w)) for w in widths],
        compiler_params=params(16),
        cost_estimate=cost(0.2),
        name="unpack",
    )(info, *pieces)


def pair_index(qb, kb):
    return qb * (qb + 1) // 2 + kb


def prepare(parts, block, docs, info_ref, bias_ref, open_ref):
    down = lax.broadcasted_iota(jnp.int32, (block, block), 0)
    across = lax.broadcasted_iota(jnp.int32, (1, block), 1)
    for qb in range(parts):
        lanes = qb * block + across
        opening = jnp.zeros((1, block), jnp.int32)
        first = jnp.int32(0)
        for n in range(docs):
            start = info_ref[2 + n]
            opening = jnp.where(start <= lanes, jnp.maximum(opening, start), opening)
            first = jnp.where(start <= qb * block, jnp.maximum(first, start), first)
        open_ref[qb] = first // block
        for kb in range(qb + 1):
            seen = down >= opening - kb * block
            if kb == qb:
                seen = seen & (down <= across)
            bias_ref[pair_index(qb, kb)] = jnp.where(seen, 0.0, MASKED).astype(jnp.float32)


def flip(x):
    return jnp.transpose(x.astype(jnp.float32))


def head_cols(h):
    return slice(h * HEAD_DIM, (h + 1) * HEAD_DIM)


def forward_kernel(parts, block, docs, info_ref, *refs):
    pieces = refs[:parts]
    out_ref, lse_ref = refs[parts : parts + 2]
    bias_ref, open_ref, q_s, k_s, vt_s, top_s, sum_s, acc_s = refs[parts + 2 :]
    me = info_ref[0]
    wide = GROUP * HEAD_DIM
    factor = math.log2(math.e) / math.sqrt(HEAD_DIM)
    prepare(parts, block, docs, info_ref, bias_ref, open_ref)
    for d in range(parts):
        q_s[me ^ d] = pieces[d][:, :wide]
        k_s[me ^ d] = pieces[d][:, wide : wide + HEAD_DIM]
        vt_s[me ^ d] = flip(pieces[d][:, wide + HEAD_DIM :]).astype(jnp.bfloat16)

    def rows_of(qb, carry):
        top_s[...] = jnp.full_like(top_s, 2.0 * MASKED)
        sum_s[...] = jnp.zeros_like(sum_s)
        acc_s[...] = jnp.zeros_like(acc_s)

        def pair(back, carry):
            kb = qb - back
            bias = bias_ref.at[pair_index(qb, kb)]
            for h in range(GROUP):
                raw = mm(k_s[kb], q_s[qb, :, head_cols(h)], NT) * factor + bias[...]
                old = top_s[h]
                top = jnp.maximum(old, jnp.max(raw, axis=0, keepdims=True))
                shrink = jnp.exp2(old - top)
                raised = jnp.exp2(raw - top)
                top_s[h] = top
                sum_s[h] = sum_s[h] * shrink + jnp.sum(raised, axis=0, keepdims=True)
                acc_s[h] = acc_s[h] * shrink + mm(vt_s[kb], raised.astype(jnp.bfloat16))
            return carry

        lax.fori_loop(0, qb - open_ref[qb] + 1, pair, 0)
        for h in range(GROUP):
            out_ref[me ^ qb, head_cols(h)] = (acc_s[h] / sum_s[h]).astype(jnp.bfloat16)
            lse_ref[h, me ^ qb] = jnp.broadcast_to(top_s[h] + jnp.log2(sum_s[h]), (8, block))
        return carry

    lax.fori_loop(0, parts, rows_of, 0)


def whole_block(dims):
    return pl.BlockSpec(dims, lambda i, info: (0,) * len(dims))


def piece_block(rows, cols, at):
    return pl.BlockSpec((rows, cols), lambda i, info: (0, at))


def attention(info, pieces, token, parts, docs):
    block, cols = pieces[-1][0].shape
    pairs = parts * (parts + 1) // 2
    wide = GROUP * HEAD_DIM
    vm = pltpu.VMEM
    return pl.pallas_call(
        functools.partial(forward_kernel, parts, block, docs),
        grid_spec=pltpu.PrefetchScalarGridSpec(
            num_scalar_prefetch=1,
            grid=(1,),
            in_specs=[piece_block(block, cols, at) for x, at in pieces],
            out_specs=[
                whole_block((parts, wide, block)),
                whole_block((GROUP, parts, 8, block)),
            ],
            scratch_shapes=[
                vm((pairs, block, block), jnp.float32),
                pltpu.SMEM((parts,), jnp.int32),
                vm((parts, block, wide), jnp.bfloat16),
                vm((parts, block, HEAD_DIM), jnp.bfloat16),
                vm((parts, HEAD_DIM, block), jnp.bfloat16),
                vm((GROUP, 1, block), jnp.float32),
                vm((GROUP, 1, block), jnp.float32),
                vm((GROUP, HEAD_DIM, block), jnp.float32),
            ],
        ),
        out_shape=[
            shape((parts, wide, block)),
            shape((GROUP, parts, 8, block), jnp.float32),
        ],
        compiler_params=params(60),
        cost_estimate=cost(2.5),
        name="attention",
    )(gate([info], token)[0], *[x for x, at in pieces])


def backward_kernel(parts, block, docs, info_ref, *refs):
    pieces = refs[:parts]
    grad_ref, out_ref, lse_ref = refs[parts : parts + 3]
    res_ref = refs[parts + 3]
    bias_ref, open_ref, q_s, k_s, kt_s, v_s, dk_s, dv_s, dq_s, delta_s = refs[parts + 4 :]
    me = info_ref[0]
    wide = GROUP * HEAD_DIM
    scale = 1.0 / math.sqrt(HEAD_DIM)
    factor = math.log2(math.e) * scale
    prepare(parts, block, docs, info_ref, bias_ref, open_ref)
    for d in range(parts):
        q_s[me ^ d] = pieces[d][:, :wide]
        k_s[me ^ d] = pieces[d][:, wide : wide + HEAD_DIM]
        kt_s[me ^ d] = flip(pieces[d][:, wide : wide + HEAD_DIM]).astype(jnp.bfloat16)
        v_s[me ^ d] = pieces[d][:, wide + HEAD_DIM :]
    dk_s[...] = jnp.zeros_like(dk_s)
    dv_s[...] = jnp.zeros_like(dv_s)

    def rows_of(qb, carry):
        spot = me ^ qb
        dq_s[...] = jnp.zeros_like(dq_s)
        for h in range(GROUP):
            product = flip(grad_ref[spot, :, head_cols(h)]) * out_ref[spot, head_cols(h)].astype(
                jnp.float32
            )
            delta_s[h] = jnp.sum(product, axis=0, keepdims=True)

        def pair(back, carry):
            kb = qb - back
            bias = bias_ref.at[pair_index(qb, kb)]
            key, value = k_s[kb], v_s[kb]
            dk = dk_s[kb]
            dv = dv_s[kb]
            for h in range(GROUP):
                query, grad = q_s[qb, :, head_cols(h)], grad_ref[spot, :, head_cols(h)]
                raw = mm(key, query, NT) * factor + bias[...]
                probs = jnp.exp2(raw - lse_ref[h, spot, :1])
                dv += mm(probs.astype(jnp.bfloat16), grad)
                slope = (probs * (mm(value, grad, NT) - delta_s[h])).astype(jnp.bfloat16)
                dk += mm(slope, query)
                dq_s[h] += mm(kt_s[kb], slope)
            dk_s[kb] = dk
            dv_s[kb] = dv
            return carry

        lax.fori_loop(0, qb - open_ref[qb] + 1, pair, 0)
        for h in range(GROUP):
            res_ref[spot, :, head_cols(h)] = (jnp.transpose(dq_s[h]) * scale).astype(jnp.bfloat16)
        return carry

    lax.fori_loop(0, parts, rows_of, 0)
    for kb in range(parts):
        res_ref[me ^ kb, :, wide : wide + HEAD_DIM] = (dk_s[kb] * scale).astype(jnp.bfloat16)
        res_ref[me ^ kb, :, wide + HEAD_DIM :] = dv_s[kb].astype(jnp.bfloat16)


def attention_back(info, pieces, grads, out, lse, token, parts, docs, gp):
    block, cols = pieces[-1][0].shape
    pairs = parts * (parts + 1) // 2
    wide = GROUP * HEAD_DIM
    vm = pltpu.VMEM
    return pl.pallas_call(
        functools.partial(backward_kernel, parts, block, docs),
        grid_spec=pltpu.PrefetchScalarGridSpec(
            num_scalar_prefetch=1,
            grid=(1,),
            in_specs=[piece_block(block, cols, at) for x, at in pieces]
            + [
                pl.BlockSpec((parts, block, wide), lambda i, info: (0, 0, gp)),
                whole_block((parts, wide, block)),
                whole_block((GROUP, parts, 8, block)),
            ],
            out_specs=whole_block((parts, block, cols)),
            scratch_shapes=[
                vm((pairs, block, block), jnp.float32),
                pltpu.SMEM((parts,), jnp.int32),
                vm((parts, block, wide), jnp.bfloat16),
                vm((parts, block, HEAD_DIM), jnp.bfloat16),
                vm((parts, HEAD_DIM, block), jnp.bfloat16),
                vm((parts, block, HEAD_DIM), jnp.bfloat16),
                vm((parts, block, HEAD_DIM), jnp.float32),
                vm((parts, block, HEAD_DIM), jnp.float32),
                vm((GROUP, HEAD_DIM, block), jnp.float32),
                vm((GROUP, 1, block), jnp.float32),
            ],
        ),
        out_shape=shape((parts, block, cols)),
        compiler_params=params(60),
        cost_estimate=cost(1.0),
        name="attention_back",
    )(gate([info], token)[0], *[x for x, at in pieces], grads, out, lse)


def place_of(share, order):
    out = 0 * share
    for k, bit in enumerate(order):
        out = out + ((share >> bit) & 1) * (1 << k)
    return out


def unplace(place, order):
    out = 0 * place
    for k, bit in enumerate(order):
        out = out + ((place >> k) & 1) * (1 << bit)
    return out


def reverse_bits(x, bits):
    out = 0 * x
    for b in range(bits):
        out = out + ((x >> b) & 1) * (1 << (bits - 1 - b))
    return out


def weight_kernel(parts, groups, width, order, info_ref, *refs):
    outs, lows, highs = refs[:groups], refs[groups : groups + 2], refs[groups + 2 : groups + 4]
    chunk = refs[groups + 4 : groups + 2 + parts]
    keep_ref, send_ref = refs[groups + 2 + parts :]
    odd = ((info_ref[1] >> order[0]) & 1) == 1
    rows = GROUP * HEAD_DIM
    grads = [jnp.concatenate([lows[d][...], highs[d][...]], axis=1) for d in range(2)]
    for gp in range(groups):
        total = mm(outs[gp][0], grads[0]) + mm(outs[gp][1], grads[1])
        for d in range(2, parts):
            total += mm(outs[gp][d], chunk[d - 2][...])
        low, high = total[:, :width], total[:, width:]
        spot = slice(gp * rows, (gp + 1) * rows)
        keep_ref[0, spot] = jnp.where(odd, high, low)
        send_ref[0, spot] = jnp.where(odd, low, high).astype(jnp.bfloat16)


def weight_terms(info, outs, near, chunk, token, shares, c, chunks, width, order):
    groups, parts = len(outs), 2 + len(chunk)
    _, rows, block = outs[0].shape
    half = shares // 2
    bits = half.bit_length() - 1
    spot = pl.BlockSpec((1, groups * rows, width), lambda t, info: (reverse_bits(t, bits), 0, 0))

    def mate(t, info):
        return t ^ (place_of(info[1], order) >> 1)

    def original(side, x):
        shift = (x.shape[1] - shares * chunks * width) // width
        return pl.BlockSpec(
            (block, width),
            lambda t, info: (0, shift + unplace(2 * mate(t, info) + side, order) * chunks + c),
        )

    return pl.pallas_call(
        functools.partial(weight_kernel, parts, groups, width, order),
        grid_spec=pltpu.PrefetchScalarGridSpec(
            num_scalar_prefetch=1,
            grid=(half,),
            in_specs=[pl.BlockSpec((parts, rows, block), lambda t, info: (0, 0, 0))] * groups
            + [original(side, x) for side in range(2) for x in near]
            + [pl.BlockSpec((block, 2 * width), lambda t, info: (0, mate(t, info)))] * len(chunk),
            out_specs=[spot, spot],
        ),
        out_shape=[
            shape((half, groups * rows, width), jnp.float32),
            shape((half, groups * rows, width)),
        ],
        compiler_params=params(16),
        cost_estimate=cost(0.3),
        name="weight_terms",
    )(gate([info], token)[0], *outs, *near, *near, *chunk)


def merge_kernel(keep_low, keep_high, got_low, got_high, keep_ref, send_ref):
    keep_ref[...] = keep_low[...] + got_low[...].astype(jnp.float32)
    send_ref[...] = (keep_high[...] + got_high[...].astype(jnp.float32)).astype(jnp.bfloat16)


def merge(keep, got, token):
    count, rows, width = keep.shape
    half = count // 2
    keep = gate([keep], token)[0]
    low = pl.BlockSpec((1, rows, width), lambda t: (t, 0, 0))
    high = pl.BlockSpec((1, rows, width), lambda t: (t + half, 0, 0))
    return pl.pallas_call(
        merge_kernel,
        grid=(half,),
        in_specs=[low, high, low, high],
        out_specs=[low, low],
        out_shape=[
            shape((half, rows, width), jnp.float32),
            shape((half, rows, width)),
        ],
        compiler_params=params(12),
        cost_estimate=cost(0.02),
        name="merge",
    )(keep, keep, got, got)


def finish_kernel(scale, keep_ref, got_ref, *refs):
    refs[-1][...] = (keep_ref[0] + got_ref[0].astype(jnp.float32)) * scale


def finish(keep, got, so_far, token, c, chunks, scale):
    _, rows, width = keep.shape
    more = [] if so_far is None else [so_far]
    step = rows // 2
    spec = pl.BlockSpec((1, step, width), lambda i: (0, i, 0))
    return pl.pallas_call(
        functools.partial(finish_kernel, scale),
        grid=(rows // step,),
        in_specs=[spec, spec] + [ANY] * len(more),
        out_specs=pl.BlockSpec((step, width), lambda i: (i, c)),
        out_shape=shape((rows, width * chunks), jnp.float32),
        input_output_aliases={2: 0} if more else {},
        compiler_params=params(8),
        cost_estimate=cost(0.02),
        name="finish",
    )(gate([keep], token)[0], got, *more)


def shifted(ref, like, columns):
    more = ref.shape[1] - like.shape[1]
    return slice(columns.start + more, columns.stop + more)


def project_kernel(parts, shares, width, chunks, orders, picked, first, last, *refs):
    w_ref, near = refs[0], refs[1:3]
    far = refs[3 : 3 + len(picked) * (parts - 2)]
    acc_ref, out_ref = refs[-2] if not first else None, refs[-1]
    columns = [(c, unplace(p, orders[c])) for c in picked for p in range(shares)]
    weights = jnp.concatenate([w_ref[:, column(j, c, chunks, width)] for c, j in columns], axis=1)
    for d in range(parts):
        if d < 2:
            rows = jnp.concatenate([near[d][:, shifted(near[d], w_ref, column(j, c, chunks, width))] for c, j in columns], axis=1)
        else:
            mine = [far[i * (parts - 2) + d - 2][...] for i in range(len(picked))]
            rows = mine[0] if len(mine) == 1 else jnp.concatenate(mine, axis=1)
        total = mm(rows, weights, NT)
        if not first:
            total += acc_ref[d]
        out_ref[d] = total.astype(out_ref.dtype)


def project(out_weight, near, far, acc, token, orders, picked, shares, width, last):
    feats, model = out_weight.shape
    rows = near[0].shape[0]
    parts = 2 + len(far[0])
    step = min(256, feats)
    flat = [x for group in far for x in group]
    first = acc is None
    block = pl.BlockSpec((parts, rows, step), lambda i: (0, 0, i))
    return pl.pallas_call(
        functools.partial(
            project_kernel, parts, shares, width, len(orders), orders, picked, first, last
        ),
        grid=(feats // step,),
        in_specs=[pl.BlockSpec((step, model), lambda i: (i, 0))]
        + [pl.BlockSpec((rows, x.shape[1]), lambda i: (0, 0)) for x in near]
        + [pl.BlockSpec((rows, shares * width), lambda i: (0, 0))] * len(flat)
        + ([] if first else [block]),
        out_specs=block,
        out_shape=shape((parts, rows, feats), jnp.bfloat16 if last else jnp.float32),
        compiler_params=params(24),
        cost_estimate=cost(0.5),
        name="project",
    )(gate([out_weight], token)[0], *near, *flat, *([] if first else [acc]))


def body(grad_out, queries, keys, values, out_weight, doc_starts):
    parts, shares = lax.axis_size("seq"), lax.axis_size("dp")
    groups = KV_HEADS // parts
    docs = doc_starts.shape[-1]
    cotangent = grad_out[0]
    rows, model = cotangent.shape
    chunks = max(1, min(4, model // shares // 128))
    width = model // shares // chunks
    bits = tuple(range(shares.bit_length() - 1))
    turned = bits[1:] + bits[:1]
    orders = [turned if c == 0 else bits for c in range(chunks)]
    scale = 1.0 / math.sqrt(rows * parts * shares)
    info = jnp.concatenate(
        [
            jnp.stack([lax.axis_index("seq"), lax.axis_index("dp")]).astype(jnp.int32),
            doc_starts[0],
        ]
    )

    def over_seq(x, d):
        return lax.ppermute(x, "seq", [(i, i ^ d) for i in range(parts)])

    def over_dp(x, d):
        return lax.ppermute(x, "dp", [(i, i ^ d) for i in range(shares)])

    far = range(2, parts)
    all_groups = tuple(range(groups))
    me = lax.axis_index("seq").astype(jnp.int32).reshape(1)
    sources = (queries[0], keys[0], values[0])
    packed = [pack(me, sources, parts, tuple((d, (0,)) for d in far))]
    rest = [(d, (gp,)) for gp in range(1, groups) for d in far]
    rest = pack(
        gate([me], packed[0][0])[0],
        sources,
        parts,
        tuple([(0, all_groups), (1, all_groups)] + rest),
    )
    for gp in range(1, groups):
        packed.append(rest[2 + (gp - 1) * len(far) : 2 + gp * len(far)])
    sent_far = [[over_seq(x, d) for x, d in zip(group, far)] for group in packed]
    core = over_seq(rest[1], 1)
    pieces = [[(rest[0], gp), (core, gp)] + [(x, 0) for x in sent_far[gp]] for gp in range(groups)]
    sends = pack_chunks(gate([cotangent], rest[0])[0], orders, shares, width)
    near = [cotangent, over_seq(gate([cotangent], *sent_far[0], sends[-1])[0], 1)]

    far_half = {}

    def send_chunk(c, *tokens):
        mine = gate([sends[c]], *tokens)[0]
        far_half[c] = [over_seq(mine, d) for d in range(2, parts, 2)]

    for c in range(chunks):
        if c < groups:
            send_chunk(c, *sent_far[c], sends[-1])
        else:
            send_chunk(c, *far_half[max(0, c - groups)])

    fwd = []
    token = sends[-1]
    for gp in range(groups):
        fwd.append(attention(info, pieces[gp], token, parts, docs))
        token = fwd[-1][0]
        if gp == 0:
            token = (token, near[1])
    outs = [pair[0] for pair in fwd]

    fars, state, back, results = {}, {}, {}, {}
    acc = weight_grad = None

    def hop(c, send, stage):
        return over_dp(send, 1 << orders[c][stage])

    def weigh(c):
        nonlocal token
        fars[c] = []
        for x in gate(far_half[c], token):
            fars[c] += [x, over_seq(x, 1)]
        keep, send = weight_terms(
            info, outs, near, fars[c], token, shares, c, chunks, width, orders[c]
        )
        token = send
        state[c] = (keep, hop(c, send, 0), 1)

    def advance(c):
        nonlocal token, weight_grad
        if c not in state or state[c] is None:
            return
        keep, got, stage = state[c]
        if stage == len(bits):
            token = weight_grad = finish(keep, got, weight_grad, token, c, chunks, scale)
            state[c] = None
        else:
            keep, send = merge(keep, got, token)
            token = send
            state[c] = (keep, hop(c, send, stage), stage + 1)

    def project_step(picked, last):
        nonlocal token, acc
        token = acc = project(
            out_weight, near, [fars[c] for c in picked], acc, token, orders, picked, shares, width, last
        )

    def send_back(gp):
        nonlocal token
        res = attention_back(info, pieces[gp], acc, outs[gp], fwd[gp][1], token, parts, docs, gp)
        token = results[gp] = res
        back[gp] = {d: over_seq(res[d : d + 2], d) for d in range(2, parts, 2)}

    def hand_over(gp, *tokens):
        got = gate([back[gp][d] for d in range(2, parts, 2)], *tokens)
        mine = [results[gp][1:2]] + [x[1:2] for x in got]
        crossed = over_seq(jnp.concatenate(mine, axis=0), 1)
        out = [results[gp][0], crossed[0]]
        for i, x in enumerate(got):
            out += [x[0], crossed[1 + i]]
        return out

    last = chunks - 1
    for c in range(last):
        weigh(c)
    advance(0)
    if last:
        project_step(list(range(last)), False)
    weigh(last)
    advance(1)
    project_step([last], True)
    send_back(0)
    for c in (0, 1, 2):
        advance(c)
    for gp in range(1, groups):
        send_back(gp)
    advance(1)
    advance(2)
    firsts = hand_over(0, token)
    token = (token, firsts[1])
    advance(3)
    advance(0)
    lasts = [hand_over(gp, token) for gp in range(1, groups)]
    advance(3)
    for _ in bits:
        for c in range(last):
            advance(c)
    back = firsts + [x for group in lasts for x in group]
    grad_q, grad_k, grad_v = unpack(gate([info], token)[0], back, parts, groups)
    token = grad_q
    for _ in bits:
        advance(last)
    return (grad_q[None], grad_k[None], grad_v[None], weight_grad)


def solution(mesh):
    return jax.shard_map(
        body,
        mesh=mesh,
        in_specs=(
            P("dp", "seq", None),
            P("dp", "seq", None),
            P("dp", "seq", None),
            P("dp", "seq", None),
            P("seq", None),
            P("dp", None),
        ),
        out_specs=(
            P("dp", "seq", None),
            P("dp", "seq", None),
            P("dp", "seq", None),
            P("seq", "dp"),
        ),
        check_vma=False,
    )
```

```python
import functools
import math

import jax
import jax.numpy as jnp
from jax import lax
from jax.experimental import pallas as pl
from jax.experimental.pallas import tpu as pltpu
from jax.sharding import PartitionSpec as P

HEADS = 32
KV_HEADS = 8
HEAD_DIM = 128
GROUP = HEADS // KV_HEADS
MASKED = -1e30
NT = (((1,), (1,)), ((), ()))
NN = (((1,), (0,)), ((), ()))


def mm(a, b, dims=NN):
    return lax.dot_general(a, b, dims, preferred_element_type=jnp.float32)


def params(mib):
    return pltpu.CompilerParams(vmem_limit_bytes=mib * 2**20)


def cost(weight):
    return pl.CostEstimate(flops=int(weight * 1e9), bytes_accessed=1024, transcendentals=0)


ANY = pl.BlockSpec(memory_space=pl.ANY)


def shape(dims, dtype=jnp.bfloat16):
    return jax.ShapeDtypeStruct(dims, dtype)


def gate(arrays, *tokens):
    flat = [x for token in tokens for x in (token if isinstance(token, tuple) else (token,))]
    return list(lax.optimization_barrier((*arrays, *flat)))[: len(arrays)]


def pack_kernel(jobs, joined, me_ref, *refs):
    wide = GROUP * HEAD_DIM
    size = wide + 2 * HEAD_DIM
    sources, outs = iter(refs[: len(refs) - len(jobs)]), refs[len(refs) - len(jobs) :]
    if joined:
        outs[1][:, size * len(jobs[1][1]) :] = refs[0][...]
        next(sources)
    for out, (d, members) in zip(outs, jobs):
        for slot in range(len(members)):
            start = slot * size
            for width in (wide, HEAD_DIM, HEAD_DIM):
                out[:, start : start + width] = next(sources)[...]
                start += width


def pack(me, sources, parts, jobs, joined=None):
    rows = sources[0].shape[0]
    groups = KV_HEADS // parts
    wide = GROUP * HEAD_DIM
    size = wide + 2 * HEAD_DIM
    step = min(128, rows)

    def pick(width, d, gp):
        return pl.BlockSpec((step, width), lambda i, me: (i, (me[0] ^ d) * groups + gp))

    specs = [
        pick(width, d, gp)
        for d, members in jobs
        for gp in members
        for width in (wide, HEAD_DIM, HEAD_DIM)
    ]
    more = [] if joined is None else [joined]
    widths = [size * len(members) for d, members in jobs]
    if more:
        widths[1] += joined.shape[1]
    return pl.pallas_call(
        functools.partial(pack_kernel, jobs, bool(more)),
        grid_spec=pltpu.PrefetchScalarGridSpec(
            num_scalar_prefetch=1,
            grid=(rows // step,),
            in_specs=[pl.BlockSpec((step, x.shape[1]), lambda i, me: (i, 0)) for x in more] + specs,
            out_specs=[pl.BlockSpec((step, width), lambda i, me: (i, 0)) for width in widths],
        ),
        out_shape=[shape((rows, width)) for width in widths],
        compiler_params=params(60),
        cost_estimate=cost(0.2),
        name="pack",
    )(me, *more, *sources * (len(specs) // 3))


def column(share, c, chunks, width):
    return slice((share * chunks + c) * width, (share * chunks + c + 1) * width)


def pack_chunks_kernel(orders, shares, width, g_ref, *out_refs):
    for c, order in enumerate(orders):
        for place in range(shares):
            share = unplace(place, order)
            out_refs[c][:, place * width : (place + 1) * width] = g_ref[
                :, column(share, c, len(orders), width)
            ]


def pack_chunks(cotangent, orders, shares, width):
    rows, model = cotangent.shape
    step = min(64, rows)
    return pl.pallas_call(
        functools.partial(pack_chunks_kernel, orders, shares, width),
        grid=(rows // step,),
        in_specs=[pl.BlockSpec((step, model), lambda i: (i, 0))],
        out_specs=[pl.BlockSpec((step, shares * width), lambda i: (i, 0))] * len(orders),
        out_shape=[shape((rows, shares * width)) for order in orders],
        compiler_params=params(60),
        cost_estimate=cost(0.2),
        name="pack_chunks",
    )(cotangent)


def unpack_kernel(parts, groups, info_ref, *refs):
    count = parts * groups
    q_ref, k_ref, v_ref = refs[count:]
    wide = GROUP * HEAD_DIM
    for gp in range(groups):
        for d in range(parts):
            piece = refs[gp * parts + d]
            place = (info_ref[0] ^ d) * groups + gp
            q_ref[:, pl.ds(pl.multiple_of(place * wide, wide), wide)] = piece[:, :wide]
            narrow = pl.ds(pl.multiple_of(place * HEAD_DIM, HEAD_DIM), HEAD_DIM)
            k_ref[:, narrow] = piece[:, wide : wide + HEAD_DIM]
            v_ref[:, narrow] = piece[:, wide + HEAD_DIM :]


def unpack(info, pieces, parts, groups):
    rows, cols = pieces[0].shape
    wide = GROUP * HEAD_DIM
    step = min(64, rows)
    total = parts * groups
    widths = (total * wide, total * HEAD_DIM, total * HEAD_DIM)
    return pl.pallas_call(
        functools.partial(unpack_kernel, parts, groups),
        grid_spec=pltpu.PrefetchScalarGridSpec(
            num_scalar_prefetch=1,
            grid=(rows // step,),
            in_specs=[pl.BlockSpec((step, cols), lambda i, info: (i, 0))] * total,
            out_specs=[pl.BlockSpec((step, w), lambda i, info: (i, 0)) for w in widths],
        ),
        out_shape=[shape((rows, w)) for w in widths],
        compiler_params=params(16),
        cost_estimate=cost(0.2),
        name="unpack",
    )(info, *pieces)


def pair_index(qb, kb):
    return qb * (qb + 1) // 2 + kb


def prepare(parts, block, docs, info_ref, bias_ref, open_ref):
    down = lax.broadcasted_iota(jnp.int32, (block, block), 0)
    across = lax.broadcasted_iota(jnp.int32, (1, block), 1)
    for qb in range(parts):
        lanes = qb * block + across
        opening = jnp.zeros((1, block), jnp.int32)
        first = jnp.int32(0)
        for n in range(docs):
            start = info_ref[2 + n]
            opening = jnp.where(start <= lanes, jnp.maximum(opening, start), opening)
            first = jnp.where(start <= qb * block, jnp.maximum(first, start), first)
        open_ref[qb] = first // block
        for kb in range(qb + 1):
            seen = down >= opening - kb * block
            if kb == qb:
                seen = seen & (down <= across)
            bias_ref[pair_index(qb, kb)] = jnp.where(seen, 0.0, MASKED).astype(jnp.float32)


def flip(x):
    return jnp.transpose(x.astype(jnp.float32))


def head_cols(h):
    return slice(h * HEAD_DIM, (h + 1) * HEAD_DIM)


def over_heads(tile):
    return jnp.concatenate([tile] * GROUP, axis=1)


def forward_kernel(parts, block, docs, info_ref, *refs):
    pieces = refs[:parts]
    out_ref, lse_ref = refs[parts : parts + 2]
    bias_ref, open_ref, q_s, k_s, vt_s, top_s, sum_s, acc_s = refs[parts + 2 :]
    me = info_ref[0]
    wide = GROUP * HEAD_DIM
    factor = math.log2(math.e) / math.sqrt(HEAD_DIM)
    prepare(parts, block, docs, info_ref, bias_ref, open_ref)
    for d in range(parts):
        for h in range(GROUP):
            q_s[me ^ d, h * block : (h + 1) * block] = pieces[d][:, head_cols(h)]
        k_s[me ^ d] = pieces[d][:, wide : wide + HEAD_DIM]
        vt_s[me ^ d] = flip(pieces[d][:, wide + HEAD_DIM :]).astype(jnp.bfloat16)

    def rows_of(qb, carry):
        top_s[...] = jnp.full_like(top_s, 2.0 * MASKED)
        sum_s[...] = jnp.zeros_like(sum_s)
        acc_s[...] = jnp.zeros_like(acc_s)

        def pair(back, carry):
            kb = qb - back
            bias = over_heads(bias_ref[pair_index(qb, kb)])
            raw = mm(k_s[kb], q_s[qb], NT) * factor + bias
            old = top_s[...]
            top = jnp.maximum(old, jnp.max(raw, axis=0, keepdims=True))
            shrink = jnp.exp2(old - top)
            raised = jnp.exp2(raw - top)
            top_s[...] = top
            sum_s[...] = sum_s[...] * shrink + jnp.sum(raised, axis=0, keepdims=True)
            acc_s[...] = acc_s[...] * shrink + mm(vt_s[kb], raised.astype(jnp.bfloat16))
            return carry

        lax.fori_loop(0, qb - open_ref[qb] + 1, pair, 0)
        out = (acc_s[...] / sum_s[...]).astype(jnp.bfloat16)
        spot = me ^ qb
        for h in range(GROUP):
            out_ref[head_cols(h), pl.ds(pl.multiple_of(spot * block, block), block)] = out[
                :, h * block : (h + 1) * block
            ]
        lse_ref[spot] = jnp.broadcast_to(top_s[...] + jnp.log2(sum_s[...]), lse_ref.shape[1:])
        return carry

    lax.fori_loop(0, parts, rows_of, 0)


def whole_block(dims):
    return pl.BlockSpec(dims, lambda i, info: (0,) * len(dims))


def piece_block(rows, cols, at):
    return pl.BlockSpec((rows, cols), lambda i, info: (0, at))


def attention(info, pieces, token, parts, docs):
    block, cols = pieces[-1][0].shape
    pairs = parts * (parts + 1) // 2
    wide = GROUP * HEAD_DIM
    vm = pltpu.VMEM
    return pl.pallas_call(
        functools.partial(forward_kernel, parts, block, docs),
        grid_spec=pltpu.PrefetchScalarGridSpec(
            num_scalar_prefetch=1,
            grid=(1,),
            in_specs=[piece_block(block, cols, at) for x, at in pieces],
            out_specs=[
                whole_block((wide, parts * block)),
                whole_block((parts, 8, GROUP * block)),
            ],
            scratch_shapes=[
                vm((pairs, block, block), jnp.float32),
                pltpu.SMEM((parts,), jnp.int32),
                vm((parts, GROUP * block, HEAD_DIM), jnp.bfloat16),
                vm((parts, block, HEAD_DIM), jnp.bfloat16),
                vm((parts, HEAD_DIM, block), jnp.bfloat16),
                vm((1, GROUP * block), jnp.float32),
                vm((1, GROUP * block), jnp.float32),
                vm((HEAD_DIM, GROUP * block), jnp.float32),
            ],
        ),
        out_shape=[
            shape((wide, parts * block)),
            shape((parts, 8, GROUP * block), jnp.float32),
        ],
        compiler_params=params(60),
        cost_estimate=cost(2.5),
        name="attention",
    )(gate([info], token)[0], *[x for x, at in pieces])


def backward_kernel(parts, block, docs, info_ref, *refs):
    pieces = refs[:parts]
    grad_ref, out_ref, lse_ref = refs[parts : parts + 3]
    res_ref = refs[parts + 3]
    bias_ref, open_ref, q_s, k_s, kt_s, v_s, do_s, dk_s, dv_s, dq_s = refs[parts + 4 :]
    me = info_ref[0]
    wide = GROUP * HEAD_DIM
    scale = 1.0 / math.sqrt(HEAD_DIM)
    factor = math.log2(math.e) * scale
    prepare(parts, block, docs, info_ref, bias_ref, open_ref)
    for d in range(parts):
        for h in range(GROUP):
            q_s[me ^ d, h * block : (h + 1) * block] = pieces[d][:, head_cols(h)]
            do_s[me ^ d, h * block : (h + 1) * block] = grad_ref[d, :, head_cols(h)]
        k_s[me ^ d] = pieces[d][:, wide : wide + HEAD_DIM]
        kt_s[me ^ d] = flip(pieces[d][:, wide : wide + HEAD_DIM]).astype(jnp.bfloat16)
        v_s[me ^ d] = pieces[d][:, wide + HEAD_DIM :]
    dk_s[...] = jnp.zeros_like(dk_s)
    dv_s[...] = jnp.zeros_like(dv_s)

    def rows_of(qb, carry):
        spot = me ^ qb
        dq_s[...] = jnp.zeros_like(dq_s)
        here = pl.ds(pl.multiple_of(spot * block, block), block)
        out = jnp.concatenate([out_ref[head_cols(h), here] for h in range(GROUP)], axis=1)
        delta = jnp.sum(flip(do_s[qb]) * out.astype(jnp.float32), axis=0, keepdims=True)
        lse = lse_ref[spot, :1]

        def pair(back, carry):
            kb = qb - back
            bias = over_heads(bias_ref[pair_index(qb, kb)])
            probs = jnp.exp2(mm(k_s[kb], q_s[qb], NT) * factor + bias - lse)
            dv_s[kb] += mm(probs.astype(jnp.bfloat16), do_s[qb])
            slope = (probs * (mm(v_s[kb], do_s[qb], NT) - delta)).astype(jnp.bfloat16)
            dk_s[kb] += mm(slope, q_s[qb])
            dq_s[...] += mm(kt_s[kb], slope)
            return carry

        lax.fori_loop(0, qb - open_ref[qb] + 1, pair, 0)
        back = (jnp.transpose(dq_s[...]) * scale).astype(jnp.bfloat16)
        for h in range(GROUP):
            res_ref[spot, :, head_cols(h)] = back[h * block : (h + 1) * block]
        return carry

    lax.fori_loop(0, parts, rows_of, 0)
    for kb in range(parts):
        res_ref[me ^ kb, :, wide : wide + HEAD_DIM] = (dk_s[kb] * scale).astype(jnp.bfloat16)
        res_ref[me ^ kb, :, wide + HEAD_DIM :] = dv_s[kb].astype(jnp.bfloat16)


def attention_back(info, pieces, grads, out, lse, token, parts, docs, gp):
    block, cols = pieces[-1][0].shape
    pairs = parts * (parts + 1) // 2
    wide = GROUP * HEAD_DIM
    vm = pltpu.VMEM
    return pl.pallas_call(
        functools.partial(backward_kernel, parts, block, docs),
        grid_spec=pltpu.PrefetchScalarGridSpec(
            num_scalar_prefetch=1,
            grid=(1,),
            in_specs=[piece_block(block, cols, at) for x, at in pieces]
            + [
                pl.BlockSpec((parts, block, wide), lambda i, info: (0, 0, gp)),
                whole_block((wide, parts * block)),
                whole_block((parts, 8, GROUP * block)),
            ],
            out_specs=whole_block((parts, block, cols)),
            scratch_shapes=[
                vm((pairs, block, block), jnp.float32),
                pltpu.SMEM((parts,), jnp.int32),
                vm((parts, GROUP * block, HEAD_DIM), jnp.bfloat16),
                vm((parts, block, HEAD_DIM), jnp.bfloat16),
                vm((parts, HEAD_DIM, block), jnp.bfloat16),
                vm((parts, block, HEAD_DIM), jnp.bfloat16),
                vm((parts, GROUP * block, HEAD_DIM), jnp.bfloat16),
                vm((parts, block, HEAD_DIM), jnp.float32),
                vm((parts, block, HEAD_DIM), jnp.float32),
                vm((HEAD_DIM, GROUP * block), jnp.float32),
            ],
        ),
        out_shape=shape((parts, block, cols)),
        compiler_params=params(60),
        cost_estimate=cost(1.0),
        name="attention_back",
    )(gate([info], token)[0], *[x for x, at in pieces], grads, out, lse)


def place_of(share, order):
    out = 0 * share
    for k, bit in enumerate(order):
        out = out + ((share >> bit) & 1) * (1 << k)
    return out


def unplace(place, order):
    out = 0 * place
    for k, bit in enumerate(order):
        out = out + ((place >> k) & 1) * (1 << bit)
    return out


def reverse_bits(x, bits):
    out = 0 * x
    for b in range(bits):
        out = out + ((x >> b) & 1) * (1 << (bits - 1 - b))
    return out


def weight_kernel(parts, groups, width, order, info_ref, *refs):
    outs, lows, highs = refs[:groups], refs[groups : groups + 2], refs[groups + 2 : groups + 4]
    chunk = refs[groups + 4 : groups + 2 + parts]
    keep_ref, send_ref = refs[groups + 2 + parts :]
    odd = ((info_ref[1] >> order[0]) & 1) == 1
    rows = GROUP * HEAD_DIM
    grads = [jnp.concatenate([lows[d][...], highs[d][...]], axis=1) for d in range(2)]
    grads = jnp.concatenate(grads + [x[...] for x in chunk], axis=0)
    for gp in range(groups):
        total = mm(outs[gp][...], grads)
        low, high = total[:, :width], total[:, width:]
        spot = slice(gp * rows, (gp + 1) * rows)
        keep_ref[0, spot] = jnp.where(odd, high, low)
        send_ref[0, spot] = jnp.where(odd, low, high).astype(jnp.bfloat16)


def weight_terms(info, outs, near, chunk, token, shares, c, chunks, width, order):
    groups, parts = len(outs), 2 + len(chunk)
    rows, block = outs[0].shape[0], near[0].shape[0]
    half = shares // 2
    bits = half.bit_length() - 1
    spot = pl.BlockSpec((1, groups * rows, width), lambda t, info: (reverse_bits(t, bits), 0, 0))

    def mate(t, info):
        return t ^ (place_of(info[1], order) >> 1)

    def original(side, x):
        shift = (x.shape[1] - shares * chunks * width) // width
        return pl.BlockSpec(
            (block, width),
            lambda t, info: (0, shift + unplace(2 * mate(t, info) + side, order) * chunks + c),
        )

    return pl.pallas_call(
        functools.partial(weight_kernel, parts, groups, width, order),
        grid_spec=pltpu.PrefetchScalarGridSpec(
            num_scalar_prefetch=1,
            grid=(half,),
            in_specs=[pl.BlockSpec((rows, parts * block), lambda t, info: (0, 0))] * groups
            + [original(side, x) for side in range(2) for x in near]
            + [pl.BlockSpec((block, 2 * width), lambda t, info: (0, mate(t, info)))] * len(chunk),
            out_specs=[spot, spot],
        ),
        out_shape=[
            shape((half, groups * rows, width), jnp.float32),
            shape((half, groups * rows, width)),
        ],
        compiler_params=params(16),
        cost_estimate=cost(0.3),
        name="weight_terms",
    )(gate([info], token)[0], *outs, *near, *near, *chunk)


def merge_kernel(keep_low, keep_high, got_low, got_high, keep_ref, send_ref):
    keep_ref[...] = keep_low[...] + got_low[...].astype(jnp.float32)
    send_ref[...] = (keep_high[...] + got_high[...].astype(jnp.float32)).astype(jnp.bfloat16)


def merge(keep, got, token):
    count, rows, width = keep.shape
    half = count // 2
    keep = gate([keep], token)[0]
    low = pl.BlockSpec((1, rows, width), lambda t: (t, 0, 0))
    high = pl.BlockSpec((1, rows, width), lambda t: (t + half, 0, 0))
    return pl.pallas_call(
        merge_kernel,
        grid=(half,),
        in_specs=[low, high, low, high],
        out_specs=[low, low],
        out_shape=[
            shape((half, rows, width), jnp.float32),
            shape((half, rows, width)),
        ],
        compiler_params=params(12),
        cost_estimate=cost(0.02),
        name="merge",
    )(keep, keep, got, got)


def finish_kernel(scale, keep_ref, got_ref, *refs):
    refs[-1][...] = (keep_ref[0] + got_ref[0].astype(jnp.float32)) * scale


def finish(keep, got, so_far, token, c, chunks, scale):
    _, rows, width = keep.shape
    more = [] if so_far is None else [so_far]
    step = rows // 2
    spec = pl.BlockSpec((1, step, width), lambda i: (0, i, 0))
    return pl.pallas_call(
        functools.partial(finish_kernel, scale),
        grid=(rows // step,),
        in_specs=[spec, spec] + [ANY] * len(more),
        out_specs=pl.BlockSpec((step, width), lambda i: (i, c)),
        out_shape=shape((rows, width * chunks), jnp.float32),
        input_output_aliases={2: 0} if more else {},
        compiler_params=params(8),
        cost_estimate=cost(0.02),
        name="finish",
    )(gate([keep], token)[0], got, *more)


def shifted(ref, like, columns):
    more = ref.shape[1] - like.shape[1]
    return slice(columns.start + more, columns.stop + more)


def project_kernel(parts, shares, width, chunks, orders, picked, first, last, *refs):
    w_ref, near = refs[0], refs[1:3]
    far = refs[3 : 3 + len(picked) * (parts - 2)]
    acc_ref, out_ref = refs[-2] if not first else None, refs[-1]
    columns = [(c, unplace(p, orders[c])) for c in picked for p in range(shares)]
    weights = jnp.concatenate([w_ref[:, column(j, c, chunks, width)] for c, j in columns], axis=1)
    for d in range(parts):
        if d < 2:
            rows = jnp.concatenate([near[d][:, shifted(near[d], w_ref, column(j, c, chunks, width))] for c, j in columns], axis=1)
        else:
            mine = [far[i * (parts - 2) + d - 2][...] for i in range(len(picked))]
            rows = mine[0] if len(mine) == 1 else jnp.concatenate(mine, axis=1)
        total = mm(rows, weights, NT)
        if not first:
            total += acc_ref[d]
        out_ref[d] = total.astype(out_ref.dtype)


def project(out_weight, near, far, acc, token, orders, picked, shares, width, last):
    feats, model = out_weight.shape
    rows = near[0].shape[0]
    parts = 2 + len(far[0])
    step = min(256, feats)
    flat = [x for group in far for x in group]
    first = acc is None
    block = pl.BlockSpec((parts, rows, step), lambda i: (0, 0, i))
    return pl.pallas_call(
        functools.partial(
            project_kernel, parts, shares, width, len(orders), orders, picked, first, last
        ),
        grid=(feats // step,),
        in_specs=[pl.BlockSpec((step, model), lambda i: (i, 0))]
        + [pl.BlockSpec((rows, x.shape[1]), lambda i: (0, 0)) for x in near]
        + [pl.BlockSpec((rows, shares * width), lambda i: (0, 0))] * len(flat)
        + ([] if first else [block]),
        out_specs=block,
        out_shape=shape((parts, rows, feats), jnp.bfloat16 if last else jnp.float32),
        compiler_params=params(24),
        cost_estimate=cost(0.5),
        name="project",
    )(gate([out_weight], token)[0], *near, *flat, *([] if first else [acc]))


def body(grad_out, queries, keys, values, out_weight, doc_starts):
    parts, shares = lax.axis_size("seq"), lax.axis_size("dp")
    groups = KV_HEADS // parts
    docs = doc_starts.shape[-1]
    cotangent = grad_out[0]
    rows, model = cotangent.shape
    chunks = max(1, min(4, model // shares // 128))
    width = model // shares // chunks
    bits = tuple(range(shares.bit_length() - 1))
    turned = bits[1:] + bits[:1]
    orders = [turned if c == 0 else bits for c in range(chunks)]
    scale = 1.0 / math.sqrt(rows * parts * shares)
    info = jnp.concatenate(
        [
            jnp.stack([lax.axis_index("seq"), lax.axis_index("dp")]).astype(jnp.int32),
            doc_starts[0],
        ]
    )

    def over_seq(x, d):
        return lax.ppermute(x, "seq", [(i, i ^ d) for i in range(parts)])

    def over_dp(x, d):
        return lax.ppermute(x, "dp", [(i, i ^ d) for i in range(shares)])

    far = range(2, parts)
    all_groups = tuple(range(groups))
    me = lax.axis_index("seq").astype(jnp.int32).reshape(1)
    sources = (queries[0], keys[0], values[0])
    packed = [pack(me, sources, parts, tuple((d, (0,)) for d in far))]
    rest = [(d, (gp,)) for gp in range(1, groups) for d in far]
    rest = pack(
        gate([me], packed[0][0])[0],
        sources,
        parts,
        tuple([(0, all_groups), (1, all_groups)] + rest),
    )
    for gp in range(1, groups):
        packed.append(rest[2 + (gp - 1) * len(far) : 2 + gp * len(far)])
    sent_far = [[over_seq(x, d) for x, d in zip(group, far)] for group in packed]
    core = over_seq(rest[1], 1)
    pieces = [[(rest[0], gp), (core, gp)] + [(x, 0) for x in sent_far[gp]] for gp in range(groups)]
    sends = pack_chunks(gate([cotangent], rest[0])[0], orders, shares, width)
    near = [cotangent, over_seq(gate([cotangent], *sent_far[0], sends[-1])[0], 1)]

    far_half = {}

    def send_chunk(c, *tokens):
        mine = gate([sends[c]], *tokens)[0]
        far_half[c] = [over_seq(mine, d) for d in range(2, parts, 2)]

    for c in range(chunks):
        if c < groups:
            send_chunk(c, *sent_far[c], sends[-1])
        else:
            send_chunk(c, *far_half[max(0, c - groups)])

    fwd = []
    token = sends[-1]
    for gp in range(groups):
        fwd.append(attention(info, pieces[gp], token, parts, docs))
        token = fwd[-1][0]
        if gp == 0:
            token = (token, near[1])
    outs = [pair[0] for pair in fwd]

    fars, state, back, results = {}, {}, {}, {}
    acc = weight_grad = None

    def hop(c, send, stage):
        return over_dp(send, 1 << orders[c][stage])

    def receive(c):
        fars[c] = []
        for x in gate(far_half[c], token):
            fars[c] += [x, over_seq(x, 1)]

    def weigh(c):
        nonlocal token
        if c not in fars:
            receive(c)
        keep, send = weight_terms(
            info, outs, near, fars[c], token, shares, c, chunks, width, orders[c]
        )
        token = send
        state[c] = (keep, hop(c, send, 0), 1)

    def advance(c):
        nonlocal token, weight_grad
        if c not in state or state[c] is None:
            return
        keep, got, stage = state[c]
        if stage == len(bits):
            token = weight_grad = finish(keep, got, weight_grad, token, c, chunks, scale)
            state[c] = None
        else:
            keep, send = merge(keep, got, token)
            token = send
            state[c] = (keep, hop(c, send, stage), stage + 1)

    def project_step(picked, last):
        nonlocal token, acc
        token = acc = project(
            out_weight, near, [fars[c] for c in picked], acc, token, orders, picked, shares, width, last
        )

    def send_back(gp):
        nonlocal token
        res = attention_back(info, pieces[gp], acc, outs[gp], fwd[gp][1], token, parts, docs, gp)
        token = results[gp] = res
        back[gp] = {d: over_seq(res[d : d + 2], d) for d in range(2, parts, 2)}

    def hand_over(gp, *tokens):
        got = gate([back[gp][d] for d in range(2, parts, 2)], *tokens)
        mine = [results[gp][1:2]] + [x[1:2] for x in got]
        crossed = over_seq(jnp.concatenate(mine, axis=0), 1)
        out = [results[gp][0], crossed[0]]
        for i, x in enumerate(got):
            out += [x[0], crossed[1 + i]]
        return out

    last = chunks - 1
    for c in range(last):
        weigh(c)
    receive(last)
    advance(0)
    if last:
        project_step(list(range(last)), False)
    weigh(last)
    advance(1)
    project_step([last], True)
    send_back(0)
    for c in (0, 1, 2):
        advance(c)
    for gp in range(1, groups):
        send_back(gp)
    advance(1)
    advance(2)
    advance(3)
    firsts = hand_over(0, token)
    advance(0)
    token = (token, firsts[1])
    advance(3)
    for _ in bits:
        for c in range(chunks):
            advance(c)
    lasts = [hand_over(gp, token) for gp in range(1, groups)]
    back = firsts + [x for group in lasts for x in group]
    grad_q, grad_k, grad_v = unpack(gate([info], token)[0], back, parts, groups)
    return (grad_q[None], grad_k[None], grad_v[None], weight_grad)


def solution(mesh):
    return jax.shard_map(
        body,
        mesh=mesh,
        in_specs=(
            P("dp", "seq", None),
            P("dp", "seq", None),
            P("dp", "seq", None),
            P("dp", "seq", None),
            P("seq", None),
            P("dp", None),
        ),
        out_specs=(
            P("dp", "seq", None),
            P("dp", "seq", None),
            P("dp", "seq", None),
            P("seq", "dp"),
        ),
        check_vma=False,
    )
```

```python
import functools
import math

import jax
import jax.numpy as jnp
from jax import lax
from jax.experimental import pallas as pl
from jax.experimental.pallas import tpu as pltpu
from jax.sharding import PartitionSpec as P

HEADS = 32
KV_HEADS = 8
HEAD_DIM = 128
GROUP = HEADS // KV_HEADS
MASKED = -1e30
NT = (((1,), (1,)), ((), ()))
NN = (((1,), (0,)), ((), ()))


def mm(a, b, dims=NN):
    return lax.dot_general(a, b, dims, preferred_element_type=jnp.float32)


def params(mib):
    return pltpu.CompilerParams(vmem_limit_bytes=mib * 2**20)


def cost(weight):
    return pl.CostEstimate(flops=int(weight * 1e9), bytes_accessed=1024, transcendentals=0)


ANY = pl.BlockSpec(memory_space=pl.ANY)


def shape(dims, dtype=jnp.bfloat16):
    return jax.ShapeDtypeStruct(dims, dtype)


def gate(arrays, *tokens):
    flat = [x for token in tokens for x in (token if isinstance(token, tuple) else (token,))]
    return list(lax.optimization_barrier((*arrays, *flat)))[: len(arrays)]


def pack_kernel(jobs, joined, me_ref, *refs):
    wide = GROUP * HEAD_DIM
    size = wide + 2 * HEAD_DIM
    sources, outs = iter(refs[: len(refs) - len(jobs)]), refs[len(refs) - len(jobs) :]
    if joined:
        outs[1][:, size * len(jobs[1][1]) :] = refs[0][...]
        next(sources)
    for out, (d, members) in zip(outs, jobs):
        for slot in range(len(members)):
            start = slot * size
            for width in (wide, HEAD_DIM, HEAD_DIM):
                out[:, start : start + width] = next(sources)[...]
                start += width


def pack(me, sources, parts, jobs, joined=None):
    rows = sources[0].shape[0]
    groups = KV_HEADS // parts
    wide = GROUP * HEAD_DIM
    size = wide + 2 * HEAD_DIM
    step = min(128, rows)

    def pick(width, d, gp):
        return pl.BlockSpec((step, width), lambda i, me: (i, (me[0] ^ d) * groups + gp))

    specs = [
        pick(width, d, gp)
        for d, members in jobs
        for gp in members
        for width in (wide, HEAD_DIM, HEAD_DIM)
    ]
    more = [] if joined is None else [joined]
    widths = [size * len(members) for d, members in jobs]
    if more:
        widths[1] += joined.shape[1]
    return pl.pallas_call(
        functools.partial(pack_kernel, jobs, bool(more)),
        grid_spec=pltpu.PrefetchScalarGridSpec(
            num_scalar_prefetch=1,
            grid=(rows // step,),
            in_specs=[pl.BlockSpec((step, x.shape[1]), lambda i, me: (i, 0)) for x in more] + specs,
            out_specs=[pl.BlockSpec((step, width), lambda i, me: (i, 0)) for width in widths],
        ),
        out_shape=[shape((rows, width)) for width in widths],
        compiler_params=params(60),
        cost_estimate=cost(0.2),
        name="pack",
    )(me, *more, *sources * (len(specs) // 3))


def column(share, c, chunks, width):
    return slice((share * chunks + c) * width, (share * chunks + c + 1) * width)


def pack_chunks_kernel(orders, shares, width, g_ref, *out_refs):
    for c, order in enumerate(orders):
        for place in range(shares):
            share = unplace(place, order)
            out_refs[c][:, place * width : (place + 1) * width] = g_ref[
                :, column(share, c, len(orders), width)
            ]


def pack_chunks(cotangent, orders, shares, width):
    rows, model = cotangent.shape
    step = min(64, rows)
    return pl.pallas_call(
        functools.partial(pack_chunks_kernel, orders, shares, width),
        grid=(rows // step,),
        in_specs=[pl.BlockSpec((step, model), lambda i: (i, 0))],
        out_specs=[pl.BlockSpec((step, shares * width), lambda i: (i, 0))] * len(orders),
        out_shape=[shape((rows, shares * width)) for order in orders],
        compiler_params=params(60),
        cost_estimate=cost(0.2),
        name="pack_chunks",
    )(cotangent)


def unpack_kernel(parts, groups, info_ref, *refs):
    count = parts * groups
    q_ref, k_ref, v_ref = refs[count:]
    wide = GROUP * HEAD_DIM
    for gp in range(groups):
        for d in range(parts):
            piece = refs[gp * parts + d]
            place = (info_ref[0] ^ d) * groups + gp
            q_ref[:, pl.ds(pl.multiple_of(place * wide, wide), wide)] = piece[:, :wide]
            narrow = pl.ds(pl.multiple_of(place * HEAD_DIM, HEAD_DIM), HEAD_DIM)
            k_ref[:, narrow] = piece[:, wide : wide + HEAD_DIM]
            v_ref[:, narrow] = piece[:, wide + HEAD_DIM :]


def unpack(info, pieces, parts, groups):
    rows, cols = pieces[0].shape
    wide = GROUP * HEAD_DIM
    step = min(64, rows)
    total = parts * groups
    widths = (total * wide, total * HEAD_DIM, total * HEAD_DIM)
    return pl.pallas_call(
        functools.partial(unpack_kernel, parts, groups),
        grid_spec=pltpu.PrefetchScalarGridSpec(
            num_scalar_prefetch=1,
            grid=(rows // step,),
            in_specs=[pl.BlockSpec((step, cols), lambda i, info: (i, 0))] * total,
            out_specs=[pl.BlockSpec((step, w), lambda i, info: (i, 0)) for w in widths],
        ),
        out_shape=[shape((rows, w)) for w in widths],
        compiler_params=params(16),
        cost_estimate=cost(0.2),
        name="unpack",
    )(info, *pieces)


def pair_index(qb, kb):
    return qb * (qb + 1) // 2 + kb


def prepare(parts, block, docs, info_ref, bias_ref, open_ref):
    down = lax.broadcasted_iota(jnp.int32, (block, block), 0)
    across = lax.broadcasted_iota(jnp.int32, (1, block), 1)
    for qb in range(parts):
        lanes = qb * block + across
        opening = jnp.zeros((1, block), jnp.int32)
        first = jnp.int32(0)
        for n in range(docs):
            start = info_ref[2 + n]
            opening = jnp.where(start <= lanes, jnp.maximum(opening, start), opening)
            first = jnp.where(start <= qb * block, jnp.maximum(first, start), first)
        open_ref[qb] = first // block
        for kb in range(qb + 1):
            seen = down >= opening - kb * block
            if kb == qb:
                seen = seen & (down <= across)
            bias_ref[pair_index(qb, kb)] = jnp.where(seen, 0.0, MASKED).astype(jnp.float32)


def flip(x):
    return jnp.transpose(x.astype(jnp.float32))


def head_cols(h):
    return slice(h * HEAD_DIM, (h + 1) * HEAD_DIM)


def over_heads(tile):
    return jnp.concatenate([tile] * GROUP, axis=1)


def forward_kernel(parts, block, docs, info_ref, *refs):
    pieces = refs[:parts]
    out_ref, lse_ref = refs[parts : parts + 2]
    bias_ref, open_ref, q_s, k_s, vt_s, top_s, sum_s, acc_s = refs[parts + 2 :]
    me = info_ref[0]
    wide = GROUP * HEAD_DIM
    factor = math.log2(math.e) / math.sqrt(HEAD_DIM)
    prepare(parts, block, docs, info_ref, bias_ref, open_ref)
    for d in range(parts):
        for h in range(GROUP):
            q_s[me ^ d, h * block : (h + 1) * block] = pieces[d][:, head_cols(h)]
        k_s[me ^ d] = pieces[d][:, wide : wide + HEAD_DIM]
        vt_s[me ^ d] = flip(pieces[d][:, wide + HEAD_DIM :]).astype(jnp.bfloat16)

    def rows_of(qb, carry):
        top_s[...] = jnp.full_like(top_s, 2.0 * MASKED)
        sum_s[...] = jnp.zeros_like(sum_s)
        acc_s[...] = jnp.zeros_like(acc_s)

        def pair(back, carry):
            kb = qb - back
            bias = over_heads(bias_ref[pair_index(qb, kb)])
            raw = mm(k_s[kb], q_s[qb], NT) * factor + bias
            old = top_s[...]
            top = jnp.maximum(old, jnp.max(raw, axis=0, keepdims=True))
            shrink = jnp.exp2(old - top)
            raised = jnp.exp2(raw - top)
            top_s[...] = top
            sum_s[...] = sum_s[...] * shrink + jnp.sum(raised, axis=0, keepdims=True)
            acc_s[...] = acc_s[...] * shrink + mm(vt_s[kb], raised.astype(jnp.bfloat16))
            return carry

        lax.fori_loop(0, qb - open_ref[qb] + 1, pair, 0)
        out = (acc_s[...] / sum_s[...]).astype(jnp.bfloat16)
        spot = me ^ qb
        for h in range(GROUP):
            out_ref[head_cols(h), pl.ds(pl.multiple_of(spot * block, block), block)] = out[
                :, h * block : (h + 1) * block
            ]
        lse_ref[spot] = jnp.broadcast_to(top_s[...] + jnp.log2(sum_s[...]), lse_ref.shape[1:])
        return carry

    lax.fori_loop(0, parts, rows_of, 0)


def whole_block(dims):
    return pl.BlockSpec(dims, lambda i, info: (0,) * len(dims))


def piece_block(rows, cols, at):
    return pl.BlockSpec((rows, cols), lambda i, info: (0, at))


def attention(info, pieces, token, parts, docs):
    block, cols = pieces[-1][0].shape
    pairs = parts * (parts + 1) // 2
    wide = GROUP * HEAD_DIM
    vm = pltpu.VMEM
    return pl.pallas_call(
        functools.partial(forward_kernel, parts, block, docs),
        grid_spec=pltpu.PrefetchScalarGridSpec(
            num_scalar_prefetch=1,
            grid=(1,),
            in_specs=[piece_block(block, cols, at) for x, at in pieces],
            out_specs=[
                whole_block((wide, parts * block)),
                whole_block((parts, 8, GROUP * block)),
            ],
            scratch_shapes=[
                vm((pairs, block, block), jnp.float32),
                pltpu.SMEM((parts,), jnp.int32),
                vm((parts, GROUP * block, HEAD_DIM), jnp.bfloat16),
                vm((parts, block, HEAD_DIM), jnp.bfloat16),
                vm((parts, HEAD_DIM, block), jnp.bfloat16),
                vm((1, GROUP * block), jnp.float32),
                vm((1, GROUP * block), jnp.float32),
                vm((HEAD_DIM, GROUP * block), jnp.float32),
            ],
        ),
        out_shape=[
            shape((wide, parts * block)),
            shape((parts, 8, GROUP * block), jnp.float32),
        ],
        compiler_params=params(24),
        cost_estimate=cost(2.5),
        name="attention",
    )(gate([info], token)[0], *[x for x, at in pieces])


def backward_kernel(parts, block, docs, info_ref, *refs):
    pieces = refs[:parts]
    grad_ref, out_ref, lse_ref = refs[parts : parts + 3]
    res_ref = refs[parts + 3]
    bias_ref, open_ref, q_s, k_s, kt_s, v_s, do_s, dk_s, dv_s, dq_s = refs[parts + 4 :]
    me = info_ref[0]
    wide = GROUP * HEAD_DIM
    scale = 1.0 / math.sqrt(HEAD_DIM)
    factor = math.log2(math.e) * scale
    prepare(parts, block, docs, info_ref, bias_ref, open_ref)
    for d in range(parts):
        for h in range(GROUP):
            q_s[me ^ d, h * block : (h + 1) * block] = pieces[d][:, head_cols(h)]
            do_s[me ^ d, h * block : (h + 1) * block] = grad_ref[d, :, head_cols(h)]
        k_s[me ^ d] = pieces[d][:, wide : wide + HEAD_DIM]
        kt_s[me ^ d] = flip(pieces[d][:, wide : wide + HEAD_DIM]).astype(jnp.bfloat16)
        v_s[me ^ d] = pieces[d][:, wide + HEAD_DIM :]
    dk_s[...] = jnp.zeros_like(dk_s)
    dv_s[...] = jnp.zeros_like(dv_s)

    def rows_of(qb, carry):
        spot = me ^ qb
        dq_s[...] = jnp.zeros_like(dq_s)
        here = pl.ds(pl.multiple_of(spot * block, block), block)
        out = jnp.concatenate([out_ref[head_cols(h), here] for h in range(GROUP)], axis=1)
        delta = jnp.sum(flip(do_s[qb]) * out.astype(jnp.float32), axis=0, keepdims=True)
        lse = lse_ref[spot, :1]

        def pair(back, carry):
            kb = qb - back
            bias = over_heads(bias_ref[pair_index(qb, kb)])
            probs = jnp.exp2(mm(k_s[kb], q_s[qb], NT) * factor + bias - lse)
            dv_s[kb] += mm(probs.astype(jnp.bfloat16), do_s[qb])
            slope = (probs * (mm(v_s[kb], do_s[qb], NT) - delta)).astype(jnp.bfloat16)
            dk_s[kb] += mm(slope, q_s[qb])
            dq_s[...] += mm(kt_s[kb], slope)
            return carry

        lax.fori_loop(0, qb - open_ref[qb] + 1, pair, 0)
        back = (jnp.transpose(dq_s[...]) * scale).astype(jnp.bfloat16)
        for h in range(GROUP):
            res_ref[spot, :, head_cols(h)] = back[h * block : (h + 1) * block]
        return carry

    lax.fori_loop(0, parts, rows_of, 0)
    for kb in range(parts):
        res_ref[me ^ kb, :, wide : wide + HEAD_DIM] = (dk_s[kb] * scale).astype(jnp.bfloat16)
        res_ref[me ^ kb, :, wide + HEAD_DIM :] = dv_s[kb].astype(jnp.bfloat16)


def attention_back(info, pieces, grads, out, lse, token, parts, docs, gp):
    block, cols = pieces[-1][0].shape
    pairs = parts * (parts + 1) // 2
    wide = GROUP * HEAD_DIM
    vm = pltpu.VMEM
    return pl.pallas_call(
        functools.partial(backward_kernel, parts, block, docs),
        grid_spec=pltpu.PrefetchScalarGridSpec(
            num_scalar_prefetch=1,
            grid=(1,),
            in_specs=[piece_block(block, cols, at) for x, at in pieces]
            + [
                pl.BlockSpec((parts, block, wide), lambda i, info: (0, 0, gp)),
                whole_block((wide, parts * block)),
                whole_block((parts, 8, GROUP * block)),
            ],
            out_specs=whole_block((parts, block, cols)),
            scratch_shapes=[
                vm((pairs, block, block), jnp.float32),
                pltpu.SMEM((parts,), jnp.int32),
                vm((parts, GROUP * block, HEAD_DIM), jnp.bfloat16),
                vm((parts, block, HEAD_DIM), jnp.bfloat16),
                vm((parts, HEAD_DIM, block), jnp.bfloat16),
                vm((parts, block, HEAD_DIM), jnp.bfloat16),
                vm((parts, GROUP * block, HEAD_DIM), jnp.bfloat16),
                vm((parts, block, HEAD_DIM), jnp.float32),
                vm((parts, block, HEAD_DIM), jnp.float32),
                vm((HEAD_DIM, GROUP * block), jnp.float32),
            ],
        ),
        out_shape=shape((parts, block, cols)),
        compiler_params=params(32),
        cost_estimate=cost(1.0),
        name="attention_back",
    )(gate([info], token)[0], *[x for x, at in pieces], grads, out, lse)


def place_of(share, order):
    out = 0 * share
    for k, bit in enumerate(order):
        out = out + ((share >> bit) & 1) * (1 << k)
    return out


def unplace(place, order):
    out = 0 * place
    for k, bit in enumerate(order):
        out = out + ((place >> k) & 1) * (1 << bit)
    return out


def reverse_bits(x, bits):
    out = 0 * x
    for b in range(bits):
        out = out + ((x >> b) & 1) * (1 << (bits - 1 - b))
    return out


def weight_kernel(parts, groups, width, order, info_ref, *refs):
    outs, lows, highs = refs[:groups], refs[groups : groups + 2], refs[groups + 2 : groups + 4]
    chunk = refs[groups + 4 : groups + 2 + parts]
    keep_ref, send_ref = refs[groups + 2 + parts :]
    odd = ((info_ref[1] >> order[0]) & 1) == 1
    rows = GROUP * HEAD_DIM
    grads = [jnp.concatenate([lows[d][...], highs[d][...]], axis=1) for d in range(2)]
    grads = jnp.concatenate(grads + [x[...] for x in chunk], axis=0)
    for gp in range(groups):
        total = mm(outs[gp][...], grads)
        low, high = total[:, :width], total[:, width:]
        spot = slice(gp * rows, (gp + 1) * rows)
        keep_ref[0, spot] = jnp.where(odd, high, low)
        send_ref[0, spot] = jnp.where(odd, low, high).astype(jnp.bfloat16)


def weight_terms(info, outs, near, chunk, token, shares, c, chunks, width, order):
    groups, parts = len(outs), 2 + len(chunk)
    rows, block = outs[0].shape[0], near[0].shape[0]
    half = shares // 2
    bits = half.bit_length() - 1
    spot = pl.BlockSpec((1, groups * rows, width), lambda t, info: (reverse_bits(t, bits), 0, 0))

    def mate(t, info):
        return t ^ (place_of(info[1], order) >> 1)

    def original(side, x):
        shift = (x.shape[1] - shares * chunks * width) // width
        return pl.BlockSpec(
            (block, width),
            lambda t, info: (0, shift + unplace(2 * mate(t, info) + side, order) * chunks + c),
        )

    return pl.pallas_call(
        functools.partial(weight_kernel, parts, groups, width, order),
        grid_spec=pltpu.PrefetchScalarGridSpec(
            num_scalar_prefetch=1,
            grid=(half,),
            in_specs=[pl.BlockSpec((rows, parts * block), lambda t, info: (0, 0))] * groups
            + [original(side, x) for side in range(2) for x in near]
            + [pl.BlockSpec((block, 2 * width), lambda t, info: (0, mate(t, info)))] * len(chunk),
            out_specs=[spot, spot],
        ),
        out_shape=[
            shape((half, groups * rows, width), jnp.float32),
            shape((half, groups * rows, width)),
        ],
        compiler_params=params(16),
        cost_estimate=cost(0.2),
        name="weight_terms",
    )(gate([info], token)[0], *outs, *near, *near, *chunk)


def merge_kernel(keep_low, keep_high, got_low, got_high, keep_ref, send_ref):
    keep_ref[...] = keep_low[...] + got_low[...].astype(jnp.float32)
    send_ref[...] = (keep_high[...] + got_high[...].astype(jnp.float32)).astype(jnp.bfloat16)


def merge(keep, got, token):
    count, rows, width = keep.shape
    half = count // 2
    keep = gate([keep], token)[0]
    low = pl.BlockSpec((1, rows, width), lambda t: (t, 0, 0))
    high = pl.BlockSpec((1, rows, width), lambda t: (t + half, 0, 0))
    return pl.pallas_call(
        merge_kernel,
        grid=(half,),
        in_specs=[low, high, low, high],
        out_specs=[low, low],
        out_shape=[
            shape((half, rows, width), jnp.float32),
            shape((half, rows, width)),
        ],
        compiler_params=params(12),
        cost_estimate=cost(0.02),
        name="merge",
    )(keep, keep, got, got)


def finish_kernel(scale, keep_ref, got_ref, *refs):
    refs[-1][...] = (keep_ref[0] + got_ref[0].astype(jnp.float32)) * scale


def finish(keep, got, so_far, token, c, chunks, scale):
    _, rows, width = keep.shape
    more = [] if so_far is None else [so_far]
    step = rows // 2
    spec = pl.BlockSpec((1, step, width), lambda i: (0, i, 0))
    return pl.pallas_call(
        functools.partial(finish_kernel, scale),
        grid=(rows // step,),
        in_specs=[spec, spec] + [ANY] * len(more),
        out_specs=pl.BlockSpec((step, width), lambda i: (i, c)),
        out_shape=shape((rows, width * chunks), jnp.float32),
        input_output_aliases={2: 0} if more else {},
        compiler_params=params(8),
        cost_estimate=cost(0.02),
        name="finish",
    )(gate([keep], token)[0], got, *more)


def shifted(ref, like, columns):
    more = ref.shape[1] - like.shape[1]
    return slice(columns.start + more, columns.stop + more)


def project_kernel(parts, shares, width, chunks, orders, picked, first, last, *refs):
    w_ref, near = refs[0], refs[1:3]
    far = refs[3 : 3 + len(picked) * (parts - 2)]
    acc_ref, out_ref = refs[-2] if not first else None, refs[-1]
    columns = [(c, unplace(p, orders[c])) for c in picked for p in range(shares)]
    weights = jnp.concatenate([w_ref[:, column(j, c, chunks, width)] for c, j in columns], axis=1)
    for d in range(parts):
        if d < 2:
            rows = jnp.concatenate([near[d][:, shifted(near[d], w_ref, column(j, c, chunks, width))] for c, j in columns], axis=1)
        else:
            mine = [far[i * (parts - 2) + d - 2][...] for i in range(len(picked))]
            rows = mine[0] if len(mine) == 1 else jnp.concatenate(mine, axis=1)
        total = mm(rows, weights, NT)
        if not first:
            total += acc_ref[d]
        out_ref[d] = total.astype(out_ref.dtype)


def project(out_weight, near, far, acc, token, orders, picked, shares, width, last):
    feats, model = out_weight.shape
    rows = near[0].shape[0]
    parts = 2 + len(far[0])
    step = min(256, feats)
    flat = [x for group in far for x in group]
    first = acc is None
    block = pl.BlockSpec((parts, rows, step), lambda i: (0, 0, i))
    return pl.pallas_call(
        functools.partial(
            project_kernel, parts, shares, width, len(orders), orders, picked, first, last
        ),
        grid=(feats // step,),
        in_specs=[pl.BlockSpec((step, model), lambda i: (i, 0))]
        + [pl.BlockSpec((rows, x.shape[1]), lambda i: (0, 0)) for x in near]
        + [pl.BlockSpec((rows, shares * width), lambda i: (0, 0))] * len(flat)
        + ([] if first else [block]),
        out_specs=block,
        out_shape=shape((parts, rows, feats), jnp.bfloat16 if last else jnp.float32),
        compiler_params=params(24),
        cost_estimate=cost(0.2),
        name="project",
    )(gate([out_weight], token)[0], *near, *flat, *([] if first else [acc]))


def body(grad_out, queries, keys, values, out_weight, doc_starts):
    parts, shares = lax.axis_size("seq"), lax.axis_size("dp")
    groups = KV_HEADS // parts
    docs = doc_starts.shape[-1]
    cotangent = grad_out[0]
    rows, model = cotangent.shape
    chunks = max(1, min(4, model // shares // 128))
    width = model // shares // chunks
    bits = tuple(range(shares.bit_length() - 1))
    turned = bits[1:] + bits[:1]
    orders = [turned if c == 0 else bits for c in range(chunks)]
    scale = 1.0 / math.sqrt(rows * parts * shares)
    info = jnp.concatenate(
        [
            jnp.stack([lax.axis_index("seq"), lax.axis_index("dp")]).astype(jnp.int32),
            doc_starts[0],
        ]
    )

    def over_seq(x, d):
        return lax.ppermute(x, "seq", [(i, i ^ d) for i in range(parts)])

    def over_dp(x, d):
        return lax.ppermute(x, "dp", [(i, i ^ d) for i in range(shares)])

    far = range(2, parts)
    all_groups = tuple(range(groups))
    me = lax.axis_index("seq").astype(jnp.int32).reshape(1)
    sources = (queries[0], keys[0], values[0])
    packed = [pack(me, sources, parts, tuple((d, (0,)) for d in far))]
    rest = [(d, (gp,)) for gp in range(1, groups) for d in far]
    rest = pack(
        gate([me], packed[0][0])[0],
        sources,
        parts,
        tuple([(0, all_groups), (1, all_groups)] + rest),
    )
    for gp in range(1, groups):
        packed.append(rest[2 + (gp - 1) * len(far) : 2 + gp * len(far)])
    sent_far = [[over_seq(x, d) for x, d in zip(group, far)] for group in packed]
    core = over_seq(rest[1], 1)
    pieces = [[(rest[0], gp), (core, gp)] + [(x, 0) for x in sent_far[gp]] for gp in range(groups)]
    sends = pack_chunks(gate([cotangent], rest[0])[0], orders, shares, width)
    near = [cotangent, over_seq(gate([cotangent], *sent_far[0], sends[-1])[0], 1)]

    far_half = {}

    def send_chunk(c, *tokens):
        mine = gate([sends[c]], *tokens)[0]
        far_half[c] = [over_seq(mine, d) for d in range(2, parts, 2)]

    for c in range(chunks):
        if c < groups:
            send_chunk(c, *sent_far[c], sends[-1])
        else:
            send_chunk(c, *far_half[max(0, c - groups)])

    fwd = []
    token = sends[-1]
    for gp in range(groups):
        fwd.append(attention(info, pieces[gp], token, parts, docs))
        token = fwd[-1][0]
        if gp == 0:
            token = (token, near[1])
    outs = [pair[0] for pair in fwd]

    fars, state, back, results = {}, {}, {}, {}
    acc = weight_grad = None

    def hop(c, send, stage):
        return over_dp(send, 1 << orders[c][stage])

    def receive(c):
        fars[c] = []
        for x in gate(far_half[c], token):
            fars[c] += [x, over_seq(x, 1)]

    def weigh(c):
        nonlocal token
        if c not in fars:
            receive(c)
        keep, send = weight_terms(
            info, outs, near, fars[c], token, shares, c, chunks, width, orders[c]
        )
        token = send
        state[c] = (keep, hop(c, send, 0), 1)

    def advance(c):
        nonlocal token, weight_grad
        if c not in state or state[c] is None:
            return
        keep, got, stage = state[c]
        if stage == len(bits):
            token = weight_grad = finish(keep, got, weight_grad, token, c, chunks, scale)
            state[c] = None
        else:
            keep, send = merge(keep, got, token)
            token = send
            state[c] = (keep, hop(c, send, stage), stage + 1)

    def project_step(picked, last):
        nonlocal token, acc
        token = acc = project(
            out_weight, near, [fars[c] for c in picked], acc, token, orders, picked, shares, width, last
        )

    def send_back(gp):
        nonlocal token
        res = attention_back(info, pieces[gp], acc, outs[gp], fwd[gp][1], token, parts, docs, gp)
        token = results[gp] = res
        back[gp] = {d: over_seq(res[d : d + 2], d) for d in range(2, parts, 2)}

    def hand_over(gp, *tokens):
        got = gate([back[gp][d] for d in range(2, parts, 2)], *tokens)
        mine = [results[gp][1:2]] + [x[1:2] for x in got]
        crossed = over_seq(jnp.concatenate(mine, axis=0), 1)
        out = [results[gp][0], crossed[0]]
        for i, x in enumerate(got):
            out += [x[0], crossed[1 + i]]
        return out

    last = chunks - 1
    for c in range(chunks):
        if c > 1:
            advance(c - 2)
        weigh(c)
        if c == last and c > 1:
            advance(0)
        project_step([c], c == last)
    send_back(0)
    advance(last - 2)
    advance(last - 1)
    for gp in range(1, groups):
        send_back(gp)
    advance(last - 1)
    advance(last - 2)
    advance(last)
    firsts = hand_over(0, token)
    advance(0)
    token = (token, firsts[1])
    advance(last)
    lasts = [hand_over(gp, token) for gp in range(1, groups)]
    for _ in bits:
        for c in range(chunks):
            advance(c)
    back = firsts + [x for group in lasts for x in group]
    grad_q, grad_k, grad_v = unpack(gate([info], token)[0], back, parts, groups)
    return (grad_q[None], grad_k[None], grad_v[None], weight_grad)


def solution(mesh):
    return jax.shard_map(
        body,
        mesh=mesh,
        in_specs=(
            P("dp", "seq", None),
            P("dp", "seq", None),
            P("dp", "seq", None),
            P("dp", "seq", None),
            P("seq", None),
            P("dp", None),
        ),
        out_specs=(
            P("dp", "seq", None),
            P("dp", "seq", None),
            P("dp", "seq", None),
            P("seq", "dp"),
        ),
        check_vma=False,
    )
```

```python
import functools
import math

import jax
import jax.numpy as jnp
from jax import lax
from jax.experimental import pallas as pl
from jax.experimental.pallas import tpu as pltpu
from jax.sharding import PartitionSpec as P

HEADS = 32
KV_HEADS = 8
HEAD_DIM = 128
GROUP = HEADS // KV_HEADS
MASKED = -1e30
NT = (((1,), (1,)), ((), ()))
NN = (((1,), (0,)), ((), ()))


def mm(a, b, dims=NN):
    return lax.dot_general(a, b, dims, preferred_element_type=jnp.float32)


def params(mib):
    return pltpu.CompilerParams(vmem_limit_bytes=mib * 2**20)


def cost(weight):
    return pl.CostEstimate(flops=int(weight * 1e9), bytes_accessed=1024, transcendentals=0)


ANY = pl.BlockSpec(memory_space=pl.ANY)


def shape(dims, dtype=jnp.bfloat16):
    return jax.ShapeDtypeStruct(dims, dtype)


def gate(arrays, *tokens):
    flat = [x for token in tokens for x in (token if isinstance(token, tuple) else (token,))]
    return list(lax.optimization_barrier((*arrays, *flat)))[: len(arrays)]


def pack_kernel(jobs, joined, me_ref, *refs):
    wide = GROUP * HEAD_DIM
    size = wide + 2 * HEAD_DIM
    sources, outs = iter(refs[: len(refs) - len(jobs)]), refs[len(refs) - len(jobs) :]
    if joined:
        outs[1][:, size * len(jobs[1][1]) :] = refs[0][...]
        next(sources)
    for out, (d, members) in zip(outs, jobs):
        for slot in range(len(members)):
            start = slot * size
            for width in (wide, HEAD_DIM, HEAD_DIM):
                out[:, start : start + width] = next(sources)[...]
                start += width


def pack(me, sources, parts, jobs, joined=None):
    rows = sources[0].shape[0]
    groups = KV_HEADS // parts
    wide = GROUP * HEAD_DIM
    size = wide + 2 * HEAD_DIM
    step = min(128, rows)

    def pick(width, d, gp):
        return pl.BlockSpec((step, width), lambda i, me: (i, (me[0] ^ d) * groups + gp))

    specs = [
        pick(width, d, gp)
        for d, members in jobs
        for gp in members
        for width in (wide, HEAD_DIM, HEAD_DIM)
    ]
    more = [] if joined is None else [joined]
    widths = [size * len(members) for d, members in jobs]
    if more:
        widths[1] += joined.shape[1]
    return pl.pallas_call(
        functools.partial(pack_kernel, jobs, bool(more)),
        grid_spec=pltpu.PrefetchScalarGridSpec(
            num_scalar_prefetch=1,
            grid=(rows // step,),
            in_specs=[pl.BlockSpec((step, x.shape[1]), lambda i, me: (i, 0)) for x in more] + specs,
            out_specs=[pl.BlockSpec((step, width), lambda i, me: (i, 0)) for width in widths],
        ),
        out_shape=[shape((rows, width)) for width in widths],
        compiler_params=params(60),
        cost_estimate=cost(0.2),
        name="pack",
    )(me, *more, *sources * (len(specs) // 3))


def column(share, c, chunks, width):
    return slice((share * chunks + c) * width, (share * chunks + c + 1) * width)


def pack_chunks_kernel(orders, shares, width, g_ref, *out_refs):
    for c, order in enumerate(orders):
        for place in range(shares):
            share = unplace(place, order)
            out_refs[c][:, place * width : (place + 1) * width] = g_ref[
                :, column(share, c, len(orders), width)
            ]


def pack_chunks(cotangent, orders, shares, width):
    rows, model = cotangent.shape
    step = min(64, rows)
    return pl.pallas_call(
        functools.partial(pack_chunks_kernel, orders, shares, width),
        grid=(rows // step,),
        in_specs=[pl.BlockSpec((step, model), lambda i: (i, 0))],
        out_specs=[pl.BlockSpec((step, shares * width), lambda i: (i, 0))] * len(orders),
        out_shape=[shape((rows, shares * width)) for order in orders],
        compiler_params=params(60),
        cost_estimate=cost(0.2),
        name="pack_chunks",
    )(cotangent)


def unpack_kernel(parts, groups, info_ref, *refs):
    count = parts * groups
    q_ref, k_ref, v_ref = refs[count:]
    wide = GROUP * HEAD_DIM
    for gp in range(groups):
        for d in range(parts):
            piece = refs[gp * parts + d]
            place = (info_ref[0] ^ d) * groups + gp
            q_ref[:, pl.ds(pl.multiple_of(place * wide, wide), wide)] = piece[:, :wide]
            narrow = pl.ds(pl.multiple_of(place * HEAD_DIM, HEAD_DIM), HEAD_DIM)
            k_ref[:, narrow] = piece[:, wide : wide + HEAD_DIM]
            v_ref[:, narrow] = piece[:, wide + HEAD_DIM :]


def unpack(info, pieces, parts, groups):
    rows, cols = pieces[0].shape
    wide = GROUP * HEAD_DIM
    step = min(64, rows)
    total = parts * groups
    widths = (total * wide, total * HEAD_DIM, total * HEAD_DIM)
    return pl.pallas_call(
        functools.partial(unpack_kernel, parts, groups),
        grid_spec=pltpu.PrefetchScalarGridSpec(
            num_scalar_prefetch=1,
            grid=(rows // step,),
            in_specs=[pl.BlockSpec((step, cols), lambda i, info: (i, 0))] * total,
            out_specs=[pl.BlockSpec((step, w), lambda i, info: (i, 0)) for w in widths],
        ),
        out_shape=[shape((rows, w)) for w in widths],
        compiler_params=params(16),
        cost_estimate=cost(0.2),
        name="unpack",
    )(info, *pieces)


def pair_index(qb, kb):
    return qb * (qb + 1) // 2 + kb


def prepare(parts, block, docs, info_ref, bias_ref, open_ref):
    down = lax.broadcasted_iota(jnp.int32, (block, block), 0)
    across = lax.broadcasted_iota(jnp.int32, (1, block), 1)
    for qb in range(parts):
        lanes = qb * block + across
        opening = jnp.zeros((1, block), jnp.int32)
        first = jnp.int32(0)
        for n in range(docs):
            start = info_ref[2 + n]
            opening = jnp.where(start <= lanes, jnp.maximum(opening, start), opening)
            first = jnp.where(start <= qb * block, jnp.maximum(first, start), first)
        open_ref[qb] = first // block
        for kb in range(qb + 1):
            seen = down >= opening - kb * block
            if kb == qb:
                seen = seen & (down <= across)
            bias_ref[pair_index(qb, kb)] = jnp.where(seen, 0.0, MASKED).astype(jnp.float32)


def flip(x):
    return jnp.transpose(x.astype(jnp.float32))


def head_cols(h):
    return slice(h * HEAD_DIM, (h + 1) * HEAD_DIM)


def over_heads(tile):
    return jnp.concatenate([tile] * GROUP, axis=1)


def forward_kernel(parts, block, docs, info_ref, *refs):
    pieces = refs[:parts]
    out_ref, lse_ref = refs[parts : parts + 2]
    bias_ref, open_ref, q_s, k_s, vt_s, top_s, sum_s, acc_s = refs[parts + 2 :]
    me = info_ref[0]
    wide = GROUP * HEAD_DIM
    factor = math.log2(math.e) / math.sqrt(HEAD_DIM)
    prepare(parts, block, docs, info_ref, bias_ref, open_ref)
    for d in range(parts):
        for h in range(GROUP):
            q_s[me ^ d, h * block : (h + 1) * block] = pieces[d][:, head_cols(h)]
        k_s[me ^ d] = pieces[d][:, wide : wide + HEAD_DIM]
        vt_s[me ^ d] = flip(pieces[d][:, wide + HEAD_DIM :]).astype(jnp.bfloat16)

    def rows_of(qb, carry):
        top_s[...] = jnp.full_like(top_s, 2.0 * MASKED)
        sum_s[...] = jnp.zeros_like(sum_s)
        acc_s[...] = jnp.zeros_like(acc_s)

        def pair(back, carry):
            kb = qb - back
            bias = over_heads(bias_ref[pair_index(qb, kb)])
            raw = mm(k_s[kb], q_s[qb], NT) * factor + bias
            old = top_s[...]
            top = jnp.maximum(old, jnp.max(raw, axis=0, keepdims=True))
            shrink = jnp.exp2(old - top)
            raised = jnp.exp2(raw - top)
            top_s[...] = top
            sum_s[...] = sum_s[...] * shrink + jnp.sum(raised, axis=0, keepdims=True)
            acc_s[...] = acc_s[...] * shrink + mm(vt_s[kb], raised.astype(jnp.bfloat16))
            return carry

        lax.fori_loop(0, qb - open_ref[qb] + 1, pair, 0)
        out = (acc_s[...] / sum_s[...]).astype(jnp.bfloat16)
        spot = me ^ qb
        for h in range(GROUP):
            out_ref[head_cols(h), pl.ds(pl.multiple_of(spot * block, block), block)] = out[
                :, h * block : (h + 1) * block
            ]
        lse_ref[spot] = jnp.broadcast_to(top_s[...] + jnp.log2(sum_s[...]), lse_ref.shape[1:])
        return carry

    lax.fori_loop(0, parts, rows_of, 0)


def whole_block(dims):
    return pl.BlockSpec(dims, lambda i, info: (0,) * len(dims))


def piece_block(rows, cols, at):
    return pl.BlockSpec((rows, cols), lambda i, info: (0, at))


def attention(info, pieces, token, parts, docs):
    block, cols = pieces[-1][0].shape
    pairs = parts * (parts + 1) // 2
    wide = GROUP * HEAD_DIM
    vm = pltpu.VMEM
    return pl.pallas_call(
        functools.partial(forward_kernel, parts, block, docs),
        grid_spec=pltpu.PrefetchScalarGridSpec(
            num_scalar_prefetch=1,
            grid=(1,),
            in_specs=[piece_block(block, cols, at) for x, at in pieces],
            out_specs=[
                whole_block((wide, parts * block)),
                whole_block((parts, 8, GROUP * block)),
            ],
            scratch_shapes=[
                vm((pairs, block, block), jnp.float32),
                pltpu.SMEM((parts,), jnp.int32),
                vm((parts, GROUP * block, HEAD_DIM), jnp.bfloat16),
                vm((parts, block, HEAD_DIM), jnp.bfloat16),
                vm((parts, HEAD_DIM, block), jnp.bfloat16),
                vm((1, GROUP * block), jnp.float32),
                vm((1, GROUP * block), jnp.float32),
                vm((HEAD_DIM, GROUP * block), jnp.float32),
            ],
        ),
        out_shape=[
            shape((wide, parts * block)),
            shape((parts, 8, GROUP * block), jnp.float32),
        ],
        compiler_params=params(60),
        cost_estimate=cost(2.5),
        name="attention",
    )(gate([info], token)[0], *[x for x, at in pieces])


def backward_kernel(parts, block, docs, info_ref, *refs):
    pieces = refs[:parts]
    grad_ref, out_ref, lse_ref = refs[parts : parts + 3]
    res_ref = refs[parts + 3]
    bias_ref, open_ref, q_s, k_s, kt_s, v_s, do_s, dk_s, dv_s, dq_s = refs[parts + 4 :]
    me = info_ref[0]
    wide = GROUP * HEAD_DIM
    scale = 1.0 / math.sqrt(HEAD_DIM)
    factor = math.log2(math.e) * scale
    prepare(parts, block, docs, info_ref, bias_ref, open_ref)
    for d in range(parts):
        for h in range(GROUP):
            q_s[me ^ d, h * block : (h + 1) * block] = pieces[d][:, head_cols(h)]
            do_s[me ^ d, h * block : (h + 1) * block] = grad_ref[d, :, head_cols(h)]
        k_s[me ^ d] = pieces[d][:, wide : wide + HEAD_DIM]
        kt_s[me ^ d] = flip(pieces[d][:, wide : wide + HEAD_DIM]).astype(jnp.bfloat16)
        v_s[me ^ d] = pieces[d][:, wide + HEAD_DIM :]
    dk_s[...] = jnp.zeros_like(dk_s)
    dv_s[...] = jnp.zeros_like(dv_s)

    def rows_of(qb, carry):
        spot = me ^ qb
        dq_s[...] = jnp.zeros_like(dq_s)
        here = pl.ds(pl.multiple_of(spot * block, block), block)
        out = jnp.concatenate([out_ref[head_cols(h), here] for h in range(GROUP)], axis=1)
        delta = jnp.sum(flip(do_s[qb]) * out.astype(jnp.float32), axis=0, keepdims=True)
        lse = lse_ref[spot, :1]

        def pair(back, carry):
            kb = qb - back
            bias = over_heads(bias_ref[pair_index(qb, kb)])
            probs = jnp.exp2(mm(k_s[kb], q_s[qb], NT) * factor + bias - lse)
            dv_s[kb] += mm(probs.astype(jnp.bfloat16), do_s[qb])
            slope = (probs * (mm(v_s[kb], do_s[qb], NT) - delta)).astype(jnp.bfloat16)
            dk_s[kb] += mm(slope, q_s[qb])
            dq_s[...] += mm(kt_s[kb], slope)
            return carry

        lax.fori_loop(0, qb - open_ref[qb] + 1, pair, 0)
        back = (jnp.transpose(dq_s[...]) * scale).astype(jnp.bfloat16)
        for h in range(GROUP):
            res_ref[spot, :, head_cols(h)] = back[h * block : (h + 1) * block]
        return carry

    lax.fori_loop(0, parts, rows_of, 0)
    for kb in range(parts):
        res_ref[me ^ kb, :, wide : wide + HEAD_DIM] = (dk_s[kb] * scale).astype(jnp.bfloat16)
        res_ref[me ^ kb, :, wide + HEAD_DIM :] = dv_s[kb].astype(jnp.bfloat16)


def attention_back(info, pieces, grads, out, lse, token, parts, docs, gp):
    block, cols = pieces[-1][0].shape
    pairs = parts * (parts + 1) // 2
    wide = GROUP * HEAD_DIM
    vm = pltpu.VMEM
    return pl.pallas_call(
        functools.partial(backward_kernel, parts, block, docs),
        grid_spec=pltpu.PrefetchScalarGridSpec(
            num_scalar_prefetch=1,
            grid=(1,),
            in_specs=[piece_block(block, cols, at) for x, at in pieces]
            + [
                pl.BlockSpec((parts, block, wide), lambda i, info: (0, 0, gp)),
                whole_block((wide, parts * block)),
                whole_block((parts, 8, GROUP * block)),
            ],
            out_specs=whole_block((parts, block, cols)),
            scratch_shapes=[
                vm((pairs, block, block), jnp.float32),
                pltpu.SMEM((parts,), jnp.int32),
                vm((parts, GROUP * block, HEAD_DIM), jnp.bfloat16),
                vm((parts, block, HEAD_DIM), jnp.bfloat16),
                vm((parts, HEAD_DIM, block), jnp.bfloat16),
                vm((parts, block, HEAD_DIM), jnp.bfloat16),
                vm((parts, GROUP * block, HEAD_DIM), jnp.bfloat16),
                vm((parts, block, HEAD_DIM), jnp.float32),
                vm((parts, block, HEAD_DIM), jnp.float32),
                vm((HEAD_DIM, GROUP * block), jnp.float32),
            ],
        ),
        out_shape=shape((parts, block, cols)),
        compiler_params=params(32),
        cost_estimate=cost(1.0),
        name="attention_back",
    )(gate([info], token)[0], *[x for x, at in pieces], grads, out, lse)


def place_of(share, order):
    out = 0 * share
    for k, bit in enumerate(order):
        out = out + ((share >> bit) & 1) * (1 << k)
    return out


def unplace(place, order):
    out = 0 * place
    for k, bit in enumerate(order):
        out = out + ((place >> k) & 1) * (1 << bit)
    return out


def reverse_bits(x, bits):
    out = 0 * x
    for b in range(bits):
        out = out + ((x >> b) & 1) * (1 << (bits - 1 - b))
    return out


def weight_kernel(parts, groups, width, order, info_ref, *refs):
    outs, lows, highs = refs[:groups], refs[groups : groups + 2], refs[groups + 2 : groups + 4]
    chunk = refs[groups + 4 : groups + 2 + parts]
    keep_ref, send_ref = refs[groups + 2 + parts :]
    odd = ((info_ref[1] >> order[0]) & 1) == 1
    rows = GROUP * HEAD_DIM
    grads = [jnp.concatenate([lows[d][...], highs[d][...]], axis=1) for d in range(2)]
    grads = jnp.concatenate(grads + [x[...] for x in chunk], axis=0)
    for gp in range(groups):
        total = mm(outs[gp][...], grads)
        low, high = total[:, :width], total[:, width:]
        spot = slice(gp * rows, (gp + 1) * rows)
        keep_ref[0, spot] = jnp.where(odd, high, low)
        send_ref[0, spot] = jnp.where(odd, low, high).astype(jnp.bfloat16)


def weight_terms(info, outs, near, chunk, token, shares, c, chunks, width, order):
    groups, parts = len(outs), 2 + len(chunk)
    rows, block = outs[0].shape[0], near[0].shape[0]
    half = shares // 2
    bits = half.bit_length() - 1
    spot = pl.BlockSpec((1, groups * rows, width), lambda t, info: (reverse_bits(t, bits), 0, 0))

    def mate(t, info):
        return t ^ (place_of(info[1], order) >> 1)

    def original(side, x):
        shift = (x.shape[1] - shares * chunks * width) // width
        return pl.BlockSpec(
            (block, width),
            lambda t, info: (0, shift + unplace(2 * mate(t, info) + side, order) * chunks + c),
        )

    return pl.pallas_call(
        functools.partial(weight_kernel, parts, groups, width, order),
        grid_spec=pltpu.PrefetchScalarGridSpec(
            num_scalar_prefetch=1,
            grid=(half,),
            in_specs=[pl.BlockSpec((rows, parts * block), lambda t, info: (0, 0))] * groups
            + [original(side, x) for side in range(2) for x in near]
            + [pl.BlockSpec((block, 2 * width), lambda t, info: (0, mate(t, info)))] * len(chunk),
            out_specs=[spot, spot],
        ),
        out_shape=[
            shape((half, groups * rows, width), jnp.float32),
            shape((half, groups * rows, width)),
        ],
        compiler_params=params(16),
        cost_estimate=cost(0.2),
        name="weight_terms",
    )(gate([info], token)[0], *outs, *near, *near, *chunk)


def merge_kernel(keep_low, keep_high, got_low, got_high, keep_ref, send_ref):
    keep_ref[...] = keep_low[...] + got_low[...].astype(jnp.float32)
    send_ref[...] = (keep_high[...] + got_high[...].astype(jnp.float32)).astype(jnp.bfloat16)


def merge(keep, got, token):
    count, rows, width = keep.shape
    half = count // 2
    keep = gate([keep], token)[0]
    low = pl.BlockSpec((1, rows, width), lambda t: (t, 0, 0))
    high = pl.BlockSpec((1, rows, width), lambda t: (t + half, 0, 0))
    return pl.pallas_call(
        merge_kernel,
        grid=(half,),
        in_specs=[low, high, low, high],
        out_specs=[low, low],
        out_shape=[
            shape((half, rows, width), jnp.float32),
            shape((half, rows, width)),
        ],
        compiler_params=params(12),
        cost_estimate=cost(0.02),
        name="merge",
    )(keep, keep, got, got)


def finish_kernel(scale, keep_ref, got_ref, *refs):
    refs[-1][...] = (keep_ref[0] + got_ref[0].astype(jnp.float32)) * scale


def finish(keep, got, so_far, token, c, chunks, scale):
    _, rows, width = keep.shape
    more = [] if so_far is None else [so_far]
    step = rows // 2
    spec = pl.BlockSpec((1, step, width), lambda i: (0, i, 0))
    return pl.pallas_call(
        functools.partial(finish_kernel, scale),
        grid=(rows // step,),
        in_specs=[spec, spec] + [ANY] * len(more),
        out_specs=pl.BlockSpec((step, width), lambda i: (i, c)),
        out_shape=shape((rows, width * chunks), jnp.float32),
        input_output_aliases={2: 0} if more else {},
        compiler_params=params(8),
        cost_estimate=cost(0.02),
        name="finish",
    )(gate([keep], token)[0], got, *more)


def shifted(ref, like, columns):
    more = ref.shape[1] - like.shape[1]
    return slice(columns.start + more, columns.stop + more)


def project_kernel(parts, shares, width, chunks, orders, picked, first, last, *refs):
    w_ref, near = refs[0], refs[1:3]
    far = refs[3 : 3 + len(picked) * (parts - 2)]
    acc_ref, out_ref = refs[-2] if not first else None, refs[-1]
    columns = [(c, unplace(p, orders[c])) for c in picked for p in range(shares)]
    weights = jnp.concatenate([w_ref[:, column(j, c, chunks, width)] for c, j in columns], axis=1)
    for d in range(parts):
        if d < 2:
            rows = jnp.concatenate([near[d][:, shifted(near[d], w_ref, column(j, c, chunks, width))] for c, j in columns], axis=1)
        else:
            mine = [far[i * (parts - 2) + d - 2][...] for i in range(len(picked))]
            rows = mine[0] if len(mine) == 1 else jnp.concatenate(mine, axis=1)
        total = mm(rows, weights, NT)
        if not first:
            total += acc_ref[d]
        out_ref[d] = total.astype(out_ref.dtype)


def project(out_weight, near, far, acc, token, orders, picked, shares, width, last):
    feats, model = out_weight.shape
    rows = near[0].shape[0]
    parts = 2 + len(far[0])
    step = min(256, feats)
    flat = [x for group in far for x in group]
    first = acc is None
    block = pl.BlockSpec((parts, rows, step), lambda i: (0, 0, i))
    return pl.pallas_call(
        functools.partial(
            project_kernel, parts, shares, width, len(orders), orders, picked, first, last
        ),
        grid=(feats // step,),
        in_specs=[pl.BlockSpec((step, model), lambda i: (i, 0))]
        + [pl.BlockSpec((rows, x.shape[1]), lambda i: (0, 0)) for x in near]
        + [pl.BlockSpec((rows, shares * width), lambda i: (0, 0))] * len(flat)
        + ([] if first else [block]),
        out_specs=block,
        out_shape=shape((parts, rows, feats), jnp.bfloat16 if last else jnp.float32),
        compiler_params=params(24),
        cost_estimate=cost(0.2),
        name="project",
    )(gate([out_weight], token)[0], *near, *flat, *([] if first else [acc]))


def body(grad_out, queries, keys, values, out_weight, doc_starts):
    parts, shares = lax.axis_size("seq"), lax.axis_size("dp")
    groups = KV_HEADS // parts
    docs = doc_starts.shape[-1]
    cotangent = grad_out[0]
    rows, model = cotangent.shape
    chunks = max(1, min(4, model // shares // 128))
    width = model // shares // chunks
    bits = tuple(range(shares.bit_length() - 1))
    turned = bits[1:] + bits[:1]
    orders = [turned if c == 0 else bits for c in range(chunks)]
    scale = 1.0 / math.sqrt(rows * parts * shares)
    info = jnp.concatenate(
        [
            jnp.stack([lax.axis_index("seq"), lax.axis_index("dp")]).astype(jnp.int32),
            doc_starts[0],
        ]
    )

    def over_seq(x, d):
        return lax.ppermute(x, "seq", [(i, i ^ d) for i in range(parts)])

    def over_dp(x, d):
        return lax.ppermute(x, "dp", [(i, i ^ d) for i in range(shares)])

    far = range(2, parts)
    all_groups = tuple(range(groups))
    me = lax.axis_index("seq").astype(jnp.int32).reshape(1)
    sources = (queries[0], keys[0], values[0])
    packed = [pack(me, sources, parts, tuple((d, (0,)) for d in far))]
    rest = [(d, (gp,)) for gp in range(1, groups) for d in far]
    rest = pack(
        gate([me], packed[0][0])[0],
        sources,
        parts,
        tuple([(0, all_groups), (1, all_groups)] + rest),
    )
    for gp in range(1, groups):
        packed.append(rest[2 + (gp - 1) * len(far) : 2 + gp * len(far)])
    sent_far = [[over_seq(x, d) for x, d in zip(group, far)] for group in packed]
    core = over_seq(rest[1], 1)
    pieces = [[(rest[0], gp), (core, gp)] + [(x, 0) for x in sent_far[gp]] for gp in range(groups)]
    sends = pack_chunks(gate([cotangent], rest[0])[0], orders, shares, width)
    near = [cotangent, over_seq(gate([cotangent], *sent_far[0], sends[-1])[0], 1)]

    far_half = {}

    def send_chunk(c, *tokens):
        mine = gate([sends[c]], *tokens)[0]
        far_half[c] = [over_seq(mine, d) for d in range(2, parts, 2)]

    for c in range(chunks):
        if c < groups:
            send_chunk(c, *sent_far[c], sends[-1])
        else:
            send_chunk(c, *far_half[max(0, c - groups)])

    fwd = []
    token = sends[-1]
    for gp in range(groups):
        fwd.append(attention(info, pieces[gp], token, parts, docs))
        token = fwd[-1][0]
        if gp == 0:
            token = (token, near[1])
    outs = [pair[0] for pair in fwd]

    fars, state, back, results = {}, {}, {}, {}
    acc = weight_grad = None

    def hop(c, send, stage):
        return over_dp(send, 1 << orders[c][stage])

    def receive(c):
        fars[c] = []
        for x in gate(far_half[c], token):
            fars[c] += [x, over_seq(x, 1)]

    def weigh(c):
        nonlocal token
        if c not in fars:
            receive(c)
        keep, send = weight_terms(
            info, outs, near, fars[c], token, shares, c, chunks, width, orders[c]
        )
        token = send
        state[c] = (keep, hop(c, send, 0), 1)

    def advance(c):
        nonlocal token, weight_grad
        if c not in state or state[c] is None:
            return
        keep, got, stage = state[c]
        if stage == len(bits):
            token = weight_grad = finish(keep, got, weight_grad, token, c, chunks, scale)
            state[c] = None
        else:
            keep, send = merge(keep, got, token)
            token = send
            state[c] = (keep, hop(c, send, stage), stage + 1)

    def project_step(picked, last):
        nonlocal token, acc
        token = acc = project(
            out_weight, near, [fars[c] for c in picked], acc, token, orders, picked, shares, width, last
        )

    def send_back(gp):
        nonlocal token
        res = attention_back(info, pieces[gp], acc, outs[gp], fwd[gp][1], token, parts, docs, gp)
        token = results[gp] = res
        back[gp] = {d: over_seq(res[d : d + 2], d) for d in range(2, parts, 2)}

    def hand_over(gp, *tokens):
        got = gate([back[gp][d] for d in range(2, parts, 2)], *tokens)
        mine = [results[gp][1:2]] + [x[1:2] for x in got]
        crossed = over_seq(jnp.concatenate(mine, axis=0), 1)
        out = [results[gp][0], crossed[0]]
        for i, x in enumerate(got):
            out += [x[0], crossed[1 + i]]
        return out

    last = chunks - 1
    for c in range(chunks):
        if c > 1:
            advance(c - 2)
        weigh(c)
        project_step([c], c == last)
    send_back(0)
    for c in range(last):
        advance(c)
    for gp in range(1, groups):
        send_back(gp)
    advance(last - 1)
    advance(last - 2)
    advance(last)
    firsts = hand_over(0, token)
    advance(0)
    advance(last - 1)
    token = (token, firsts[1])
    advance(last)
    lasts = [hand_over(gp, token) for gp in range(1, groups)]
    for _ in bits:
        for c in range(chunks):
            advance(c)
    back = firsts + [x for group in lasts for x in group]
    grad_q, grad_k, grad_v = unpack(gate([info], token)[0], back, parts, groups)
    return (grad_q[None], grad_k[None], grad_v[None], weight_grad)


def solution(mesh):
    return jax.shard_map(
        body,
        mesh=mesh,
        in_specs=(
            P("dp", "seq", None),
            P("dp", "seq", None),
            P("dp", "seq", None),
            P("dp", "seq", None),
            P("seq", None),
            P("dp", None),
        ),
        out_specs=(
            P("dp", "seq", None),
            P("dp", "seq", None),
            P("dp", "seq", None),
            P("seq", "dp"),
        ),
        check_vma=False,
    )
```

```python
import functools
import math

import jax
import jax.numpy as jnp
from jax import lax
from jax.experimental import pallas as pl
from jax.experimental.pallas import tpu as pltpu
from jax.sharding import PartitionSpec as P

HEADS = 32
KV_HEADS = 8
HEAD_DIM = 128
GROUP = HEADS // KV_HEADS
MASKED = -1e30
NT = (((1,), (1,)), ((), ()))
NN = (((1,), (0,)), ((), ()))


def mm(a, b, dims=NN):
    return lax.dot_general(a, b, dims, preferred_element_type=jnp.float32)


def params(mib):
    return pltpu.CompilerParams(vmem_limit_bytes=mib * 2**20)


def cost(weight):
    return pl.CostEstimate(flops=int(weight * 1e9), bytes_accessed=1024, transcendentals=0)


ANY = pl.BlockSpec(memory_space=pl.ANY)


def shape(dims, dtype=jnp.bfloat16):
    return jax.ShapeDtypeStruct(dims, dtype)


def gate(arrays, *tokens):
    flat = [x for token in tokens for x in (token if isinstance(token, tuple) else (token,))]
    return list(lax.optimization_barrier((*arrays, *flat)))[: len(arrays)]


def pack_kernel(jobs, joined, me_ref, *refs):
    wide = GROUP * HEAD_DIM
    size = wide + 2 * HEAD_DIM
    sources, outs = iter(refs[: len(refs) - len(jobs)]), refs[len(refs) - len(jobs) :]
    if joined:
        outs[1][:, size * len(jobs[1][1]) :] = refs[0][...]
        next(sources)
    for out, (d, members) in zip(outs, jobs):
        for slot in range(len(members)):
            start = slot * size
            for width in (wide, HEAD_DIM, HEAD_DIM):
                out[:, start : start + width] = next(sources)[...]
                start += width


def pack(me, sources, parts, jobs, joined=None):
    rows = sources[0].shape[0]
    groups = KV_HEADS // parts
    wide = GROUP * HEAD_DIM
    size = wide + 2 * HEAD_DIM
    step = min(128, rows)

    def pick(width, d, gp):
        return pl.BlockSpec((step, width), lambda i, me: (i, (me[0] ^ d) * groups + gp))

    specs = [
        pick(width, d, gp)
        for d, members in jobs
        for gp in members
        for width in (wide, HEAD_DIM, HEAD_DIM)
    ]
    more = [] if joined is None else [joined]
    widths = [size * len(members) for d, members in jobs]
    if more:
        widths[1] += joined.shape[1]
    return pl.pallas_call(
        functools.partial(pack_kernel, jobs, bool(more)),
        grid_spec=pltpu.PrefetchScalarGridSpec(
            num_scalar_prefetch=1,
            grid=(rows // step,),
            in_specs=[pl.BlockSpec((step, x.shape[1]), lambda i, me: (i, 0)) for x in more] + specs,
            out_specs=[pl.BlockSpec((step, width), lambda i, me: (i, 0)) for width in widths],
        ),
        out_shape=[shape((rows, width)) for width in widths],
        compiler_params=params(60),
        cost_estimate=cost(0.2),
        name="pack",
    )(me, *more, *sources * (len(specs) // 3))


def column(share, c, chunks, width):
    return slice((share * chunks + c) * width, (share * chunks + c + 1) * width)


def pack_chunks_kernel(orders, shares, width, g_ref, *out_refs):
    for c, order in enumerate(orders):
        for place in range(shares):
            share = unplace(place, order)
            out_refs[c][:, place * width : (place + 1) * width] = g_ref[
                :, column(share, c, len(orders), width)
            ]


def pack_chunks(cotangent, orders, shares, width):
    rows, model = cotangent.shape
    step = min(64, rows)
    return pl.pallas_call(
        functools.partial(pack_chunks_kernel, orders, shares, width),
        grid=(rows // step,),
        in_specs=[pl.BlockSpec((step, model), lambda i: (i, 0))],
        out_specs=[pl.BlockSpec((step, shares * width), lambda i: (i, 0))] * len(orders),
        out_shape=[shape((rows, shares * width)) for order in orders],
        compiler_params=params(60),
        cost_estimate=cost(0.2),
        name="pack_chunks",
    )(cotangent)


def unpack_kernel(parts, groups, info_ref, *refs):
    count = parts * groups
    q_ref, k_ref, v_ref = refs[count:]
    wide = GROUP * HEAD_DIM
    for gp in range(groups):
        for d in range(parts):
            piece = refs[gp * parts + d]
            place = (info_ref[0] ^ d) * groups + gp
            q_ref[:, pl.ds(pl.multiple_of(place * wide, wide), wide)] = piece[:, :wide]
            narrow = pl.ds(pl.multiple_of(place * HEAD_DIM, HEAD_DIM), HEAD_DIM)
            k_ref[:, narrow] = piece[:, wide : wide + HEAD_DIM]
            v_ref[:, narrow] = piece[:, wide + HEAD_DIM :]


def unpack(info, pieces, parts, groups):
    rows, cols = pieces[0].shape
    wide = GROUP * HEAD_DIM
    step = min(64, rows)
    total = parts * groups
    widths = (total * wide, total * HEAD_DIM, total * HEAD_DIM)
    return pl.pallas_call(
        functools.partial(unpack_kernel, parts, groups),
        grid_spec=pltpu.PrefetchScalarGridSpec(
            num_scalar_prefetch=1,
            grid=(rows // step,),
            in_specs=[pl.BlockSpec((step, cols), lambda i, info: (i, 0))] * total,
            out_specs=[pl.BlockSpec((step, w), lambda i, info: (i, 0)) for w in widths],
        ),
        out_shape=[shape((rows, w)) for w in widths],
        compiler_params=params(16),
        cost_estimate=cost(0.2),
        name="unpack",
    )(info, *pieces)


def pair_index(qb, kb):
    return qb * (qb + 1) // 2 + kb


def prepare(parts, block, docs, info_ref, bias_ref, open_ref):
    down = lax.broadcasted_iota(jnp.int32, (block, block), 0)
    across = lax.broadcasted_iota(jnp.int32, (1, block), 1)
    for qb in range(parts):
        lanes = qb * block + across
        opening = jnp.zeros((1, block), jnp.int32)
        first = jnp.int32(0)
        for n in range(docs):
            start = info_ref[2 + n]
            opening = jnp.where(start <= lanes, jnp.maximum(opening, start), opening)
            first = jnp.where(start <= qb * block, jnp.maximum(first, start), first)
        open_ref[qb] = first // block
        for kb in range(qb + 1):
            seen = down >= opening - kb * block
            if kb == qb:
                seen = seen & (down <= across)
            bias_ref[pair_index(qb, kb)] = jnp.where(seen, 0.0, MASKED).astype(jnp.float32)


def flip(x):
    return jnp.transpose(x.astype(jnp.float32))


def head_cols(h):
    return slice(h * HEAD_DIM, (h + 1) * HEAD_DIM)


def over_heads(tile):
    return jnp.concatenate([tile] * GROUP, axis=1)


def forward_kernel(parts, block, docs, info_ref, *refs):
    pieces = refs[:parts]
    out_ref, lse_ref = refs[parts : parts + 2]
    bias_ref, open_ref, q_s, k_s, vt_s, top_s, sum_s, acc_s = refs[parts + 2 :]
    me = info_ref[0]
    wide = GROUP * HEAD_DIM
    factor = math.log2(math.e) / math.sqrt(HEAD_DIM)
    prepare(parts, block, docs, info_ref, bias_ref, open_ref)
    for d in range(parts):
        for h in range(GROUP):
            q_s[me ^ d, h * block : (h + 1) * block] = pieces[d][:, head_cols(h)]
        k_s[me ^ d] = pieces[d][:, wide : wide + HEAD_DIM]
        vt_s[me ^ d] = flip(pieces[d][:, wide + HEAD_DIM :]).astype(jnp.bfloat16)

    def rows_of(qb, carry):
        top_s[...] = jnp.full_like(top_s, 2.0 * MASKED)
        sum_s[...] = jnp.zeros_like(sum_s)
        acc_s[...] = jnp.zeros_like(acc_s)

        def pair(back, carry):
            kb = qb - back
            bias = over_heads(bias_ref[pair_index(qb, kb)])
            raw = mm(k_s[kb], q_s[qb], NT) * factor + bias
            old = top_s[...]
            top = jnp.maximum(old, jnp.max(raw, axis=0, keepdims=True))
            shrink = jnp.exp2(old - top)
            raised = jnp.exp2(raw - top)
            top_s[...] = top
            sum_s[...] = sum_s[...] * shrink + jnp.sum(raised, axis=0, keepdims=True)
            acc_s[...] = acc_s[...] * shrink + mm(vt_s[kb], raised.astype(jnp.bfloat16))
            return carry

        lax.fori_loop(0, qb - open_ref[qb] + 1, pair, 0)
        out = (acc_s[...] / sum_s[...]).astype(jnp.bfloat16)
        spot = me ^ qb
        for h in range(GROUP):
            out_ref[head_cols(h), pl.ds(pl.multiple_of(spot * block, block), block)] = out[
                :, h * block : (h + 1) * block
            ]
        lse_ref[spot] = jnp.broadcast_to(top_s[...] + jnp.log2(sum_s[...]), lse_ref.shape[1:])
        return carry

    lax.fori_loop(0, parts, rows_of, 0)


def whole_block(dims):
    return pl.BlockSpec(dims, lambda i, info: (0,) * len(dims))


def piece_block(rows, cols, at):
    return pl.BlockSpec((rows, cols), lambda i, info: (0, at))


def attention(info, pieces, token, parts, docs):
    block, cols = pieces[-1][0].shape
    pairs = parts * (parts + 1) // 2
    wide = GROUP * HEAD_DIM
    vm = pltpu.VMEM
    return pl.pallas_call(
        functools.partial(forward_kernel, parts, block, docs),
        grid_spec=pltpu.PrefetchScalarGridSpec(
            num_scalar_prefetch=1,
            grid=(1,),
            in_specs=[piece_block(block, cols, at) for x, at in pieces],
            out_specs=[
                whole_block((wide, parts * block)),
                whole_block((parts, 8, GROUP * block)),
            ],
            scratch_shapes=[
                vm((pairs, block, block), jnp.float32),
                pltpu.SMEM((parts,), jnp.int32),
                vm((parts, GROUP * block, HEAD_DIM), jnp.bfloat16),
                vm((parts, block, HEAD_DIM), jnp.bfloat16),
                vm((parts, HEAD_DIM, block), jnp.bfloat16),
                vm((1, GROUP * block), jnp.float32),
                vm((1, GROUP * block), jnp.float32),
                vm((HEAD_DIM, GROUP * block), jnp.float32),
            ],
        ),
        out_shape=[
            shape((wide, parts * block)),
            shape((parts, 8, GROUP * block), jnp.float32),
        ],
        compiler_params=params(60),
        cost_estimate=cost(2.5),
        name="attention",
    )(gate([info], token)[0], *[x for x, at in pieces])


def backward_kernel(parts, block, docs, info_ref, *refs):
    pieces = refs[:parts]
    grad_ref, out_ref, lse_ref = refs[parts : parts + 3]
    res_ref = refs[parts + 3]
    bias_ref, open_ref, q_s, k_s, kt_s, v_s, do_s, dk_s, dv_s, dq_s = refs[parts + 4 :]
    me = info_ref[0]
    wide = GROUP * HEAD_DIM
    scale = 1.0 / math.sqrt(HEAD_DIM)
    factor = math.log2(math.e) * scale
    prepare(parts, block, docs, info_ref, bias_ref, open_ref)
    for d in range(parts):
        for h in range(GROUP):
            q_s[me ^ d, h * block : (h + 1) * block] = pieces[d][:, head_cols(h)]
            do_s[me ^ d, h * block : (h + 1) * block] = grad_ref[d, :, head_cols(h)]
        k_s[me ^ d] = pieces[d][:, wide : wide + HEAD_DIM]
        kt_s[me ^ d] = flip(pieces[d][:, wide : wide + HEAD_DIM]).astype(jnp.bfloat16)
        v_s[me ^ d] = pieces[d][:, wide + HEAD_DIM :]
    dk_s[...] = jnp.zeros_like(dk_s)
    dv_s[...] = jnp.zeros_like(dv_s)

    def rows_of(qb, carry):
        spot = me ^ qb
        dq_s[...] = jnp.zeros_like(dq_s)
        here = pl.ds(pl.multiple_of(spot * block, block), block)
        out = jnp.concatenate([out_ref[head_cols(h), here] for h in range(GROUP)], axis=1)
        delta = jnp.sum(flip(do_s[qb]) * out.astype(jnp.float32), axis=0, keepdims=True)
        lse = lse_ref[spot, :1]

        def pair(back, carry):
            kb = qb - back
            bias = over_heads(bias_ref[pair_index(qb, kb)])
            probs = jnp.exp2(mm(k_s[kb], q_s[qb], NT) * factor + bias - lse)
            dv_s[kb] += mm(probs.astype(jnp.bfloat16), do_s[qb])
            slope = (probs * (mm(v_s[kb], do_s[qb], NT) - delta)).astype(jnp.bfloat16)
            dk_s[kb] += mm(slope, q_s[qb])
            dq_s[...] += mm(kt_s[kb], slope)
            return carry

        lax.fori_loop(0, qb - open_ref[qb] + 1, pair, 0)
        back = (jnp.transpose(dq_s[...]) * scale).astype(jnp.bfloat16)
        for h in range(GROUP):
            res_ref[spot, :, head_cols(h)] = back[h * block : (h + 1) * block]
        return carry

    lax.fori_loop(0, parts, rows_of, 0)
    for kb in range(parts):
        res_ref[me ^ kb, :, wide : wide + HEAD_DIM] = (dk_s[kb] * scale).astype(jnp.bfloat16)
        res_ref[me ^ kb, :, wide + HEAD_DIM :] = dv_s[kb].astype(jnp.bfloat16)


def attention_back(info, pieces, grads, out, lse, token, parts, docs, gp):
    block, cols = pieces[-1][0].shape
    pairs = parts * (parts + 1) // 2
    wide = GROUP * HEAD_DIM
    vm = pltpu.VMEM
    return pl.pallas_call(
        functools.partial(backward_kernel, parts, block, docs),
        grid_spec=pltpu.PrefetchScalarGridSpec(
            num_scalar_prefetch=1,
            grid=(1,),
            in_specs=[piece_block(block, cols, at) for x, at in pieces]
            + [
                pl.BlockSpec((parts, block, wide), lambda i, info: (0, 0, gp)),
                whole_block((wide, parts * block)),
                whole_block((parts, 8, GROUP * block)),
            ],
            out_specs=whole_block((parts, block, cols)),
            scratch_shapes=[
                vm((pairs, block, block), jnp.float32),
                pltpu.SMEM((parts,), jnp.int32),
                vm((parts, GROUP * block, HEAD_DIM), jnp.bfloat16),
                vm((parts, block, HEAD_DIM), jnp.bfloat16),
                vm((parts, HEAD_DIM, block), jnp.bfloat16),
                vm((parts, block, HEAD_DIM), jnp.bfloat16),
                vm((parts, GROUP * block, HEAD_DIM), jnp.bfloat16),
                vm((parts, block, HEAD_DIM), jnp.float32),
                vm((parts, block, HEAD_DIM), jnp.float32),
                vm((HEAD_DIM, GROUP * block), jnp.float32),
            ],
        ),
        out_shape=shape((parts, block, cols)),
        compiler_params=params(32),
        cost_estimate=cost(1.0),
        name="attention_back",
    )(gate([info], token)[0], *[x for x, at in pieces], grads, out, lse)


def place_of(share, order):
    out = 0 * share
    for k, bit in enumerate(order):
        out = out + ((share >> bit) & 1) * (1 << k)
    return out


def unplace(place, order):
    out = 0 * place
    for k, bit in enumerate(order):
        out = out + ((place >> k) & 1) * (1 << bit)
    return out


def reverse_bits(x, bits):
    out = 0 * x
    for b in range(bits):
        out = out + ((x >> b) & 1) * (1 << (bits - 1 - b))
    return out


def weight_kernel(parts, groups, width, order, info_ref, *refs):
    outs, lows, highs = refs[:groups], refs[groups : groups + 2], refs[groups + 2 : groups + 4]
    chunk = refs[groups + 4 : groups + 2 + parts]
    keep_ref, send_ref = refs[groups + 2 + parts :]
    odd = ((info_ref[1] >> order[0]) & 1) == 1
    rows = GROUP * HEAD_DIM
    grads = [jnp.concatenate([lows[d][...], highs[d][...]], axis=1) for d in range(2)]
    grads = jnp.concatenate(grads + [x[...] for x in chunk], axis=0)
    for gp in range(groups):
        total = mm(outs[gp][...], grads)
        low, high = total[:, :width], total[:, width:]
        spot = slice(gp * rows, (gp + 1) * rows)
        keep_ref[0, spot] = jnp.where(odd, high, low)
        send_ref[0, spot] = jnp.where(odd, low, high).astype(jnp.bfloat16)


def weight_terms(info, outs, near, chunk, token, shares, c, chunks, width, order):
    groups, parts = len(outs), 2 + len(chunk)
    rows, block = outs[0].shape[0], near[0].shape[0]
    half = shares // 2
    bits = half.bit_length() - 1
    spot = pl.BlockSpec((1, groups * rows, width), lambda t, info: (reverse_bits(t, bits), 0, 0))

    def mate(t, info):
        return t ^ (place_of(info[1], order) >> 1)

    def original(side, x):
        shift = (x.shape[1] - shares * chunks * width) // width
        return pl.BlockSpec(
            (block, width),
            lambda t, info: (0, shift + unplace(2 * mate(t, info) + side, order) * chunks + c),
        )

    return pl.pallas_call(
        functools.partial(weight_kernel, parts, groups, width, order),
        grid_spec=pltpu.PrefetchScalarGridSpec(
            num_scalar_prefetch=1,
            grid=(half,),
            in_specs=[pl.BlockSpec((rows, parts * block), lambda t, info: (0, 0))] * groups
            + [original(side, x) for side in range(2) for x in near]
            + [pl.BlockSpec((block, 2 * width), lambda t, info: (0, mate(t, info)))] * len(chunk),
            out_specs=[spot, spot],
        ),
        out_shape=[
            shape((half, groups * rows, width), jnp.float32),
            shape((half, groups * rows, width)),
        ],
        compiler_params=params(16),
        cost_estimate=cost(0.2),
        name="weight_terms",
    )(gate([info], token)[0], *outs, *near, *near, *chunk)


def merge_kernel(keep_low, keep_high, got_low, got_high, keep_ref, send_ref):
    keep_ref[...] = keep_low[...] + got_low[...].astype(jnp.float32)
    send_ref[...] = (keep_high[...] + got_high[...].astype(jnp.float32)).astype(jnp.bfloat16)


def merge(keep, got, token):
    count, rows, width = keep.shape
    half = count // 2
    keep = gate([keep], token)[0]
    low = pl.BlockSpec((1, rows, width), lambda t: (t, 0, 0))
    high = pl.BlockSpec((1, rows, width), lambda t: (t + half, 0, 0))
    return pl.pallas_call(
        merge_kernel,
        grid=(half,),
        in_specs=[low, high, low, high],
        out_specs=[low, low],
        out_shape=[
            shape((half, rows, width), jnp.float32),
            shape((half, rows, width)),
        ],
        compiler_params=params(12),
        cost_estimate=cost(0.02),
        name="merge",
    )(keep, keep, got, got)


def finish_kernel(scale, keep_ref, got_ref, *refs):
    refs[-1][...] = (keep_ref[0] + got_ref[0].astype(jnp.float32)) * scale


def finish(keep, got, so_far, token, c, chunks, scale):
    _, rows, width = keep.shape
    more = [] if so_far is None else [so_far]
    step = rows // 2
    spec = pl.BlockSpec((1, step, width), lambda i: (0, i, 0))
    return pl.pallas_call(
        functools.partial(finish_kernel, scale),
        grid=(rows // step,),
        in_specs=[spec, spec] + [ANY] * len(more),
        out_specs=pl.BlockSpec((step, width), lambda i: (i, c)),
        out_shape=shape((rows, width * chunks), jnp.float32),
        input_output_aliases={2: 0} if more else {},
        compiler_params=params(8),
        cost_estimate=cost(0.02),
        name="finish",
    )(gate([keep], token)[0], got, *more)


def shifted(ref, like, columns):
    more = ref.shape[1] - like.shape[1]
    return slice(columns.start + more, columns.stop + more)


def project_kernel(parts, shares, width, chunks, orders, picked, first, last, *refs):
    w_ref, near = refs[0], refs[1:3]
    far = refs[3 : 3 + len(picked) * (parts - 2)]
    acc_ref, out_ref = refs[-2] if not first else None, refs[-1]
    columns = [(c, unplace(p, orders[c])) for c in picked for p in range(shares)]
    weights = jnp.concatenate([w_ref[:, column(j, c, chunks, width)] for c, j in columns], axis=1)
    for d in range(parts):
        if d < 2:
            rows = jnp.concatenate([near[d][:, shifted(near[d], w_ref, column(j, c, chunks, width))] for c, j in columns], axis=1)
        else:
            mine = [far[i * (parts - 2) + d - 2][...] for i in range(len(picked))]
            rows = mine[0] if len(mine) == 1 else jnp.concatenate(mine, axis=1)
        total = mm(rows, weights, NT)
        if not first:
            total += acc_ref[d]
        out_ref[d] = total.astype(out_ref.dtype)


def project(out_weight, near, far, acc, token, orders, picked, shares, width, last):
    feats, model = out_weight.shape
    rows = near[0].shape[0]
    parts = 2 + len(far[0])
    step = min(256, feats)
    flat = [x for group in far for x in group]
    first = acc is None
    block = pl.BlockSpec((parts, rows, step), lambda i: (0, 0, i))
    return pl.pallas_call(
        functools.partial(
            project_kernel, parts, shares, width, len(orders), orders, picked, first, last
        ),
        grid=(feats // step,),
        in_specs=[pl.BlockSpec((step, model), lambda i: (i, 0))]
        + [pl.BlockSpec((rows, x.shape[1]), lambda i: (0, 0)) for x in near]
        + [pl.BlockSpec((rows, shares * width), lambda i: (0, 0))] * len(flat)
        + ([] if first else [block]),
        out_specs=block,
        out_shape=shape((parts, rows, feats), jnp.bfloat16 if last else jnp.float32),
        compiler_params=params(54),
        cost_estimate=cost(0.2),
        name="project",
    )(gate([out_weight], token)[0], *near, *flat, *([] if first else [acc]))


def body(grad_out, queries, keys, values, out_weight, doc_starts):
    parts, shares = lax.axis_size("seq"), lax.axis_size("dp")
    groups = KV_HEADS // parts
    docs = doc_starts.shape[-1]
    cotangent = grad_out[0]
    rows, model = cotangent.shape
    chunks = max(1, min(4, model // shares // 128))
    width = model // shares // chunks
    bits = tuple(range(shares.bit_length() - 1))
    orders = [bits] * chunks
    scale = 1.0 / math.sqrt(rows * parts * shares)
    info = jnp.concatenate(
        [
            jnp.stack([lax.axis_index("seq"), lax.axis_index("dp")]).astype(jnp.int32),
            doc_starts[0],
        ]
    )

    def over_seq(x, d):
        return lax.ppermute(x, "seq", [(i, i ^ d) for i in range(parts)])

    def over_dp(x, d):
        return lax.ppermute(x, "dp", [(i, i ^ d) for i in range(shares)])

    far = range(2, parts)
    all_groups = tuple(range(groups))
    me = lax.axis_index("seq").astype(jnp.int32).reshape(1)
    sources = (queries[0], keys[0], values[0])
    packed = [pack(me, sources, parts, tuple((d, (0,)) for d in far))]
    rest = [(d, (gp,)) for gp in range(1, groups) for d in far]
    rest = pack(
        gate([me], packed[0][0])[0],
        sources,
        parts,
        tuple([(0, all_groups), (1, all_groups)] + rest),
    )
    for gp in range(1, groups):
        packed.append(rest[2 + (gp - 1) * len(far) : 2 + gp * len(far)])
    sent_far = [[over_seq(x, d) for x, d in zip(group, far)] for group in packed]
    core = over_seq(rest[1], 1)
    pieces = [[(rest[0], gp), (core, gp)] + [(x, 0) for x in sent_far[gp]] for gp in range(groups)]
    sends = pack_chunks(gate([cotangent], rest[0])[0], orders, shares, width)
    near = [cotangent, over_seq(gate([cotangent], *sent_far[0], sends[-1])[0], 1)]

    far_half = {}

    def send_chunk(c, *tokens):
        mine = gate([sends[c]], *tokens)[0]
        far_half[c] = [over_seq(mine, d) for d in range(2, parts, 2)]

    for c in range(chunks):
        if c < groups:
            send_chunk(c, *sent_far[c], sends[-1])
        else:
            send_chunk(c, *far_half[max(0, c - groups)])

    fwd = []
    token = sends[-1]
    for gp in range(groups):
        fwd.append(attention(info, pieces[gp], token, parts, docs))
        token = fwd[-1][0]
        if gp == 0:
            token = (token, near[1])
    outs = [pair[0] for pair in fwd]

    fars, state, back, results = {}, {}, {}, {}
    acc = weight_grad = None

    def hop(c, send, stage):
        return over_dp(send, 1 << orders[c][stage])

    def receive(c):
        fars[c] = []
        for x in gate(far_half[c], token):
            fars[c] += [x, over_seq(x, 1)]

    def weigh(c):
        nonlocal token
        if c not in fars:
            receive(c)
        keep, send = weight_terms(
            info, outs, near, fars[c], token, shares, c, chunks, width, orders[c]
        )
        token = send
        state[c] = (keep, hop(c, send, 0), 1)

    def advance(c):
        nonlocal token, weight_grad
        if c not in state or state[c] is None:
            return
        keep, got, stage = state[c]
        if stage == len(bits):
            token = weight_grad = finish(keep, got, weight_grad, token, c, chunks, scale)
            state[c] = None
        else:
            keep, send = merge(keep, got, token)
            token = send
            state[c] = (keep, hop(c, send, stage), stage + 1)

    def project_step(picked, last):
        nonlocal token, acc
        token = acc = project(
            out_weight, near, [fars[c] for c in picked], acc, token, orders, picked, shares, width, last
        )

    def send_back(gp):
        nonlocal token
        res = attention_back(info, pieces[gp], acc, outs[gp], fwd[gp][1], token, parts, docs, gp)
        token = results[gp] = res
        back[gp] = {d: over_seq(res[d : d + 2], d) for d in range(2, parts, 2)}

    def hand_over(gp, *tokens):
        got = gate([back[gp][d] for d in range(2, parts, 2)], *tokens)
        mine = [results[gp][1:2]] + [x[1:2] for x in got]
        crossed = over_seq(jnp.concatenate(mine, axis=0), 1)
        out = [results[gp][0], crossed[0]]
        for i, x in enumerate(got):
            out += [x[0], crossed[1 + i]]
        return out

    last = chunks - 1
    for c in range(chunks):
        if c > 1:
            advance(c - 2)
        if c == 3:
            advance(0)
        weigh(c)
        project_step([c], c == last)
    advance(1)
    send_back(0)
    advance(0)
    advance(2)
    for gp in range(1, groups):
        send_back(gp)
    advance(3)
    advance(2)
    advance(1)
    firsts = hand_over(0, token)
    token = (token, firsts[1])
    advance(3)
    advance(2)
    lasts = [hand_over(gp, token) for gp in range(1, groups)]
    for _ in bits:
        for c in range(chunks):
            advance(c)
    back = firsts + [x for group in lasts for x in group]
    grad_q, grad_k, grad_v = unpack(gate([info], token)[0], back, parts, groups)
    return (grad_q[None], grad_k[None], grad_v[None], weight_grad)


def solution(mesh):
    return jax.shard_map(
        body,
        mesh=mesh,
        in_specs=(
            P("dp", "seq", None),
            P("dp", "seq", None),
            P("dp", "seq", None),
            P("dp", "seq", None),
            P("seq", None),
            P("dp", None),
        ),
        out_specs=(
            P("dp", "seq", None),
            P("dp", "seq", None),
            P("dp", "seq", None),
            P("seq", "dp"),
        ),
        check_vma=False,
    )
```

```python
import functools
import math

import jax
import jax.numpy as jnp
from jax import lax
from jax.experimental import pallas as pl
from jax.experimental.pallas import tpu as pltpu
from jax.sharding import PartitionSpec as P

HEADS = 32
KV_HEADS = 8
HEAD_DIM = 128
GROUP = HEADS // KV_HEADS
MASKED = -1e30
NT = (((1,), (1,)), ((), ()))
NN = (((1,), (0,)), ((), ()))


def mm(a, b, dims=NN):
    return lax.dot_general(a, b, dims, preferred_element_type=jnp.float32)


def params(mib):
    return pltpu.CompilerParams(vmem_limit_bytes=mib * 2**20)


def cost(weight):
    return pl.CostEstimate(flops=int(weight * 1e9), bytes_accessed=1024, transcendentals=0)


ANY = pl.BlockSpec(memory_space=pl.ANY)


def shape(dims, dtype=jnp.bfloat16):
    return jax.ShapeDtypeStruct(dims, dtype)


def gate(arrays, *tokens):
    flat = [x for token in tokens for x in (token if isinstance(token, tuple) else (token,))]
    return list(lax.optimization_barrier((*arrays, *flat)))[: len(arrays)]


def pack_kernel(jobs, joined, me_ref, *refs):
    wide = GROUP * HEAD_DIM
    size = wide + 2 * HEAD_DIM
    sources, outs = iter(refs[: len(refs) - len(jobs)]), refs[len(refs) - len(jobs) :]
    if joined:
        outs[1][:, size * len(jobs[1][1]) :] = refs[0][...]
        next(sources)
    for out, (d, members) in zip(outs, jobs):
        for slot in range(len(members)):
            start = slot * size
            for width in (wide, HEAD_DIM, HEAD_DIM):
                out[:, start : start + width] = next(sources)[...]
                start += width


def pack(me, sources, parts, jobs, joined=None):
    rows = sources[0].shape[0]
    groups = KV_HEADS // parts
    wide = GROUP * HEAD_DIM
    size = wide + 2 * HEAD_DIM
    step = min(128, rows)

    def pick(width, d, gp):
        return pl.BlockSpec((step, width), lambda i, me: (i, (me[0] ^ d) * groups + gp))

    specs = [
        pick(width, d, gp)
        for d, members in jobs
        for gp in members
        for width in (wide, HEAD_DIM, HEAD_DIM)
    ]
    more = [] if joined is None else [joined]
    widths = [size * len(members) for d, members in jobs]
    if more:
        widths[1] += joined.shape[1]
    return pl.pallas_call(
        functools.partial(pack_kernel, jobs, bool(more)),
        grid_spec=pltpu.PrefetchScalarGridSpec(
            num_scalar_prefetch=1,
            grid=(rows // step,),
            in_specs=[pl.BlockSpec((step, x.shape[1]), lambda i, me: (i, 0)) for x in more] + specs,
            out_specs=[pl.BlockSpec((step, width), lambda i, me: (i, 0)) for width in widths],
        ),
        out_shape=[shape((rows, width)) for width in widths],
        compiler_params=params(60),
        cost_estimate=cost(0.2),
        name="pack",
    )(me, *more, *sources * (len(specs) // 3))


def column(share, c, chunks, width):
    return slice((share * chunks + c) * width, (share * chunks + c + 1) * width)


def pack_chunks_kernel(orders, shares, width, g_ref, *out_refs):
    for c, order in enumerate(orders):
        for place in range(shares):
            share = unplace(place, order)
            out_refs[c][:, place * width : (place + 1) * width] = g_ref[
                :, column(share, c, len(orders), width)
            ]


def pack_chunks(cotangent, orders, shares, width):
    rows, model = cotangent.shape
    step = min(64, rows)
    return pl.pallas_call(
        functools.partial(pack_chunks_kernel, orders, shares, width),
        grid=(rows // step,),
        in_specs=[pl.BlockSpec((step, model), lambda i: (i, 0))],
        out_specs=[pl.BlockSpec((step, shares * width), lambda i: (i, 0))] * len(orders),
        out_shape=[shape((rows, shares * width)) for order in orders],
        compiler_params=params(60),
        cost_estimate=cost(0.2),
        name="pack_chunks",
    )(cotangent)


def unpack_kernel(parts, groups, info_ref, *refs):
    count = parts * groups
    q_ref, k_ref, v_ref = refs[count:]
    wide = GROUP * HEAD_DIM
    for gp in range(groups):
        for d in range(parts):
            piece = refs[gp * parts + d]
            place = (info_ref[0] ^ d) * groups + gp
            q_ref[:, pl.ds(pl.multiple_of(place * wide, wide), wide)] = piece[:, :wide]
            narrow = pl.ds(pl.multiple_of(place * HEAD_DIM, HEAD_DIM), HEAD_DIM)
            k_ref[:, narrow] = piece[:, wide : wide + HEAD_DIM]
            v_ref[:, narrow] = piece[:, wide + HEAD_DIM :]


def unpack(info, pieces, parts, groups):
    rows, cols = pieces[0].shape
    wide = GROUP * HEAD_DIM
    step = min(64, rows)
    total = parts * groups
    widths = (total * wide, total * HEAD_DIM, total * HEAD_DIM)
    return pl.pallas_call(
        functools.partial(unpack_kernel, parts, groups),
        grid_spec=pltpu.PrefetchScalarGridSpec(
            num_scalar_prefetch=1,
            grid=(rows // step,),
            in_specs=[pl.BlockSpec((step, cols), lambda i, info: (i, 0))] * total,
            out_specs=[pl.BlockSpec((step, w), lambda i, info: (i, 0)) for w in widths],
        ),
        out_shape=[shape((rows, w)) for w in widths],
        compiler_params=params(16),
        cost_estimate=cost(0.2),
        name="unpack",
    )(info, *pieces)


def pair_index(qb, kb):
    return qb * (qb + 1) // 2 + kb


def prepare(parts, block, docs, info_ref, bias_ref, open_ref):
    down = lax.broadcasted_iota(jnp.int32, (block, block), 0)
    across = lax.broadcasted_iota(jnp.int32, (1, block), 1)
    for qb in range(parts):
        lanes = qb * block + across
        opening = jnp.zeros((1, block), jnp.int32)
        first = jnp.int32(0)
        for n in range(docs):
            start = info_ref[2 + n]
            opening = jnp.where(start <= lanes, jnp.maximum(opening, start), opening)
            first = jnp.where(start <= qb * block, jnp.maximum(first, start), first)
        open_ref[qb] = first // block
        for kb in range(qb + 1):
            seen = down >= opening - kb * block
            if kb == qb:
                seen = seen & (down <= across)
            bias_ref[pair_index(qb, kb)] = jnp.where(seen, 0.0, MASKED).astype(jnp.float32)


def flip(x):
    return jnp.transpose(x.astype(jnp.float32))


def head_cols(h):
    return slice(h * HEAD_DIM, (h + 1) * HEAD_DIM)


def over_heads(tile):
    return jnp.concatenate([tile] * GROUP, axis=1)


def forward_kernel(parts, block, docs, info_ref, *refs):
    pieces = refs[:parts]
    out_ref, lse_ref = refs[parts : parts + 2]
    bias_ref, open_ref, q_s, k_s, vt_s, top_s, sum_s, acc_s = refs[parts + 2 :]
    me = info_ref[0]
    wide = GROUP * HEAD_DIM
    factor = math.log2(math.e) / math.sqrt(HEAD_DIM)
    prepare(parts, block, docs, info_ref, bias_ref, open_ref)
    for d in range(parts):
        for h in range(GROUP):
            q_s[me ^ d, h * block : (h + 1) * block] = pieces[d][:, head_cols(h)]
        k_s[me ^ d] = pieces[d][:, wide : wide + HEAD_DIM]
        vt_s[me ^ d] = flip(pieces[d][:, wide + HEAD_DIM :]).astype(jnp.bfloat16)

    def rows_of(qb, carry):
        top_s[...] = jnp.full_like(top_s, 2.0 * MASKED)
        sum_s[...] = jnp.zeros_like(sum_s)
        acc_s[...] = jnp.zeros_like(acc_s)

        def pair(back, carry):
            kb = qb - back
            bias = over_heads(bias_ref[pair_index(qb, kb)])
            raw = mm(k_s[kb], q_s[qb], NT) * factor + bias
            old = top_s[...]
            top = jnp.maximum(old, jnp.max(raw, axis=0, keepdims=True))
            shrink = jnp.exp2(old - top)
            raised = jnp.exp2(raw - top)
            top_s[...] = top
            sum_s[...] = sum_s[...] * shrink + jnp.sum(raised, axis=0, keepdims=True)
            acc_s[...] = acc_s[...] * shrink + mm(vt_s[kb], raised.astype(jnp.bfloat16))
            return carry

        lax.fori_loop(0, qb - open_ref[qb] + 1, pair, 0)
        out = (acc_s[...] / sum_s[...]).astype(jnp.bfloat16)
        spot = me ^ qb
        for h in range(GROUP):
            out_ref[head_cols(h), pl.ds(pl.multiple_of(spot * block, block), block)] = out[
                :, h * block : (h + 1) * block
            ]
        lse_ref[spot] = jnp.broadcast_to(top_s[...] + jnp.log2(sum_s[...]), lse_ref.shape[1:])
        return carry

    lax.fori_loop(0, parts, rows_of, 0)


def whole_block(dims):
    return pl.BlockSpec(dims, lambda i, info: (0,) * len(dims))


def piece_block(rows, cols, at):
    return pl.BlockSpec((rows, cols), lambda i, info: (0, at))


def attention(info, pieces, token, parts, docs):
    block, cols = pieces[-1][0].shape
    pairs = parts * (parts + 1) // 2
    wide = GROUP * HEAD_DIM
    vm = pltpu.VMEM
    return pl.pallas_call(
        functools.partial(forward_kernel, parts, block, docs),
        grid_spec=pltpu.PrefetchScalarGridSpec(
            num_scalar_prefetch=1,
            grid=(1,),
            in_specs=[piece_block(block, cols, at) for x, at in pieces],
            out_specs=[
                whole_block((wide, parts * block)),
                whole_block((parts, 8, GROUP * block)),
            ],
            scratch_shapes=[
                vm((pairs, block, block), jnp.float32),
                pltpu.SMEM((parts,), jnp.int32),
                vm((parts, GROUP * block, HEAD_DIM), jnp.bfloat16),
                vm((parts, block, HEAD_DIM), jnp.bfloat16),
                vm((parts, HEAD_DIM, block), jnp.bfloat16),
                vm((1, GROUP * block), jnp.float32),
                vm((1, GROUP * block), jnp.float32),
                vm((HEAD_DIM, GROUP * block), jnp.float32),
            ],
        ),
        out_shape=[
            shape((wide, parts * block)),
            shape((parts, 8, GROUP * block), jnp.float32),
        ],
        compiler_params=params(24),
        cost_estimate=cost(2.5),
        name="attention",
    )(gate([info], token)[0], *[x for x, at in pieces])


def backward_kernel(parts, block, docs, info_ref, *refs):
    pieces = refs[:parts]
    grad_ref, out_ref, lse_ref = refs[parts : parts + 3]
    res_ref = refs[parts + 3]
    bias_ref, open_ref, q_s, k_s, kt_s, v_s, do_s, dk_s, dv_s, dq_s = refs[parts + 4 :]
    me = info_ref[0]
    wide = GROUP * HEAD_DIM
    scale = 1.0 / math.sqrt(HEAD_DIM)
    factor = math.log2(math.e) * scale
    prepare(parts, block, docs, info_ref, bias_ref, open_ref)
    for d in range(parts):
        for h in range(GROUP):
            q_s[me ^ d, h * block : (h + 1) * block] = pieces[d][:, head_cols(h)]
            do_s[me ^ d, h * block : (h + 1) * block] = grad_ref[d, :, head_cols(h)]
        k_s[me ^ d] = pieces[d][:, wide : wide + HEAD_DIM]
        kt_s[me ^ d] = flip(pieces[d][:, wide : wide + HEAD_DIM]).astype(jnp.bfloat16)
        v_s[me ^ d] = pieces[d][:, wide + HEAD_DIM :]
    dk_s[...] = jnp.zeros_like(dk_s)
    dv_s[...] = jnp.zeros_like(dv_s)

    def rows_of(qb, carry):
        spot = me ^ qb
        dq_s[...] = jnp.zeros_like(dq_s)
        here = pl.ds(pl.multiple_of(spot * block, block), block)
        out = jnp.concatenate([out_ref[head_cols(h), here] for h in range(GROUP)], axis=1)
        delta = jnp.sum(flip(do_s[qb]) * out.astype(jnp.float32), axis=0, keepdims=True)
        lse = lse_ref[spot, :1]

        def pair(back, carry):
            kb = qb - back
            bias = over_heads(bias_ref[pair_index(qb, kb)])
            probs = jnp.exp2(mm(k_s[kb], q_s[qb], NT) * factor + bias - lse)
            dv_s[kb] += mm(probs.astype(jnp.bfloat16), do_s[qb])
            slope = (probs * (mm(v_s[kb], do_s[qb], NT) - delta)).astype(jnp.bfloat16)
            dk_s[kb] += mm(slope, q_s[qb])
            dq_s[...] += mm(kt_s[kb], slope)
            return carry

        lax.fori_loop(0, qb - open_ref[qb] + 1, pair, 0)
        back = (jnp.transpose(dq_s[...]) * scale).astype(jnp.bfloat16)
        for h in range(GROUP):
            res_ref[spot, :, head_cols(h)] = back[h * block : (h + 1) * block]
        return carry

    lax.fori_loop(0, parts, rows_of, 0)
    for kb in range(parts):
        res_ref[me ^ kb, :, wide : wide + HEAD_DIM] = (dk_s[kb] * scale).astype(jnp.bfloat16)
        res_ref[me ^ kb, :, wide + HEAD_DIM :] = dv_s[kb].astype(jnp.bfloat16)


def attention_back(info, pieces, grads, out, lse, token, parts, docs, gp):
    block, cols = pieces[-1][0].shape
    pairs = parts * (parts + 1) // 2
    wide = GROUP * HEAD_DIM
    vm = pltpu.VMEM
    return pl.pallas_call(
        functools.partial(backward_kernel, parts, block, docs),
        grid_spec=pltpu.PrefetchScalarGridSpec(
            num_scalar_prefetch=1,
            grid=(1,),
            in_specs=[piece_block(block, cols, at) for x, at in pieces]
            + [
                pl.BlockSpec((parts, block, wide), lambda i, info: (0, 0, gp)),
                whole_block((wide, parts * block)),
                whole_block((parts, 8, GROUP * block)),
            ],
            out_specs=whole_block((parts, block, cols)),
            scratch_shapes=[
                vm((pairs, block, block), jnp.float32),
                pltpu.SMEM((parts,), jnp.int32),
                vm((parts, GROUP * block, HEAD_DIM), jnp.bfloat16),
                vm((parts, block, HEAD_DIM), jnp.bfloat16),
                vm((parts, HEAD_DIM, block), jnp.bfloat16),
                vm((parts, block, HEAD_DIM), jnp.bfloat16),
                vm((parts, GROUP * block, HEAD_DIM), jnp.bfloat16),
                vm((parts, block, HEAD_DIM), jnp.float32),
                vm((parts, block, HEAD_DIM), jnp.float32),
                vm((HEAD_DIM, GROUP * block), jnp.float32),
            ],
        ),
        out_shape=shape((parts, block, cols)),
        compiler_params=params(32),
        cost_estimate=cost(0.3),
        name="attention_back",
    )(gate([info], token)[0], *[x for x, at in pieces], grads, out, lse)


def place_of(share, order):
    out = 0 * share
    for k, bit in enumerate(order):
        out = out + ((share >> bit) & 1) * (1 << k)
    return out


def unplace(place, order):
    out = 0 * place
    for k, bit in enumerate(order):
        out = out + ((place >> k) & 1) * (1 << bit)
    return out


def reverse_bits(x, bits):
    out = 0 * x
    for b in range(bits):
        out = out + ((x >> b) & 1) * (1 << (bits - 1 - b))
    return out


def weight_kernel(parts, groups, width, order, info_ref, *refs):
    outs, lows, highs = refs[:groups], refs[groups : groups + 2], refs[groups + 2 : groups + 4]
    chunk = refs[groups + 4 : groups + 2 + parts]
    keep_ref, send_ref = refs[groups + 2 + parts :]
    odd = ((info_ref[1] >> order[0]) & 1) == 1
    rows = GROUP * HEAD_DIM
    grads = [jnp.concatenate([lows[d][...], highs[d][...]], axis=1) for d in range(2)]
    grads = jnp.concatenate(grads + [x[...] for x in chunk], axis=0)
    for gp in range(groups):
        total = mm(outs[gp][...], grads)
        low, high = total[:, :width], total[:, width:]
        spot = slice(gp * rows, (gp + 1) * rows)
        keep_ref[0, spot] = jnp.where(odd, high, low)
        send_ref[0, spot] = jnp.where(odd, low, high).astype(jnp.bfloat16)


def weight_terms(info, outs, near, chunk, token, shares, c, chunks, width, order):
    groups, parts = len(outs), 2 + len(chunk)
    rows, block = outs[0].shape[0], near[0].shape[0]
    half = shares // 2
    bits = half.bit_length() - 1
    spot = pl.BlockSpec((1, groups * rows, width), lambda t, info: (reverse_bits(t, bits), 0, 0))

    def mate(t, info):
        return t ^ (place_of(info[1], order) >> 1)

    def original(side, x):
        shift = (x.shape[1] - shares * chunks * width) // width
        return pl.BlockSpec(
            (block, width),
            lambda t, info: (0, shift + unplace(2 * mate(t, info) + side, order) * chunks + c),
        )

    return pl.pallas_call(
        functools.partial(weight_kernel, parts, groups, width, order),
        grid_spec=pltpu.PrefetchScalarGridSpec(
            num_scalar_prefetch=1,
            grid=(half,),
            in_specs=[pl.BlockSpec((rows, parts * block), lambda t, info: (0, 0))] * groups
            + [original(side, x) for side in range(2) for x in near]
            + [pl.BlockSpec((block, 2 * width), lambda t, info: (0, mate(t, info)))] * len(chunk),
            out_specs=[spot, spot],
        ),
        out_shape=[
            shape((half, groups * rows, width), jnp.float32),
            shape((half, groups * rows, width)),
        ],
        compiler_params=params(16),
        cost_estimate=cost(0.2),
        name="weight_terms",
    )(gate([info], token)[0], *outs, *near, *near, *chunk)


def merge_kernel(keep_low, keep_high, got_low, got_high, keep_ref, send_ref):
    keep_ref[...] = keep_low[...] + got_low[...].astype(jnp.float32)
    send_ref[...] = (keep_high[...] + got_high[...].astype(jnp.float32)).astype(jnp.bfloat16)


def merge(keep, got, token):
    count, rows, width = keep.shape
    half = count // 2
    keep = gate([keep], token)[0]
    low = pl.BlockSpec((1, rows, width), lambda t: (t, 0, 0))
    high = pl.BlockSpec((1, rows, width), lambda t: (t + half, 0, 0))
    return pl.pallas_call(
        merge_kernel,
        grid=(half,),
        in_specs=[low, high, low, high],
        out_specs=[low, low],
        out_shape=[
            shape((half, rows, width), jnp.float32),
            shape((half, rows, width)),
        ],
        compiler_params=params(12),
        cost_estimate=cost(0.02),
        name="merge",
    )(keep, keep, got, got)


def finish_kernel(scale, keep_ref, got_ref, *refs):
    refs[-1][...] = (keep_ref[0] + got_ref[0].astype(jnp.float32)) * scale


def finish(keep, got, so_far, token, c, chunks, scale):
    _, rows, width = keep.shape
    more = [] if so_far is None else [so_far]
    step = rows // 2
    spec = pl.BlockSpec((1, step, width), lambda i: (0, i, 0))
    return pl.pallas_call(
        functools.partial(finish_kernel, scale),
        grid=(rows // step,),
        in_specs=[spec, spec] + [ANY] * len(more),
        out_specs=pl.BlockSpec((step, width), lambda i: (i, c)),
        out_shape=shape((rows, width * chunks), jnp.float32),
        input_output_aliases={2: 0} if more else {},
        compiler_params=params(8),
        cost_estimate=cost(0.02),
        name="finish",
    )(gate([keep], token)[0], got, *more)


def shifted(ref, like, columns):
    more = ref.shape[1] - like.shape[1]
    return slice(columns.start + more, columns.stop + more)


def project_kernel(parts, shares, width, chunks, orders, picked, first, last, *refs):
    w_ref, near = refs[0], refs[1:3]
    far = refs[3 : 3 + len(picked) * (parts - 2)]
    acc_ref, out_ref = refs[-2] if not first else None, refs[-1]
    columns = [(c, unplace(p, orders[c])) for c in picked for p in range(shares)]
    weights = jnp.concatenate([w_ref[:, column(j, c, chunks, width)] for c, j in columns], axis=1)
    for d in range(parts):
        if d < 2:
            rows = jnp.concatenate([near[d][:, shifted(near[d], w_ref, column(j, c, chunks, width))] for c, j in columns], axis=1)
        else:
            mine = [far[i * (parts - 2) + d - 2][...] for i in range(len(picked))]
            rows = mine[0] if len(mine) == 1 else jnp.concatenate(mine, axis=1)
        total = mm(rows, weights, NT)
        if not first:
            total += acc_ref[d]
        out_ref[d] = total.astype(out_ref.dtype)


def project(out_weight, near, far, acc, token, orders, picked, shares, width, last):
    feats, model = out_weight.shape
    rows = near[0].shape[0]
    parts = 2 + len(far[0])
    step = min(256, feats)
    flat = [x for group in far for x in group]
    first = acc is None
    block = pl.BlockSpec((parts, rows, step), lambda i: (0, 0, i))
    return pl.pallas_call(
        functools.partial(
            project_kernel, parts, shares, width, len(orders), orders, picked, first, last
        ),
        grid=(feats // step,),
        in_specs=[pl.BlockSpec((step, model), lambda i: (i, 0))]
        + [pl.BlockSpec((rows, x.shape[1]), lambda i: (0, 0)) for x in near]
        + [pl.BlockSpec((rows, shares * width), lambda i: (0, 0))] * len(flat)
        + ([] if first else [block]),
        out_specs=block,
        out_shape=shape((parts, rows, feats), jnp.bfloat16 if last else jnp.float32),
        compiler_params=params(24),
        cost_estimate=cost(0.2),
        name="project",
    )(gate([out_weight], token)[0], *near, *flat, *([] if first else [acc]))


def body(grad_out, queries, keys, values, out_weight, doc_starts):
    parts, shares = lax.axis_size("seq"), lax.axis_size("dp")
    groups = KV_HEADS // parts
    docs = doc_starts.shape[-1]
    cotangent = grad_out[0]
    rows, model = cotangent.shape
    chunks = max(1, min(4, model // shares // 128))
    width = model // shares // chunks
    bits = tuple(range(shares.bit_length() - 1))
    orders = [bits] * chunks
    scale = 1.0 / math.sqrt(rows * parts * shares)
    info = jnp.concatenate(
        [
            jnp.stack([lax.axis_index("seq"), lax.axis_index("dp")]).astype(jnp.int32),
            doc_starts[0],
        ]
    )

    def over_seq(x, d):
        return lax.ppermute(x, "seq", [(i, i ^ d) for i in range(parts)])

    def over_dp(x, d):
        return lax.ppermute(x, "dp", [(i, i ^ d) for i in range(shares)])

    far = range(2, parts)
    all_groups = tuple(range(groups))
    me = lax.axis_index("seq").astype(jnp.int32).reshape(1)
    sources = (queries[0], keys[0], values[0])
    packed = [pack(me, sources, parts, tuple((d, (0,)) for d in far))]
    rest = [(d, (gp,)) for gp in range(1, groups) for d in far]
    rest = pack(
        gate([me], packed[0][0])[0],
        sources,
        parts,
        tuple([(0, all_groups), (1, all_groups)] + rest),
    )
    for gp in range(1, groups):
        packed.append(rest[2 + (gp - 1) * len(far) : 2 + gp * len(far)])
    sent_far = [[over_seq(x, d) for x, d in zip(group, far)] for group in packed]
    core = over_seq(rest[1], 1)
    pieces = [[(rest[0], gp), (core, gp)] + [(x, 0) for x in sent_far[gp]] for gp in range(groups)]
    sends = pack_chunks(gate([cotangent], rest[0])[0], orders, shares, width)
    near = [cotangent, over_seq(gate([cotangent], *sent_far[0], sends[-1])[0], 1)]

    far_half = {}

    def send_chunk(c, *tokens):
        mine = gate([sends[c]], *tokens)[0]
        far_half[c] = [over_seq(mine, d) for d in range(2, parts, 2)]

    for c in range(chunks):
        if c < groups:
            send_chunk(c, *sent_far[c], sends[-1])
        else:
            send_chunk(c, *far_half[max(0, c - groups)])

    fwd = []
    token = sends[-1]
    for gp in range(groups):
        fwd.append(attention(info, pieces[gp], token, parts, docs))
        token = fwd[-1][0]
        if gp == 0:
            token = (token, near[1])
    outs = [pair[0] for pair in fwd]

    fars, state, back, results = {}, {}, {}, {}
    acc = weight_grad = None

    def hop(c, send, stage):
        return over_dp(send, 1 << orders[c][stage])

    def receive(c):
        fars[c] = []
        for x in gate(far_half[c], token):
            fars[c] += [x, over_seq(x, 1)]

    def weigh(c):
        nonlocal token
        if c not in fars:
            receive(c)
        keep, send = weight_terms(
            info, outs, near, fars[c], token, shares, c, chunks, width, orders[c]
        )
        token = send
        state[c] = (keep, hop(c, send, 0), 1)

    def advance(c):
        nonlocal token, weight_grad
        if c not in state or state[c] is None:
            return
        keep, got, stage = state[c]
        if stage == len(bits):
            token = weight_grad = finish(keep, got, weight_grad, token, c, chunks, scale)
            state[c] = None
        else:
            keep, send = merge(keep, got, token)
            token = send
            state[c] = (keep, hop(c, send, stage), stage + 1)

    def project_step(picked, last):
        nonlocal token, acc
        token = acc = project(
            out_weight, near, [fars[c] for c in picked], acc, token, orders, picked, shares, width, last
        )

    def send_back(gp):
        nonlocal token
        res = attention_back(info, pieces[gp], acc, outs[gp], fwd[gp][1], token, parts, docs, gp)
        token = results[gp] = res
        back[gp] = {d: over_seq(res[d : d + 2], d) for d in range(2, parts, 2)}

    def hand_over(gp, *tokens):
        got = gate([back[gp][d] for d in range(2, parts, 2)], *tokens)
        mine = [results[gp][1:2]] + [x[1:2] for x in got]
        crossed = over_seq(jnp.concatenate(mine, axis=0), 1)
        out = [results[gp][0], crossed[0]]
        for i, x in enumerate(got):
            out += [x[0], crossed[1 + i]]
        return out

    last = chunks - 1
    for c in range(chunks):
        if c > 1:
            advance(c - 2)
        if c == 3:
            advance(0)
        weigh(c)
        project_step([c], c == last)
    advance(1)
    advance(2)
    advance(0)
    send_back(0)
    for gp in range(1, groups):
        send_back(gp)
    advance(1)
    advance(3)
    advance(2)
    firsts = hand_over(0, token)
    token = (token, firsts[1])
    advance(3)
    lasts = [hand_over(gp, token) for gp in range(1, groups)]
    for _ in bits:
        for c in range(chunks):
            advance(c)
    back = firsts + [x for group in lasts for x in group]
    grad_q, grad_k, grad_v = unpack(gate([info], token)[0], back, parts, groups)
    return (grad_q[None], grad_k[None], grad_v[None], weight_grad)


def solution(mesh):
    return jax.shard_map(
        body,
        mesh=mesh,
        in_specs=(
            P("dp", "seq", None),
            P("dp", "seq", None),
            P("dp", "seq", None),
            P("dp", "seq", None),
            P("seq", None),
            P("dp", None),
        ),
        out_specs=(
            P("dp", "seq", None),
            P("dp", "seq", None),
            P("dp", "seq", None),
            P("seq", "dp"),
        ),
        check_vma=False,
    )
```

```python
import functools
import math

import jax
import jax.numpy as jnp
from jax import lax
from jax.experimental import pallas as pl
from jax.experimental.pallas import tpu as pltpu
from jax.sharding import PartitionSpec as P

HEADS = 32
KV_HEADS = 8
HEAD_DIM = 128
GROUP = HEADS // KV_HEADS
MASKED = -1e30
NT = (((1,), (1,)), ((), ()))
NN = (((1,), (0,)), ((), ()))


def mm(a, b, dims=NN):
    return lax.dot_general(a, b, dims, preferred_element_type=jnp.float32)


def params(mib):
    return pltpu.CompilerParams(vmem_limit_bytes=mib * 2**20)


def cost(weight):
    return pl.CostEstimate(flops=int(weight * 1e9), bytes_accessed=1024, transcendentals=0)


ANY = pl.BlockSpec(memory_space=pl.ANY)


def shape(dims, dtype=jnp.bfloat16):
    return jax.ShapeDtypeStruct(dims, dtype)


def gate(arrays, *tokens):
    flat = [x for token in tokens for x in (token if isinstance(token, tuple) else (token,))]
    return list(lax.optimization_barrier((*arrays, *flat)))[: len(arrays)]


def pack_kernel(jobs, joined, me_ref, *refs):
    wide = GROUP * HEAD_DIM
    size = wide + 2 * HEAD_DIM
    sources, outs = iter(refs[: len(refs) - len(jobs)]), refs[len(refs) - len(jobs) :]
    if joined:
        outs[1][:, size * len(jobs[1][1]) :] = refs[0][...]
        next(sources)
    for out, (d, members) in zip(outs, jobs):
        for slot in range(len(members)):
            start = slot * size
            for width in (wide, HEAD_DIM, HEAD_DIM):
                out[:, start : start + width] = next(sources)[...]
                start += width


def pack(me, sources, parts, jobs, joined=None):
    rows = sources[0].shape[0]
    groups = KV_HEADS // parts
    wide = GROUP * HEAD_DIM
    size = wide + 2 * HEAD_DIM
    step = min(128, rows)

    def pick(width, d, gp):
        return pl.BlockSpec((step, width), lambda i, me: (i, (me[0] ^ d) * groups + gp))

    specs = [
        pick(width, d, gp)
        for d, members in jobs
        for gp in members
        for width in (wide, HEAD_DIM, HEAD_DIM)
    ]
    more = [] if joined is None else [joined]
    widths = [size * len(members) for d, members in jobs]
    if more:
        widths[1] += joined.shape[1]
    return pl.pallas_call(
        functools.partial(pack_kernel, jobs, bool(more)),
        grid_spec=pltpu.PrefetchScalarGridSpec(
            num_scalar_prefetch=1,
            grid=(rows // step,),
            in_specs=[pl.BlockSpec((step, x.shape[1]), lambda i, me: (i, 0)) for x in more] + specs,
            out_specs=[pl.BlockSpec((step, width), lambda i, me: (i, 0)) for width in widths],
        ),
        out_shape=[shape((rows, width)) for width in widths],
        compiler_params=params(60),
        cost_estimate=cost(0.2),
        name="pack",
    )(me, *more, *sources * (len(specs) // 3))


def column(share, c, chunks, width):
    return slice((share * chunks + c) * width, (share * chunks + c + 1) * width)


def pack_chunks_kernel(orders, shares, width, g_ref, *out_refs):
    for c, order in enumerate(orders):
        for place in range(shares):
            share = unplace(place, order)
            out_refs[c][:, place * width : (place + 1) * width] = g_ref[
                :, column(share, c, len(orders), width)
            ]


def pack_chunks(cotangent, orders, shares, width):
    rows, model = cotangent.shape
    step = min(64, rows)
    return pl.pallas_call(
        functools.partial(pack_chunks_kernel, orders, shares, width),
        grid=(rows // step,),
        in_specs=[pl.BlockSpec((step, model), lambda i: (i, 0))],
        out_specs=[pl.BlockSpec((step, shares * width), lambda i: (i, 0))] * len(orders),
        out_shape=[shape((rows, shares * width)) for order in orders],
        compiler_params=params(60),
        cost_estimate=cost(0.2),
        name="pack_chunks",
    )(cotangent)


def unpack_kernel(parts, groups, info_ref, *refs):
    count = parts * groups
    q_ref, k_ref, v_ref = refs[count:]
    wide = GROUP * HEAD_DIM
    for gp in range(groups):
        for d in range(parts):
            piece = refs[gp * parts + d]
            place = (info_ref[0] ^ d) * groups + gp
            q_ref[:, pl.ds(pl.multiple_of(place * wide, wide), wide)] = piece[:, :wide]
            narrow = pl.ds(pl.multiple_of(place * HEAD_DIM, HEAD_DIM), HEAD_DIM)
            k_ref[:, narrow] = piece[:, wide : wide + HEAD_DIM]
            v_ref[:, narrow] = piece[:, wide + HEAD_DIM :]


def unpack(info, pieces, parts, groups):
    rows, cols = pieces[0].shape
    wide = GROUP * HEAD_DIM
    step = min(64, rows)
    total = parts * groups
    widths = (total * wide, total * HEAD_DIM, total * HEAD_DIM)
    return pl.pallas_call(
        functools.partial(unpack_kernel, parts, groups),
        grid_spec=pltpu.PrefetchScalarGridSpec(
            num_scalar_prefetch=1,
            grid=(rows // step,),
            in_specs=[pl.BlockSpec((step, cols), lambda i, info: (i, 0))] * total,
            out_specs=[pl.BlockSpec((step, w), lambda i, info: (i, 0)) for w in widths],
        ),
        out_shape=[shape((rows, w)) for w in widths],
        compiler_params=params(16),
        cost_estimate=cost(0.2),
        name="unpack",
    )(info, *pieces)


def pair_index(qb, kb):
    return qb * (qb + 1) // 2 + kb


def prepare(parts, block, docs, info_ref, bias_ref, open_ref):
    down = lax.broadcasted_iota(jnp.int32, (block, block), 0)
    across = lax.broadcasted_iota(jnp.int32, (1, block), 1)
    for qb in range(parts):
        lanes = qb * block + across
        opening = jnp.zeros((1, block), jnp.int32)
        first = jnp.int32(0)
        for n in range(docs):
            start = info_ref[2 + n]
            opening = jnp.where(start <= lanes, jnp.maximum(opening, start), opening)
            first = jnp.where(start <= qb * block, jnp.maximum(first, start), first)
        open_ref[qb] = first // block
        for kb in range(qb + 1):
            seen = down >= opening - kb * block
            if kb == qb:
                seen = seen & (down <= across)
            bias_ref[pair_index(qb, kb)] = jnp.where(seen, 0.0, MASKED).astype(jnp.float32)


def flip(x):
    return jnp.transpose(x.astype(jnp.float32))


def head_cols(h):
    return slice(h * HEAD_DIM, (h + 1) * HEAD_DIM)


def over_heads(tile):
    return jnp.concatenate([tile] * GROUP, axis=1)


def forward_kernel(parts, block, docs, info_ref, *refs):
    pieces = refs[:parts]
    out_ref, lse_ref = refs[parts : parts + 2]
    bias_ref, open_ref, q_s, k_s, vt_s, top_s, sum_s, acc_s = refs[parts + 2 :]
    me = info_ref[0]
    wide = GROUP * HEAD_DIM
    factor = math.log2(math.e) / math.sqrt(HEAD_DIM)
    prepare(parts, block, docs, info_ref, bias_ref, open_ref)
    for d in range(parts):
        for h in range(GROUP):
            q_s[me ^ d, h * block : (h + 1) * block] = pieces[d][:, head_cols(h)]
        k_s[me ^ d] = pieces[d][:, wide : wide + HEAD_DIM]
        vt_s[me ^ d] = flip(pieces[d][:, wide + HEAD_DIM :]).astype(jnp.bfloat16)

    def rows_of(qb, carry):
        top_s[...] = jnp.full_like(top_s, 2.0 * MASKED)
        sum_s[...] = jnp.zeros_like(sum_s)
        acc_s[...] = jnp.zeros_like(acc_s)

        def pair(back, carry):
            kb = qb - back
            bias = over_heads(bias_ref[pair_index(qb, kb)])
            raw = mm(k_s[kb], q_s[qb], NT) * factor + bias
            old = top_s[...]
            top = jnp.maximum(old, jnp.max(raw, axis=0, keepdims=True))
            shrink = jnp.exp2(old - top)
            raised = jnp.exp2(raw - top)
            top_s[...] = top
            sum_s[...] = sum_s[...] * shrink + jnp.sum(raised, axis=0, keepdims=True)
            acc_s[...] = acc_s[...] * shrink + mm(vt_s[kb], raised.astype(jnp.bfloat16))
            return carry

        lax.fori_loop(0, qb - open_ref[qb] + 1, pair, 0)
        out = (acc_s[...] / sum_s[...]).astype(jnp.bfloat16)
        spot = me ^ qb
        for h in range(GROUP):
            out_ref[head_cols(h), pl.ds(pl.multiple_of(spot * block, block), block)] = out[
                :, h * block : (h + 1) * block
            ]
        lse_ref[spot] = jnp.broadcast_to(top_s[...] + jnp.log2(sum_s[...]), lse_ref.shape[1:])
        return carry

    lax.fori_loop(0, parts, rows_of, 0)


def whole_block(dims):
    return pl.BlockSpec(dims, lambda i, info: (0,) * len(dims))


def piece_block(rows, cols, at):
    return pl.BlockSpec((rows, cols), lambda i, info: (0, at))


def attention(info, pieces, token, parts, docs):
    block, cols = pieces[-1][0].shape
    pairs = parts * (parts + 1) // 2
    wide = GROUP * HEAD_DIM
    vm = pltpu.VMEM
    return pl.pallas_call(
        functools.partial(forward_kernel, parts, block, docs),
        grid_spec=pltpu.PrefetchScalarGridSpec(
            num_scalar_prefetch=1,
            grid=(1,),
            in_specs=[piece_block(block, cols, at) for x, at in pieces],
            out_specs=[
                whole_block((wide, parts * block)),
                whole_block((parts, 8, GROUP * block)),
            ],
            scratch_shapes=[
                vm((pairs, block, block), jnp.float32),
                pltpu.SMEM((parts,), jnp.int32),
                vm((parts, GROUP * block, HEAD_DIM), jnp.bfloat16),
                vm((parts, block, HEAD_DIM), jnp.bfloat16),
                vm((parts, HEAD_DIM, block), jnp.bfloat16),
                vm((1, GROUP * block), jnp.float32),
                vm((1, GROUP * block), jnp.float32),
                vm((HEAD_DIM, GROUP * block), jnp.float32),
            ],
        ),
        out_shape=[
            shape((wide, parts * block)),
            shape((parts, 8, GROUP * block), jnp.float32),
        ],
        compiler_params=params(24),
        cost_estimate=cost(2.5),
        name="attention",
    )(gate([info], token)[0], *[x for x, at in pieces])


def backward_kernel(parts, block, docs, info_ref, *refs):
    pieces = refs[:parts]
    grad_ref, out_ref, lse_ref = refs[parts : parts + 3]
    res_ref = refs[parts + 3]
    bias_ref, open_ref, q_s, k_s, kt_s, v_s, do_s, dk_s, dv_s, dq_s = refs[parts + 4 :]
    me = info_ref[0]
    wide = GROUP * HEAD_DIM
    scale = 1.0 / math.sqrt(HEAD_DIM)
    factor = math.log2(math.e) * scale
    prepare(parts, block, docs, info_ref, bias_ref, open_ref)
    for d in range(parts):
        for h in range(GROUP):
            q_s[me ^ d, h * block : (h + 1) * block] = pieces[d][:, head_cols(h)]
            do_s[me ^ d, h * block : (h + 1) * block] = grad_ref[d, :, head_cols(h)]
        k_s[me ^ d] = pieces[d][:, wide : wide + HEAD_DIM]
        kt_s[me ^ d] = flip(pieces[d][:, wide : wide + HEAD_DIM]).astype(jnp.bfloat16)
        v_s[me ^ d] = pieces[d][:, wide + HEAD_DIM :]
    dk_s[...] = jnp.zeros_like(dk_s)
    dv_s[...] = jnp.zeros_like(dv_s)

    def rows_of(qb, carry):
        spot = me ^ qb
        dq_s[...] = jnp.zeros_like(dq_s)
        here = pl.ds(pl.multiple_of(spot * block, block), block)
        out = jnp.concatenate([out_ref[head_cols(h), here] for h in range(GROUP)], axis=1)
        delta = jnp.sum(flip(do_s[qb]) * out.astype(jnp.float32), axis=0, keepdims=True)
        lse = lse_ref[spot, :1]

        def pair(back, carry):
            kb = qb - back
            bias = over_heads(bias_ref[pair_index(qb, kb)])
            probs = jnp.exp2(mm(k_s[kb], q_s[qb], NT) * factor + bias - lse)
            dv_s[kb] += mm(probs.astype(jnp.bfloat16), do_s[qb])
            slope = (probs * (mm(v_s[kb], do_s[qb], NT) - delta)).astype(jnp.bfloat16)
            dk_s[kb] += mm(slope, q_s[qb])
            dq_s[...] += mm(kt_s[kb], slope)
            return carry

        lax.fori_loop(0, qb - open_ref[qb] + 1, pair, 0)
        back = (jnp.transpose(dq_s[...]) * scale).astype(jnp.bfloat16)
        for h in range(GROUP):
            res_ref[spot, :, head_cols(h)] = back[h * block : (h + 1) * block]
        return carry

    lax.fori_loop(0, parts, rows_of, 0)
    for kb in range(parts):
        res_ref[me ^ kb, :, wide : wide + HEAD_DIM] = (dk_s[kb] * scale).astype(jnp.bfloat16)
        res_ref[me ^ kb, :, wide + HEAD_DIM :] = dv_s[kb].astype(jnp.bfloat16)


def attention_back(info, pieces, grads, out, lse, token, parts, docs, gp):
    block, cols = pieces[-1][0].shape
    pairs = parts * (parts + 1) // 2
    wide = GROUP * HEAD_DIM
    vm = pltpu.VMEM
    return pl.pallas_call(
        functools.partial(backward_kernel, parts, block, docs),
        grid_spec=pltpu.PrefetchScalarGridSpec(
            num_scalar_prefetch=1,
            grid=(1,),
            in_specs=[piece_block(block, cols, at) for x, at in pieces]
            + [
                pl.BlockSpec((parts, block, wide), lambda i, info: (0, 0, gp)),
                whole_block((wide, parts * block)),
                whole_block((parts, 8, GROUP * block)),
            ],
            out_specs=whole_block((parts, block, cols)),
            scratch_shapes=[
                vm((pairs, block, block), jnp.float32),
                pltpu.SMEM((parts,), jnp.int32),
                vm((parts, GROUP * block, HEAD_DIM), jnp.bfloat16),
                vm((parts, block, HEAD_DIM), jnp.bfloat16),
                vm((parts, HEAD_DIM, block), jnp.bfloat16),
                vm((parts, block, HEAD_DIM), jnp.bfloat16),
                vm((parts, GROUP * block, HEAD_DIM), jnp.bfloat16),
                vm((parts, block, HEAD_DIM), jnp.float32),
                vm((parts, block, HEAD_DIM), jnp.float32),
                vm((HEAD_DIM, GROUP * block), jnp.float32),
            ],
        ),
        out_shape=shape((parts, block, cols)),
        compiler_params=params(32),
        cost_estimate=cost(1.0),
        name="attention_back",
    )(gate([info], token)[0], *[x for x, at in pieces], grads, out, lse)


def place_of(share, order):
    out = 0 * share
    for k, bit in enumerate(order):
        out = out + ((share >> bit) & 1) * (1 << k)
    return out


def unplace(place, order):
    out = 0 * place
    for k, bit in enumerate(order):
        out = out + ((place >> k) & 1) * (1 << bit)
    return out


def reverse_bits(x, bits):
    out = 0 * x
    for b in range(bits):
        out = out + ((x >> b) & 1) * (1 << (bits - 1 - b))
    return out


def weight_kernel(parts, groups, width, order, info_ref, *refs):
    outs, lows, highs = refs[:groups], refs[groups : groups + 2], refs[groups + 2 : groups + 4]
    chunk = refs[groups + 4 : groups + 2 + parts]
    keep_ref, send_ref = refs[groups + 2 + parts :]
    odd = ((info_ref[1] >> order[0]) & 1) == 1
    rows = GROUP * HEAD_DIM
    grads = [jnp.concatenate([lows[d][...], highs[d][...]], axis=1) for d in range(2)]
    grads = jnp.concatenate(grads + [x[...] for x in chunk], axis=0)
    for gp in range(groups):
        total = mm(outs[gp][...], grads)
        low, high = total[:, :width], total[:, width:]
        spot = slice(gp * rows, (gp + 1) * rows)
        keep_ref[0, spot] = jnp.where(odd, high, low)
        send_ref[0, spot] = jnp.where(odd, low, high).astype(jnp.bfloat16)


def weight_terms(info, outs, near, chunk, token, shares, c, chunks, width, order):
    groups, parts = len(outs), 2 + len(chunk)
    rows, block = outs[0].shape[0], near[0].shape[0]
    half = shares // 2
    bits = half.bit_length() - 1
    spot = pl.BlockSpec((1, groups * rows, width), lambda t, info: (reverse_bits(t, bits), 0, 0))

    def mate(t, info):
        return t ^ (place_of(info[1], order) >> 1)

    def original(side, x):
        shift = (x.shape[1] - shares * chunks * width) // width
        return pl.BlockSpec(
            (block, width),
            lambda t, info: (0, shift + unplace(2 * mate(t, info) + side, order) * chunks + c),
        )

    return pl.pallas_call(
        functools.partial(weight_kernel, parts, groups, width, order),
        grid_spec=pltpu.PrefetchScalarGridSpec(
            num_scalar_prefetch=1,
            grid=(half,),
            in_specs=[pl.BlockSpec((rows, parts * block), lambda t, info: (0, 0))] * groups
            + [original(side, x) for side in range(2) for x in near]
            + [pl.BlockSpec((block, 2 * width), lambda t, info: (0, mate(t, info)))] * len(chunk),
            out_specs=[spot, spot],
        ),
        out_shape=[
            shape((half, groups * rows, width), jnp.float32),
            shape((half, groups * rows, width)),
        ],
        compiler_params=params(16),
        cost_estimate=cost(0.2),
        name="weight_terms",
    )(gate([info], token)[0], *outs, *near, *near, *chunk)


def merge_kernel(keep_low, keep_high, got_low, got_high, keep_ref, send_ref):
    keep_ref[...] = keep_low[...] + got_low[...].astype(jnp.float32)
    send_ref[...] = (keep_high[...] + got_high[...].astype(jnp.float32)).astype(jnp.bfloat16)


def merge(keep, got, token):
    count, rows, width = keep.shape
    half = count // 2
    keep = gate([keep], token)[0]
    low = pl.BlockSpec((1, rows, width), lambda t: (t, 0, 0))
    high = pl.BlockSpec((1, rows, width), lambda t: (t + half, 0, 0))
    return pl.pallas_call(
        merge_kernel,
        grid=(half,),
        in_specs=[low, high, low, high],
        out_specs=[low, low],
        out_shape=[
            shape((half, rows, width), jnp.float32),
            shape((half, rows, width)),
        ],
        compiler_params=params(12),
        cost_estimate=cost(0.02),
        name="merge",
    )(keep, keep, got, got)


def finish_kernel(scale, keep_ref, got_ref, *refs):
    refs[-1][...] = (keep_ref[0] + got_ref[0].astype(jnp.float32)) * scale


def finish(keep, got, so_far, token, c, chunks, scale):
    _, rows, width = keep.shape
    more = [] if so_far is None else [so_far]
    step = rows // 2
    spec = pl.BlockSpec((1, step, width), lambda i: (0, i, 0))
    return pl.pallas_call(
        functools.partial(finish_kernel, scale),
        grid=(rows // step,),
        in_specs=[spec, spec] + [ANY] * len(more),
        out_specs=pl.BlockSpec((step, width), lambda i: (i, c)),
        out_shape=shape((rows, width * chunks), jnp.float32),
        input_output_aliases={2: 0} if more else {},
        compiler_params=params(8),
        cost_estimate=cost(0.02),
        name="finish",
    )(gate([keep], token)[0], got, *more)


def shifted(ref, like, columns):
    more = ref.shape[1] - like.shape[1]
    return slice(columns.start + more, columns.stop + more)


def project_kernel(parts, shares, width, chunks, orders, picked, first, last, *refs):
    w_ref, near = refs[0], refs[1:3]
    far = refs[3 : 3 + len(picked) * (parts - 2)]
    acc_ref, out_ref = refs[-2] if not first else None, refs[-1]
    columns = [(c, unplace(p, orders[c])) for c in picked for p in range(shares)]
    weights = jnp.concatenate([w_ref[:, column(j, c, chunks, width)] for c, j in columns], axis=1)
    for d in range(parts):
        if d < 2:
            rows = jnp.concatenate([near[d][:, shifted(near[d], w_ref, column(j, c, chunks, width))] for c, j in columns], axis=1)
        else:
            mine = [far[i * (parts - 2) + d - 2][...] for i in range(len(picked))]
            rows = mine[0] if len(mine) == 1 else jnp.concatenate(mine, axis=1)
        total = mm(rows, weights, NT)
        if not first:
            total += acc_ref[d]
        out_ref[d] = total.astype(out_ref.dtype)


def project(out_weight, near, far, acc, token, orders, picked, shares, width, last):
    feats, model = out_weight.shape
    rows = near[0].shape[0]
    parts = 2 + len(far[0])
    step = min(256, feats)
    flat = [x for group in far for x in group]
    first = acc is None
    block = pl.BlockSpec((parts, rows, step), lambda i: (0, 0, i))
    return pl.pallas_call(
        functools.partial(
            project_kernel, parts, shares, width, len(orders), orders, picked, first, last
        ),
        grid=(feats // step,),
        in_specs=[pl.BlockSpec((step, model), lambda i: (i, 0))]
        + [pl.BlockSpec((rows, x.shape[1]), lambda i: (0, 0)) for x in near]
        + [pl.BlockSpec((rows, shares * width), lambda i: (0, 0))] * len(flat)
        + ([] if first else [block]),
        out_specs=block,
        out_shape=shape((parts, rows, feats), jnp.bfloat16 if last else jnp.float32),
        compiler_params=params(24),
        cost_estimate=cost(0.2),
        name="project",
    )(gate([out_weight], token)[0], *near, *flat, *([] if first else [acc]))


def body(grad_out, queries, keys, values, out_weight, doc_starts):
    parts, shares = lax.axis_size("seq"), lax.axis_size("dp")
    groups = KV_HEADS // parts
    docs = doc_starts.shape[-1]
    cotangent = grad_out[0]
    rows, model = cotangent.shape
    chunks = max(1, min(4, model // shares // 128))
    width = model // shares // chunks
    bits = tuple(range(shares.bit_length() - 1))
    turned = bits[1:] + bits[:1]
    orders = [turned if c == 0 else bits for c in range(chunks)]
    scale = 1.0 / math.sqrt(rows * parts * shares)
    info = jnp.concatenate(
        [
            jnp.stack([lax.axis_index("seq"), lax.axis_index("dp")]).astype(jnp.int32),
            doc_starts[0],
        ]
    )

    def over_seq(x, d):
        return lax.ppermute(x, "seq", [(i, i ^ d) for i in range(parts)])

    def over_dp(x, d):
        return lax.ppermute(x, "dp", [(i, i ^ d) for i in range(shares)])

    far = range(2, parts)
    all_groups = tuple(range(groups))
    me = lax.axis_index("seq").astype(jnp.int32).reshape(1)
    sources = (queries[0], keys[0], values[0])
    packed = [pack(me, sources, parts, tuple((d, (0,)) for d in far))]
    rest = [(d, (gp,)) for gp in range(1, groups) for d in far]
    rest = pack(
        gate([me], packed[0][0])[0],
        sources,
        parts,
        tuple([(0, all_groups), (1, all_groups)] + rest),
    )
    for gp in range(1, groups):
        packed.append(rest[2 + (gp - 1) * len(far) : 2 + gp * len(far)])
    sent_far = [[over_seq(x, d) for x, d in zip(group, far)] for group in packed]
    core = over_seq(rest[1], 1)
    pieces = [[(rest[0], gp), (core, gp)] + [(x, 0) for x in sent_far[gp]] for gp in range(groups)]
    sends = pack_chunks(gate([cotangent], rest[0])[0], orders, shares, width)
    near = [cotangent, over_seq(gate([cotangent], *sent_far[0], sends[-1])[0], 1)]

    far_half = {}

    def send_chunk(c, *tokens):
        mine = gate([sends[c]], *tokens)[0]
        far_half[c] = [over_seq(mine, d) for d in range(2, parts, 2)]

    for c in range(chunks):
        if c < groups:
            send_chunk(c, *sent_far[c], sends[-1])
        else:
            send_chunk(c, *far_half[max(0, c - groups)])

    fwd = []
    token = sends[-1]
    for gp in range(groups):
        fwd.append(attention(info, pieces[gp], token, parts, docs))
        token = fwd[-1][0]
        if gp == 0:
            token = (token, near[1])
    outs = [pair[0] for pair in fwd]

    fars, state, back, results = {}, {}, {}, {}
    acc = weight_grad = None

    def hop(c, send, stage):
        return over_dp(send, 1 << orders[c][stage])

    def receive(c):
        fars[c] = []
        for x in gate(far_half[c], token):
            fars[c] += [x, over_seq(x, 1)]

    def weigh(c):
        nonlocal token
        if c not in fars:
            receive(c)
        keep, send = weight_terms(
            info, outs, near, fars[c], token, shares, c, chunks, width, orders[c]
        )
        token = send
        state[c] = (keep, hop(c, send, 0), 1)

    def advance(c):
        nonlocal token, weight_grad
        if c not in state or state[c] is None:
            return
        keep, got, stage = state[c]
        if stage == len(bits):
            token = weight_grad = finish(keep, got, weight_grad, token, c, chunks, scale)
            state[c] = None
        else:
            keep, send = merge(keep, got, token)
            token = send
            state[c] = (keep, hop(c, send, stage), stage + 1)

    def project_step(picked, last):
        nonlocal token, acc
        token = acc = project(
            out_weight, near, [fars[c] for c in picked], acc, token, orders, picked, shares, width, last
        )

    def send_back(gp):
        nonlocal token
        res = attention_back(info, pieces[gp], acc, outs[gp], fwd[gp][1], token, parts, docs, gp)
        token = results[gp] = res
        back[gp] = {d: over_seq(res[d : d + 2], d) for d in range(2, parts, 2)}

    def hand_over(gp, *tokens):
        got = gate([back[gp][d] for d in range(2, parts, 2)], *tokens)
        mine = [results[gp][1:2]] + [x[1:2] for x in got]
        crossed = over_seq(jnp.concatenate(mine, axis=0), 1)
        out = [results[gp][0], crossed[0]]
        for i, x in enumerate(got):
            out += [x[0], crossed[1 + i]]
        return out

    last = chunks - 1
    for c in range(chunks):
        if c > 1:
            advance(c - 2)
        weigh(c)
        project_step([c], c == last)
    send_back(0)
    for c in range(last):
        advance(c)
    for gp in range(1, groups):
        send_back(gp)
    advance(last - 2)
    advance(last)
    advance(last - 1)
    firsts = hand_over(0, token)
    advance(0)
    advance(last - 1)
    token = (token, firsts[1])
    advance(last)
    lasts = [hand_over(gp, token) for gp in range(1, groups)]
    for _ in bits:
        for c in range(chunks):
            advance(c)
    back = firsts + [x for group in lasts for x in group]
    grad_q, grad_k, grad_v = unpack(gate([info], token)[0], back, parts, groups)
    return (grad_q[None], grad_k[None], grad_v[None], weight_grad)


def solution(mesh):
    return jax.shard_map(
        body,
        mesh=mesh,
        in_specs=(
            P("dp", "seq", None),
            P("dp", "seq", None),
            P("dp", "seq", None),
            P("dp", "seq", None),
            P("seq", None),
            P("dp", None),
        ),
        out_specs=(
            P("dp", "seq", None),
            P("dp", "seq", None),
            P("dp", "seq", None),
            P("seq", "dp"),
        ),
        check_vma=False,
    )
```

```python
import functools
import math

import jax
import jax.numpy as jnp
from jax import lax
from jax.experimental import pallas as pl
from jax.experimental.pallas import tpu as pltpu
from jax.sharding import PartitionSpec as P

HEADS = 32
KV_HEADS = 8
HEAD_DIM = 128
GROUP = HEADS // KV_HEADS
MASKED = -1e30
NT = (((1,), (1,)), ((), ()))
NN = (((1,), (0,)), ((), ()))


def mm(a, b, dims=NN):
    return lax.dot_general(a, b, dims, preferred_element_type=jnp.float32)


def params(mib):
    return pltpu.CompilerParams(vmem_limit_bytes=mib * 2**20)


def cost(weight):
    return pl.CostEstimate(flops=int(weight * 1e9), bytes_accessed=1024, transcendentals=0)


ANY = pl.BlockSpec(memory_space=pl.ANY)


def shape(dims, dtype=jnp.bfloat16):
    return jax.ShapeDtypeStruct(dims, dtype)


def gate(arrays, *tokens):
    flat = [x for token in tokens for x in (token if isinstance(token, tuple) else (token,))]
    return list(lax.optimization_barrier((*arrays, *flat)))[: len(arrays)]


def pack_kernel(jobs, joined, me_ref, *refs):
    wide = GROUP * HEAD_DIM
    size = wide + 2 * HEAD_DIM
    sources, outs = iter(refs[: len(refs) - len(jobs)]), refs[len(refs) - len(jobs) :]
    if joined:
        outs[1][:, size * len(jobs[1][1]) :] = refs[0][...]
        next(sources)
    for out, (d, members) in zip(outs, jobs):
        for slot in range(len(members)):
            start = slot * size
            for width in (wide, HEAD_DIM, HEAD_DIM):
                out[:, start : start + width] = next(sources)[...]
                start += width


def pack(me, sources, parts, jobs, joined=None):
    rows = sources[0].shape[0]
    groups = KV_HEADS // parts
    wide = GROUP * HEAD_DIM
    size = wide + 2 * HEAD_DIM
    step = min(128, rows)

    def pick(width, d, gp):
        return pl.BlockSpec((step, width), lambda i, me: (i, (me[0] ^ d) * groups + gp))

    specs = [
        pick(width, d, gp)
        for d, members in jobs
        for gp in members
        for width in (wide, HEAD_DIM, HEAD_DIM)
    ]
    more = [] if joined is None else [joined]
    widths = [size * len(members) for d, members in jobs]
    if more:
        widths[1] += joined.shape[1]
    return pl.pallas_call(
        functools.partial(pack_kernel, jobs, bool(more)),
        grid_spec=pltpu.PrefetchScalarGridSpec(
            num_scalar_prefetch=1,
            grid=(rows // step,),
            in_specs=[pl.BlockSpec((step, x.shape[1]), lambda i, me: (i, 0)) for x in more] + specs,
            out_specs=[pl.BlockSpec((step, width), lambda i, me: (i, 0)) for width in widths],
        ),
        out_shape=[shape((rows, width)) for width in widths],
        compiler_params=params(60),
        cost_estimate=cost(0.2),
        name="pack",
    )(me, *more, *sources * (len(specs) // 3))


def column(share, c, chunks, width):
    return slice((share * chunks + c) * width, (share * chunks + c + 1) * width)


def pack_chunks_kernel(orders, shares, width, g_ref, *out_refs):
    for c, order in enumerate(orders):
        for place in range(shares):
            share = unplace(place, order)
            out_refs[c][:, place * width : (place + 1) * width] = g_ref[
                :, column(share, c, len(orders), width)
            ]


def pack_chunks(cotangent, orders, shares, width):
    rows, model = cotangent.shape
    step = min(64, rows)
    return pl.pallas_call(
        functools.partial(pack_chunks_kernel, orders, shares, width),
        grid=(rows // step,),
        in_specs=[pl.BlockSpec((step, model), lambda i: (i, 0))],
        out_specs=[pl.BlockSpec((step, shares * width), lambda i: (i, 0))] * len(orders),
        out_shape=[shape((rows, shares * width)) for order in orders],
        compiler_params=params(60),
        cost_estimate=cost(0.2),
        name="pack_chunks",
    )(cotangent)


def unpack_kernel(parts, groups, info_ref, *refs):
    count = parts * groups
    q_ref, k_ref, v_ref = refs[count:]
    wide = GROUP * HEAD_DIM
    for gp in range(groups):
        for d in range(parts):
            piece = refs[gp * parts + d]
            place = (info_ref[0] ^ d) * groups + gp
            q_ref[:, pl.ds(pl.multiple_of(place * wide, wide), wide)] = piece[:, :wide]
            narrow = pl.ds(pl.multiple_of(place * HEAD_DIM, HEAD_DIM), HEAD_DIM)
            k_ref[:, narrow] = piece[:, wide : wide + HEAD_DIM]
            v_ref[:, narrow] = piece[:, wide + HEAD_DIM :]


def unpack(info, pieces, parts, groups):
    rows, cols = pieces[0].shape
    wide = GROUP * HEAD_DIM
    step = min(64, rows)
    total = parts * groups
    widths = (total * wide, total * HEAD_DIM, total * HEAD_DIM)
    return pl.pallas_call(
        functools.partial(unpack_kernel, parts, groups),
        grid_spec=pltpu.PrefetchScalarGridSpec(
            num_scalar_prefetch=1,
            grid=(rows // step,),
            in_specs=[pl.BlockSpec((step, cols), lambda i, info: (i, 0))] * total,
            out_specs=[pl.BlockSpec((step, w), lambda i, info: (i, 0)) for w in widths],
        ),
        out_shape=[shape((rows, w)) for w in widths],
        compiler_params=params(16),
        cost_estimate=cost(0.2),
        name="unpack",
    )(info, *pieces)


def pair_index(qb, kb):
    return qb * (qb + 1) // 2 + kb


def prepare(parts, block, docs, info_ref, bias_ref, open_ref):
    down = lax.broadcasted_iota(jnp.int32, (block, block), 0)
    across = lax.broadcasted_iota(jnp.int32, (1, block), 1)
    for qb in range(parts):
        lanes = qb * block + across
        opening = jnp.zeros((1, block), jnp.int32)
        first = jnp.int32(0)
        for n in range(docs):
            start = info_ref[2 + n]
            opening = jnp.where(start <= lanes, jnp.maximum(opening, start), opening)
            first = jnp.where(start <= qb * block, jnp.maximum(first, start), first)
        open_ref[qb] = first // block
        for kb in range(qb + 1):
            seen = down >= opening - kb * block
            if kb == qb:
                seen = seen & (down <= across)
            bias_ref[pair_index(qb, kb)] = jnp.where(seen, 0.0, MASKED).astype(jnp.float32)


def flip(x):
    return jnp.transpose(x.astype(jnp.float32))


def head_cols(h):
    return slice(h * HEAD_DIM, (h + 1) * HEAD_DIM)


def over_heads(tile):
    return jnp.concatenate([tile] * GROUP, axis=1)


def forward_kernel(parts, block, docs, info_ref, *refs):
    pieces = refs[:parts]
    out_ref, lse_ref = refs[parts : parts + 2]
    bias_ref, open_ref, q_s, k_s, vt_s, top_s, sum_s, acc_s = refs[parts + 2 :]
    me = info_ref[0]
    wide = GROUP * HEAD_DIM
    factor = math.log2(math.e) / math.sqrt(HEAD_DIM)
    prepare(parts, block, docs, info_ref, bias_ref, open_ref)
    for d in range(parts):
        for h in range(GROUP):
            q_s[me ^ d, h * block : (h + 1) * block] = pieces[d][:, head_cols(h)]
        k_s[me ^ d] = pieces[d][:, wide : wide + HEAD_DIM]
        vt_s[me ^ d] = flip(pieces[d][:, wide + HEAD_DIM :]).astype(jnp.bfloat16)

    def rows_of(qb, carry):
        top_s[...] = jnp.full_like(top_s, 2.0 * MASKED)
        sum_s[...] = jnp.zeros_like(sum_s)
        acc_s[...] = jnp.zeros_like(acc_s)

        def pair(back, carry):
            kb = qb - back
            bias = over_heads(bias_ref[pair_index(qb, kb)])
            raw = mm(k_s[kb], q_s[qb], NT) * factor + bias
            old = top_s[...]
            top = jnp.maximum(old, jnp.max(raw, axis=0, keepdims=True))
            shrink = jnp.exp2(old - top)
            raised = jnp.exp2(raw - top)
            top_s[...] = top
            sum_s[...] = sum_s[...] * shrink + jnp.sum(raised, axis=0, keepdims=True)
            acc_s[...] = acc_s[...] * shrink + mm(vt_s[kb], raised.astype(jnp.bfloat16))
            return carry

        lax.fori_loop(0, qb - open_ref[qb] + 1, pair, 0)
        out = (acc_s[...] / sum_s[...]).astype(jnp.bfloat16)
        spot = me ^ qb
        for h in range(GROUP):
            out_ref[head_cols(h), pl.ds(pl.multiple_of(spot * block, block), block)] = out[
                :, h * block : (h + 1) * block
            ]
        lse_ref[spot] = jnp.broadcast_to(top_s[...] + jnp.log2(sum_s[...]), lse_ref.shape[1:])
        return carry

    lax.fori_loop(0, parts, rows_of, 0)


def whole_block(dims):
    return pl.BlockSpec(dims, lambda i, info: (0,) * len(dims))


def piece_block(rows, cols, at):
    return pl.BlockSpec((rows, cols), lambda i, info: (0, at))


def attention(info, pieces, token, parts, docs):
    block, cols = pieces[-1][0].shape
    pairs = parts * (parts + 1) // 2
    wide = GROUP * HEAD_DIM
    vm = pltpu.VMEM
    return pl.pallas_call(
        functools.partial(forward_kernel, parts, block, docs),
        grid_spec=pltpu.PrefetchScalarGridSpec(
            num_scalar_prefetch=1,
            grid=(1,),
            in_specs=[piece_block(block, cols, at) for x, at in pieces],
            out_specs=[
                whole_block((wide, parts * block)),
                whole_block((parts, 8, GROUP * block)),
            ],
            scratch_shapes=[
                vm((pairs, block, block), jnp.float32),
                pltpu.SMEM((parts,), jnp.int32),
                vm((parts, GROUP * block, HEAD_DIM), jnp.bfloat16),
                vm((parts, block, HEAD_DIM), jnp.bfloat16),
                vm((parts, HEAD_DIM, block), jnp.bfloat16),
                vm((1, GROUP * block), jnp.float32),
                vm((1, GROUP * block), jnp.float32),
                vm((HEAD_DIM, GROUP * block), jnp.float32),
            ],
        ),
        out_shape=[
            shape((wide, parts * block)),
            shape((parts, 8, GROUP * block), jnp.float32),
        ],
        compiler_params=params(24),
        cost_estimate=cost(2.5),
        name="attention",
    )(gate([info], token)[0], *[x for x, at in pieces])


def backward_kernel(parts, block, docs, info_ref, *refs):
    pieces = refs[:parts]
    grad_ref, out_ref, lse_ref = refs[parts : parts + 3]
    res_ref = refs[parts + 3]
    bias_ref, open_ref, q_s, k_s, kt_s, v_s, do_s, dk_s, dv_s, dq_s = refs[parts + 4 :]
    me = info_ref[0]
    wide = GROUP * HEAD_DIM
    scale = 1.0 / math.sqrt(HEAD_DIM)
    factor = math.log2(math.e) * scale
    prepare(parts, block, docs, info_ref, bias_ref, open_ref)
    for d in range(parts):
        for h in range(GROUP):
            q_s[me ^ d, h * block : (h + 1) * block] = pieces[d][:, head_cols(h)]
            do_s[me ^ d, h * block : (h + 1) * block] = grad_ref[d, :, head_cols(h)]
        k_s[me ^ d] = pieces[d][:, wide : wide + HEAD_DIM]
        kt_s[me ^ d] = flip(pieces[d][:, wide : wide + HEAD_DIM]).astype(jnp.bfloat16)
        v_s[me ^ d] = pieces[d][:, wide + HEAD_DIM :]
    dk_s[...] = jnp.zeros_like(dk_s)
    dv_s[...] = jnp.zeros_like(dv_s)

    def rows_of(qb, carry):
        spot = me ^ qb
        dq_s[...] = jnp.zeros_like(dq_s)
        here = pl.ds(pl.multiple_of(spot * block, block), block)
        out = jnp.concatenate([out_ref[head_cols(h), here] for h in range(GROUP)], axis=1)
        delta = jnp.sum(flip(do_s[qb]) * out.astype(jnp.float32), axis=0, keepdims=True)
        lse = lse_ref[spot, :1]

        def pair(back, carry):
            kb = qb - back
            bias = over_heads(bias_ref[pair_index(qb, kb)])
            probs = jnp.exp2(mm(k_s[kb], q_s[qb], NT) * factor + bias - lse)
            dv_s[kb] += mm(probs.astype(jnp.bfloat16), do_s[qb])
            slope = (probs * (mm(v_s[kb], do_s[qb], NT) - delta)).astype(jnp.bfloat16)
            dk_s[kb] += mm(slope, q_s[qb])
            dq_s[...] += mm(kt_s[kb], slope)
            return carry

        lax.fori_loop(0, qb - open_ref[qb] + 1, pair, 0)
        back = (jnp.transpose(dq_s[...]) * scale).astype(jnp.bfloat16)
        for h in range(GROUP):
            res_ref[spot, :, head_cols(h)] = back[h * block : (h + 1) * block]
        return carry

    lax.fori_loop(0, parts, rows_of, 0)
    for kb in range(parts):
        res_ref[me ^ kb, :, wide : wide + HEAD_DIM] = (dk_s[kb] * scale).astype(jnp.bfloat16)
        res_ref[me ^ kb, :, wide + HEAD_DIM :] = dv_s[kb].astype(jnp.bfloat16)


def attention_back(info, pieces, grads, out, lse, token, parts, docs, gp):
    block, cols = pieces[-1][0].shape
    pairs = parts * (parts + 1) // 2
    wide = GROUP * HEAD_DIM
    vm = pltpu.VMEM
    return pl.pallas_call(
        functools.partial(backward_kernel, parts, block, docs),
        grid_spec=pltpu.PrefetchScalarGridSpec(
            num_scalar_prefetch=1,
            grid=(1,),
            in_specs=[piece_block(block, cols, at) for x, at in pieces]
            + [
                pl.BlockSpec((parts, block, wide), lambda i, info: (0, 0, gp)),
                whole_block((wide, parts * block)),
                whole_block((parts, 8, GROUP * block)),
            ],
            out_specs=whole_block((parts, block, cols)),
            scratch_shapes=[
                vm((pairs, block, block), jnp.float32),
                pltpu.SMEM((parts,), jnp.int32),
                vm((parts, GROUP * block, HEAD_DIM), jnp.bfloat16),
                vm((parts, block, HEAD_DIM), jnp.bfloat16),
                vm((parts, HEAD_DIM, block), jnp.bfloat16),
                vm((parts, block, HEAD_DIM), jnp.bfloat16),
                vm((parts, GROUP * block, HEAD_DIM), jnp.bfloat16),
                vm((parts, block, HEAD_DIM), jnp.float32),
                vm((parts, block, HEAD_DIM), jnp.float32),
                vm((HEAD_DIM, GROUP * block), jnp.float32),
            ],
        ),
        out_shape=shape((parts, block, cols)),
        compiler_params=params(32),
        cost_estimate=cost(1.0),
        name="attention_back",
    )(gate([info], token)[0], *[x for x, at in pieces], grads, out, lse)


def place_of(share, order):
    out = 0 * share
    for k, bit in enumerate(order):
        out = out + ((share >> bit) & 1) * (1 << k)
    return out


def unplace(place, order):
    out = 0 * place
    for k, bit in enumerate(order):
        out = out + ((place >> k) & 1) * (1 << bit)
    return out


def reverse_bits(x, bits):
    out = 0 * x
    for b in range(bits):
        out = out + ((x >> b) & 1) * (1 << (bits - 1 - b))
    return out


def weight_kernel(parts, groups, width, order, info_ref, *refs):
    outs, lows, highs = refs[:groups], refs[groups : groups + 2], refs[groups + 2 : groups + 4]
    chunk = refs[groups + 4 : groups + 2 + parts]
    keep_ref, send_ref = refs[groups + 2 + parts :]
    odd = ((info_ref[1] >> order[0]) & 1) == 1
    rows = GROUP * HEAD_DIM
    grads = [jnp.concatenate([lows[d][...], highs[d][...]], axis=1) for d in range(2)]
    grads = jnp.concatenate(grads + [x[...] for x in chunk], axis=0)
    for gp in range(groups):
        total = mm(outs[gp][...], grads)
        low, high = total[:, :width], total[:, width:]
        spot = slice(gp * rows, (gp + 1) * rows)
        keep_ref[0, spot] = jnp.where(odd, high, low)
        send_ref[0, spot] = jnp.where(odd, low, high).astype(jnp.bfloat16)


def weight_terms(info, outs, near, chunk, token, shares, c, chunks, width, order):
    groups, parts = len(outs), 2 + len(chunk)
    rows, block = outs[0].shape[0], near[0].shape[0]
    half = shares // 2
    bits = half.bit_length() - 1
    spot = pl.BlockSpec((1, groups * rows, width), lambda t, info: (reverse_bits(t, bits), 0, 0))

    def mate(t, info):
        return t ^ (place_of(info[1], order) >> 1)

    def original(side, x):
        shift = (x.shape[1] - shares * chunks * width) // width
        return pl.BlockSpec(
            (block, width),
            lambda t, info: (0, shift + unplace(2 * mate(t, info) + side, order) * chunks + c),
        )

    return pl.pallas_call(
        functools.partial(weight_kernel, parts, groups, width, order),
        grid_spec=pltpu.PrefetchScalarGridSpec(
            num_scalar_prefetch=1,
            grid=(half,),
            in_specs=[pl.BlockSpec((rows, parts * block), lambda t, info: (0, 0))] * groups
            + [original(side, x) for side in range(2) for x in near]
            + [pl.BlockSpec((block, 2 * width), lambda t, info: (0, mate(t, info)))] * len(chunk),
            out_specs=[spot, spot],
        ),
        out_shape=[
            shape((half, groups * rows, width), jnp.float32),
            shape((half, groups * rows, width)),
        ],
        compiler_params=params(16),
        cost_estimate=cost(0.2),
        name="weight_terms",
    )(gate([info], token)[0], *outs, *near, *near, *chunk)


def merge_kernel(keep_low, keep_high, got_low, got_high, keep_ref, send_ref):
    keep_ref[...] = keep_low[...] + got_low[...].astype(jnp.float32)
    send_ref[...] = (keep_high[...] + got_high[...].astype(jnp.float32)).astype(jnp.bfloat16)


def merge(keep, got, token):
    count, rows, width = keep.shape
    half = count // 2
    keep = gate([keep], token)[0]
    low = pl.BlockSpec((1, rows, width), lambda t: (t, 0, 0))
    high = pl.BlockSpec((1, rows, width), lambda t: (t + half, 0, 0))
    return pl.pallas_call(
        merge_kernel,
        grid=(half,),
        in_specs=[low, high, low, high],
        out_specs=[low, low],
        out_shape=[
            shape((half, rows, width), jnp.float32),
            shape((half, rows, width)),
        ],
        compiler_params=params(12),
        cost_estimate=cost(0.02),
        name="merge",
    )(keep, keep, got, got)


def finish_kernel(scale, keep_ref, got_ref, *refs):
    refs[-1][...] = (keep_ref[0] + got_ref[0].astype(jnp.float32)) * scale


def finish(keep, got, so_far, token, c, chunks, scale):
    _, rows, width = keep.shape
    more = [] if so_far is None else [so_far]
    step = rows // 2
    spec = pl.BlockSpec((1, step, width), lambda i: (0, i, 0))
    return pl.pallas_call(
        functools.partial(finish_kernel, scale),
        grid=(rows // step,),
        in_specs=[spec, spec] + [ANY] * len(more),
        out_specs=pl.BlockSpec((step, width), lambda i: (i, c)),
        out_shape=shape((rows, width * chunks), jnp.float32),
        input_output_aliases={2: 0} if more else {},
        compiler_params=params(8),
        cost_estimate=cost(0.02),
        name="finish",
    )(gate([keep], token)[0], got, *more)


def shifted(ref, like, columns):
    more = ref.shape[1] - like.shape[1]
    return slice(columns.start + more, columns.stop + more)


def project_kernel(parts, shares, width, chunks, orders, picked, first, last, *refs):
    w_ref, near = refs[0], refs[1:3]
    far = refs[3 : 3 + len(picked) * (parts - 2)]
    acc_ref, out_ref = refs[-2] if not first else None, refs[-1]
    columns = [(c, unplace(p, orders[c])) for c in picked for p in range(shares)]
    weights = jnp.concatenate([w_ref[:, column(j, c, chunks, width)] for c, j in columns], axis=1)
    for d in range(parts):
        if d < 2:
            rows = jnp.concatenate([near[d][:, shifted(near[d], w_ref, column(j, c, chunks, width))] for c, j in columns], axis=1)
        else:
            mine = [far[i * (parts - 2) + d - 2][...] for i in range(len(picked))]
            rows = mine[0] if len(mine) == 1 else jnp.concatenate(mine, axis=1)
        total = mm(rows, weights, NT)
        if not first:
            total += acc_ref[d]
        out_ref[d] = total.astype(out_ref.dtype)


def project(out_weight, near, far, acc, token, orders, picked, shares, width, last):
    feats, model = out_weight.shape
    rows = near[0].shape[0]
    parts = 2 + len(far[0])
    step = min(256, feats)
    flat = [x for group in far for x in group]
    first = acc is None
    block = pl.BlockSpec((parts, rows, step), lambda i: (0, 0, i))
    return pl.pallas_call(
        functools.partial(
            project_kernel, parts, shares, width, len(orders), orders, picked, first, last
        ),
        grid=(feats // step,),
        in_specs=[pl.BlockSpec((step, model), lambda i: (i, 0))]
        + [pl.BlockSpec((rows, x.shape[1]), lambda i: (0, 0)) for x in near]
        + [pl.BlockSpec((rows, shares * width), lambda i: (0, 0))] * len(flat)
        + ([] if first else [block]),
        out_specs=block,
        out_shape=shape((parts, rows, feats), jnp.bfloat16 if last else jnp.float32),
        compiler_params=params(24),
        cost_estimate=cost(0.2),
        name="project",
    )(gate([out_weight], token)[0], *near, *flat, *([] if first else [acc]))


def body(grad_out, queries, keys, values, out_weight, doc_starts):
    parts, shares = lax.axis_size("seq"), lax.axis_size("dp")
    groups = KV_HEADS // parts
    docs = doc_starts.shape[-1]
    cotangent = grad_out[0]
    rows, model = cotangent.shape
    chunks = max(1, min(4, model // shares // 128))
    width = model // shares // chunks
    bits = tuple(range(shares.bit_length() - 1))
    turned = bits[1:] + bits[:1]
    orders = [turned if c == 0 else bits for c in range(chunks)]
    scale = 1.0 / math.sqrt(rows * parts * shares)
    info = jnp.concatenate(
        [
            jnp.stack([lax.axis_index("seq"), lax.axis_index("dp")]).astype(jnp.int32),
            doc_starts[0],
        ]
    )

    def over_seq(x, d):
        return lax.ppermute(x, "seq", [(i, i ^ d) for i in range(parts)])

    def over_dp(x, d):
        return lax.ppermute(x, "dp", [(i, i ^ d) for i in range(shares)])

    far = range(2, parts)
    all_groups = tuple(range(groups))
    me = lax.axis_index("seq").astype(jnp.int32).reshape(1)
    sources = (queries[0], keys[0], values[0])
    packed = [pack(me, sources, parts, tuple((d, (0,)) for d in far))]
    rest = [(d, (gp,)) for gp in range(1, groups) for d in far]
    rest = pack(
        gate([me], packed[0][0])[0],
        sources,
        parts,
        tuple([(0, all_groups), (1, all_groups)] + rest),
    )
    for gp in range(1, groups):
        packed.append(rest[2 + (gp - 1) * len(far) : 2 + gp * len(far)])
    sent_far = [[over_seq(x, d) for x, d in zip(group, far)] for group in packed]
    core = over_seq(rest[1], 1)
    pieces = [[(rest[0], gp), (core, gp)] + [(x, 0) for x in sent_far[gp]] for gp in range(groups)]
    sends = pack_chunks(gate([cotangent], rest[0])[0], orders, shares, width)
    near = [cotangent, over_seq(gate([cotangent], *sent_far[0], sends[-1])[0], 1)]

    far_half = {}

    def send_chunk(c, *tokens):
        mine = gate([sends[c]], *tokens)[0]
        far_half[c] = [over_seq(mine, d) for d in range(2, parts, 2)]

    for c in range(chunks):
        if c < groups:
            send_chunk(c, *sent_far[c], sends[-1])
        else:
            send_chunk(c, *far_half[max(0, c - groups)])

    fwd = []
    token = sends[-1]
    for gp in range(groups):
        fwd.append(attention(info, pieces[gp], token, parts, docs))
        token = fwd[-1][0]
        if gp == 0:
            token = (token, near[1])
    outs = [pair[0] for pair in fwd]

    fars, state, back, results = {}, {}, {}, {}
    acc = weight_grad = None

    def hop(c, send, stage):
        return over_dp(send, 1 << orders[c][stage])

    def receive(c):
        fars[c] = []
        for x in gate(far_half[c], token):
            fars[c] += [x, over_seq(x, 1)]

    def weigh(c):
        nonlocal token
        if c not in fars:
            receive(c)
        keep, send = weight_terms(
            info, outs, near, fars[c], token, shares, c, chunks, width, orders[c]
        )
        token = send
        state[c] = (keep, hop(c, send, 0), 1)

    def advance(c):
        nonlocal token, weight_grad
        if c not in state or state[c] is None:
            return
        keep, got, stage = state[c]
        if stage == len(bits):
            token = weight_grad = finish(keep, got, weight_grad, token, c, chunks, scale)
            state[c] = None
        else:
            keep, send = merge(keep, got, token)
            token = send
            state[c] = (keep, hop(c, send, stage), stage + 1)

    def project_step(picked, last):
        nonlocal token, acc
        token = acc = project(
            out_weight, near, [fars[c] for c in picked], acc, token, orders, picked, shares, width, last
        )

    def send_back(gp):
        nonlocal token
        res = attention_back(info, pieces[gp], acc, outs[gp], fwd[gp][1], token, parts, docs, gp)
        token = results[gp] = res
        back[gp] = {d: over_seq(res[d : d + 2], d) for d in range(2, parts, 2)}

    def hand_over(gp, *tokens):
        got = gate([back[gp][d] for d in range(2, parts, 2)], *tokens)
        mine = [results[gp][1:2]] + [x[1:2] for x in got]
        crossed = over_seq(jnp.concatenate(mine, axis=0), 1)
        out = [results[gp][0], crossed[0]]
        for i, x in enumerate(got):
            out += [x[0], crossed[1 + i]]
        return out

    last = chunks - 1
    for c in range(chunks):
        if c > 1:
            advance(c - 2)
        weigh(c)
        project_step([c], c == last)
    send_back(0)
    for c in range(last):
        advance(c)
    for gp in range(1, groups):
        send_back(gp)
    advance(last - 2)
    advance(last)
    advance(last - 1)
    firsts = hand_over(0, token)
    advance(0)
    advance(last - 1)
    token = (token, firsts[1])
    advance(last)
    lasts = [hand_over(gp, token) for gp in range(1, groups)]
    for _ in bits:
        for c in range(last):
            advance(c)
    back = firsts + [x for group in lasts for x in group]
    grad_q, grad_k, grad_v = unpack(gate([info], token)[0], back, parts, groups)
    token = grad_q
    for _ in bits:
        advance(last)
    return (grad_q[None], grad_k[None], grad_v[None], weight_grad)


def solution(mesh):
    return jax.shard_map(
        body,
        mesh=mesh,
        in_specs=(
            P("dp", "seq", None),
            P("dp", "seq", None),
            P("dp", "seq", None),
            P("dp", "seq", None),
            P("seq", None),
            P("dp", None),
        ),
        out_specs=(
            P("dp", "seq", None),
            P("dp", "seq", None),
            P("dp", "seq", None),
            P("seq", "dp"),
        ),
        check_vma=False,
    )
```
